512 devices in a mesh: dom: 128 (over z, x, core), ray: 4 (over y).
Axes of the slice: x: 4, y: 4, z: 16, core: 2. Of those that a mesh axis runs over, the one named last changes fastest.
Arguments:
- anchor: float32 [3, 4, 512], P(None, 'ray'), may hold values from -4 to 4
- direct: float32 [3, 4, 512], P(None, 'ray'), may hold values from -3 to 3
- entry: float32 [4, 512, 4], P('ray'), may hold values from 0 to 2
- step: float32 [4, 512, 4], P('ray'), may hold values from 0.004 to 0.04
- counts: int32 [4, 512, 4], P('ray'), may hold values from 1 to 64
- crossing: int32 [4, 512, 4], P('ray'), may hold values from 0 to 127, all different within a row; in each aligned block of 512 rows (0 to 511, 512 to 1023, ..., all dimensions but the last counted through in order) at most 64 rows name the same one
- order: int32 [4, 8, 128], P('ray'), may hold values from 0 to 127, each once within a row
- target: float32 [3, 4, 512], P(None, 'ray'), may hold values from 0 to 1
- w_in: bfloat16 [128, 256, 63], P('dom'), may hold values from -0.75 to 0.75
- w_mid: bfloat16 [128, 256, 256], P('dom'), may hold values from -0.5 to 0.5
- w_out: bfloat16 [128, 4, 256], P('dom'), may hold values from -0.5 to 0.5
Outputs:
- rendered: float32 [3, 4, 512], P(None, 'ray', 'dom')
- grad_in: float32 [128, 256, 63], P('dom')
- grad_mid: float32 [128, 256, 256], P('dom')
- grad_out: float32 [128, 4, 256], P('dom')
The draws below stay inside these ranges and needn't reach their ends.
Inputs may be any that keep to these rules, and one draw needn't show every extreme that they name: `crossing`: each ray names 4 different partitions; among the rays of one group no partition is named by more than 64 rays, and one is named by exactly 64. `order`: each bundle's row names every partition once.
All inputs are finite; a program needn't handle non-finite values.
Results may differ from the reference program's by a relative error of at most 0.024.
Values sent between devices are 32-bit elements; how exact they have to be, the bound alone decides.
No kernel may reach another device: no remote copies, remote signals or barrier semaphores. Data moves between devices by JAX's collectives and lax.ppermute only.
A program may use at most 64 MiB of HBM per device.

```python
import math
import jax
import jax.numpy as jnp
import numpy as np
from jax import lax

H = 256
NFREQ = 10
FEATS = 63
S = 64
K = 4
NB = 8
RAYS_DEV = 4
ZONES = 128
GROUPS = 4
RG = 512
CAP = 64
N_DOM = 128


def with_ends(result, rng, least, top_value):
    dims = result.shape
    place = [jax.random.randint(jax.random.fold_in(rng, axis), (), 0, dims[axis]) for axis in range(len(dims))]
    result = result.at[tuple(place)].set(least)
    longest = dims.index(max(dims))
    place[longest] = (place[longest] + 1) % dims[longest]
    return result.at[tuple(place)].set(top_value)


def levels(own_key, extent, split, smallest, high):
    def one(dim, parts):
        steps = jax.random.uniform(jax.random.fold_in(jax.random.fold_in(own_key, 6), dim), (parts,), jnp.float32, smallest / len(split), high / len(split))
        return jnp.repeat(jnp.exp(steps), extent[dim] // parts).reshape((-1,) + (1,) * (len(extent) - dim - 1))

    gain = one(*split[0])
    for cut in split[1:]:
        gain = gain * one(*cut)
    return gain


def routed_block(own_key, own, number, rows, number_of, top, limit, lean):
    sequence = jax.random.permutation(own_key, number_of)
    packed, common = portions_of(number_of, rows * top, limit, lean, True), portions_of(number_of, rows * top, limit, lean, False)
    places = jnp.arange(number_of)

    def named(sizes, turn):
        used = int((sizes > 0).sum())
        fixed = max(1, used // 4)
        moved = fixed + (places - fixed + turn * (used - fixed)) % max(1, number_of - fixed)
        return jnp.zeros((number_of,), jnp.int32).at[sequence[jnp.where(places < fixed, places, moved)]].set(jnp.asarray(sizes, jnp.int32))

    sizes = jnp.where(number % 4 == 0, named(packed, number // 4), named(common, number - number // 4 - 1))
    mixed = jax.random.permutation(jax.random.fold_in(own, 3), number_of)
    donor, receiver = mixed[0:number_of // 2 * 2:2], mixed[1:number_of // 2 * 2:2]
    room = jnp.minimum(sizes[donor] - 1, limit - sizes[receiver]) // 2
    room = jnp.where((donor == sequence[0]) | (receiver == sequence[0]) | (sizes[receiver] == 0), 0, jnp.maximum(room, 0))
    moved = jax.random.randint(jax.random.fold_in(own, 4), (number_of // 2,), 0, 1 << 20) % (room + 1)
    sizes = sizes.at[donor].add(-moved).at[receiver].add(moved)
    members = jnp.searchsorted(jnp.cumsum(sizes), jnp.arange(rows * top), side="right").astype(jnp.int32)
    table = members.reshape(top, rows).T
    table = table[jax.random.permutation(jax.random.fold_in(own, 1), rows)]
    turn = jax.random.randint(jax.random.fold_in(own, 2), (rows, 1), 0, top)
    return jnp.take_along_axis(table, (jnp.arange(top)[None, :] + turn) % top, axis=1)


def portions_of(amount, total, reach, lean, full):
    weights = [(1 << 20) // math.isqrt(standing ** lean) + 1 for standing in range(1, amount + 1)]
    largest = reach if full else min(reach, max(-(-total // amount), total * weights[0] // sum(weights)))
    least = 1 if total - largest >= amount - 1 else 0
    holding, spare = [largest] + [least] * (amount - 1), total - largest - least * (amount - 1)
    while spare > 0:
        movable = [i for i in range(1, amount) if holding[i] < largest] or [i for i in range(1, amount) if holding[i] < reach]
        pool, left = sum([weights[i] for i in movable]), spare
        for i in movable:
            more = min(reach - holding[i], max(1, left * weights[i] // pool), spare)
            holding[i] = holding[i] + more
            spare = spare - more
    return np.array(holding)


def normal_values(key, dims, deviation, bound, cuts=(), kind=jnp.bfloat16):
    level = levels(key, dims, cuts, -0.22, 0.18) if cuts else 1.0
    result = jax.random.normal(key, dims, jnp.float32) * deviation * level
    return jnp.minimum(jnp.maximum(result, -bound), bound).astype(kind)


def setup_inputs(seed: int = 0) -> dict:
    key_list = jax.random.split(jax.random.key(seed), 12)
    anchor = normal_values(key_list[0], (3, GROUPS, RG), 1.0, 4.0, ((1, 4),), jnp.float32)
    direct = normal_values(key_list[1], (3, GROUPS, RG), 0.6, 3.0, ((1, 4),), jnp.float32)
    entry = jnp.clip(2.0 * jax.random.uniform(key_list[2], (GROUPS, RG, K), jnp.float32) ** levels(key_list[2], (GROUPS, RG, K), ((0, 4),), -0.2, 0.2), 0.0, 2.0)
    step = jnp.clip(jnp.exp(math.log(0.04) - 2.30258502 * jax.random.uniform(key_list[3], (GROUPS, RG, K), jnp.float32) ** levels(key_list[3], (GROUPS, RG, K), ((0, 4),), -0.2, 0.2)), 0.004, 0.04)
    counts = with_ends(jax.random.randint(key_list[4], (GROUPS, RG, K), 1, S + 1), jax.random.fold_in(key_list[4], 1), 1, S).astype(jnp.int32)
    crossing_keys = jax.random.split(jax.random.fold_in(key_list[5], 1), GROUPS * RG // RG)
    crossing_turns = jax.random.permutation(jax.random.fold_in(key_list[5], 3), GROUPS * RG // RG)
    crossing = jax.vmap(lambda own, number: routed_block(jax.random.fold_in(key_list[5], 2), own, number, RG, ZONES, K, CAP, 2))(crossing_keys, crossing_turns).reshape((GROUPS, RG, K))
    order = jax.vmap(lambda own: jax.random.permutation(own, ZONES))(jax.random.split(key_list[6], GROUPS * NB)).reshape((GROUPS, NB, ZONES)).astype(jnp.int32)
    target = jnp.clip(1.0 * jax.random.uniform(key_list[7], (3, GROUPS, RG), jnp.float32) ** levels(key_list[7], (3, GROUPS, RG), ((1, 4),), -0.2, 0.2), 0.0, 1.0)
    w_in = normal_values(key_list[8], (ZONES, H, FEATS), FEATS ** -0.5, 0.75, ((0, 128),))
    w_mid = normal_values(key_list[9], (ZONES, H, H), (H / 2) ** -0.5, 0.5, ((0, 128),))
    w_out = normal_values(key_list[10], (ZONES, 4, H), (H / 2) ** -0.5, 0.5, ((0, 128),))
    return {"anchor": anchor, "direct": direct, "entry": entry, "step": step, "counts": counts, "crossing": crossing, "order": order, "target": target, "w_in": w_in, "w_mid": w_mid, "w_out": w_out}


def slot_inputs(crossings, partition, anchor_g, direct_g, entry_g, step_g, counts_g, capacity):
    hit_mask = crossings == partition
    crossed = jnp.any(hit_mask, axis=1)
    places = jnp.cumsum(crossed.astype(jnp.int32)) - 1
    slot_ids = jnp.arange(capacity, dtype=jnp.int32)
    selector = jnp.logical_and(places[None, :] == slot_ids[:, None], crossed[None, :])
    hit_float = hit_mask.astype(jnp.float32)
    selector_f = selector.astype(jnp.float32)
    entry_ray = lax.optimization_barrier(jnp.sum(hit_float * entry_g, axis=1))
    step_ray = lax.optimization_barrier(jnp.sum(hit_float * step_g, axis=1))
    count_ray = lax.optimization_barrier(jnp.sum(jnp.where(hit_mask, counts_g, 0), axis=1)).astype(jnp.int32)

    def picked(values):
        return jnp.dot(values, selector_f.T, precision=lax.Precision.HIGHEST, preferred_element_type=jnp.float32)
    anchor_s = picked(anchor_g)
    direct_s = picked(direct_g)
    entry_s = picked(entry_ray[None, :])[0]
    step_s = picked(step_ray[None, :])[0]
    count_s = lax.optimization_barrier(jnp.sum(jnp.where(selector, count_ray[None, :], 0), axis=1)).astype(jnp.int32)
    return (selector_f, anchor_s, direct_s, entry_s, step_s, count_s)

def encode_points(anchor_s, direct_s, entry_s, step_s):
    offsets = jnp.arange(S, dtype=jnp.float32) + 0.5
    depths = entry_s[:, None] + offsets[None, :] * step_s[:, None]
    points = anchor_s[:, :, None] + depths[None, :, :] * direct_s[:, :, None]
    pieces = [points]
    for level in range(NFREQ):
        scaled = points * 2.0 ** level
        pieces.append(jnp.sin(scaled))
        pieces.append(jnp.cos(scaled))
    encoded = jnp.concatenate(pieces, axis=0)
    return encoded.reshape(encoded.shape[0], -1).astype(jnp.bfloat16)

def render_slots(raw_out, step_s, count_s):
    capacity = step_s.shape[0]
    raw_cube = raw_out.reshape(4, capacity, -1)
    samples = raw_cube.shape[2]
    density = jax.nn.softplus(raw_cube[0])
    albedo = jax.nn.sigmoid(raw_cube[1:])
    live_mask = (jnp.arange(samples, dtype=jnp.int32)[None, :] < count_s[:, None]).astype(jnp.float32)
    optical = density * step_s[:, None] * live_mask
    reached = jnp.cumsum(optical, axis=1)
    sample_weight = jnp.exp(optical - reached) - jnp.exp(-reached)
    colors = lax.optimization_barrier(jnp.sum(sample_weight[None] * albedo, axis=2))
    log_trans = -reached[:, -1]
    return (colors, log_trans)

def mlp_forward(encoded, weight_in, weight_mid, weight_out):
    hidden_one = jax.nn.relu(jnp.dot(weight_in, encoded, preferred_element_type=jnp.float32)).astype(jnp.bfloat16)
    hidden_two = jax.nn.relu(jnp.dot(weight_mid, hidden_one, preferred_element_type=jnp.float32)).astype(jnp.bfloat16)
    raw_out = jnp.dot(weight_out, hidden_two, preferred_element_type=jnp.float32)
    return (hidden_one, hidden_two, raw_out)

def outer_sum(left, right):
    return lax.dot_general(left, right, (((1,), (1,)), ((), ())), preferred_element_type=jnp.float32)

def back_dot(weight, grad):
    return lax.dot_general(weight, grad, (((0,), (0,)), ((), ())), preferred_element_type=jnp.float32)

def mlp_backward(encoded, hidden_one, hidden_two, d_raw, weight_mid, weight_out):
    d_low = d_raw.astype(jnp.bfloat16)
    grad_o = outer_sum(d_low, hidden_two)
    d_two = (back_dot(weight_out, d_low) * (hidden_two > 0)).astype(jnp.bfloat16)
    grad_m = outer_sum(d_two, hidden_one)
    d_one = (back_dot(weight_mid, d_two) * (hidden_one > 0)).astype(jnp.bfloat16)
    grad_i = outer_sum(d_one, encoded)
    return (grad_i, grad_m, grad_o)

def depth_ranks(order_g, partitions):
    positions = jnp.arange(partitions, dtype=jnp.int32)
    matches = order_g[:, :, None] == positions[None, None, :]
    return lax.optimization_barrier(jnp.sum(jnp.where(matches, positions[None, :, None], 0), axis=1)).astype(jnp.int32)

def reference(anchor, direct, entry, step, counts, crossing, order, target, w_in, w_mid, w_out):
    capacity = RAYS_DEV * min(4 * K, N_DOM)
    highest = lax.Precision.HIGHEST
    grad_i = jnp.zeros(w_in.shape, jnp.float32)
    grad_m = jnp.zeros(w_mid.shape, jnp.float32)
    grad_o = jnp.zeros(w_out.shape, jnp.float32)
    rendered_groups = []
    part_ids = jnp.arange(ZONES, dtype=jnp.int32)
    for group_index in range(GROUPS):
        crossings = crossing[group_index]
        anchor_g = anchor[:, group_index]
        direct_g = direct[:, group_index]

        def local_slots(partition):
            return slot_inputs(crossings, partition, anchor_g, direct_g, entry[group_index], step[group_index], counts[group_index], capacity)

        def forward(items):
            partition, weight_in, weight_mid, weight_out = items
            selector_f, anchor_s, direct_s, entry_s, step_s, count_s = local_slots(partition)
            encoded = encode_points(anchor_s, direct_s, entry_s, step_s)
            hidden_one, hidden_two, raw_out = mlp_forward(encoded, weight_in, weight_mid, weight_out)
            colors, log_trans = render_slots(raw_out, step_s, count_s)
            color_ray = jnp.dot(colors, selector_f, precision=highest, preferred_element_type=jnp.float32)
            log_ray = jnp.dot(log_trans[None, :], selector_f, precision=highest, preferred_element_type=jnp.float32)[0]
            return (color_ray, log_ray)
        color_all, log_all = lax.map(forward, (part_ids, w_in, w_mid, w_out))
        depth_rank = depth_ranks(order[group_index], ZONES)
        ahead_all = (depth_rank[:, None, :] < depth_rank[:, :, None]).astype(jnp.float32)
        before = jnp.einsum('bde,ebj->dbj', ahead_all, log_all.reshape(ZONES, NB, -1), precision=highest).reshape(ZONES, RG)
        total_log = lax.optimization_barrier(jnp.sum(log_all, axis=0))
        fade_all = jnp.exp(before)
        rendered_g = lax.optimization_barrier(jnp.sum(fade_all[:, None, :] * color_all, axis=0)) + jnp.exp(total_log)[None, :]
        residual = rendered_g - target[:, group_index]
        shares = lax.optimization_barrier(jnp.sum(residual[None] * fade_all[:, None, :] * color_all, axis=1))
        background = jnp.exp(total_log) * lax.optimization_barrier(jnp.sum(residual, axis=0))
        dlog_all = jnp.einsum('bde,dbj->ebj', ahead_all, shares.reshape(ZONES, NB, -1), precision=highest).reshape(ZONES, RG) + background[None, :]
        dcolor_all = fade_all[:, None, :] * residual[None]
        rendered_groups.append(rendered_g)

        def backward(items):
            partition, weight_in, weight_mid, weight_out, dcolor_ray, dlog_ray = items
            selector_f, anchor_s, direct_s, entry_s, step_s, count_s = local_slots(partition)
            encoded = encode_points(anchor_s, direct_s, entry_s, step_s)
            hidden_one, hidden_two, raw_out = mlp_forward(encoded, weight_in, weight_mid, weight_out)
            outputs, unravel = jax.vjp(lambda values: render_slots(values, step_s, count_s), raw_out)
            dcolor_s = jnp.dot(dcolor_ray, selector_f.T, precision=highest, preferred_element_type=jnp.float32)
            dlog_s = jnp.dot(dlog_ray[None, :], selector_f.T, precision=highest, preferred_element_type=jnp.float32)[0]
            d_raw = unravel((dcolor_s, dlog_s))[0]
            return mlp_backward(encoded, hidden_one, hidden_two, d_raw, weight_mid, weight_out)
        part_i, part_m, part_o = lax.map(backward, (part_ids, w_in, w_mid, w_out, dcolor_all, dlog_all))
        grad_i = grad_i + part_i
        grad_m = grad_m + part_m
        grad_o = grad_o + part_o
    rendered = jnp.stack(rendered_groups, axis=1)
    return (rendered, grad_i, grad_m, grad_o)
```

```python
import functools

import jax
import jax.numpy as jnp
from jax import lax
from jax.experimental import pallas as pl
from jax.experimental.pallas import tpu as pltpu
from jax.sharding import PartitionSpec as P

NFREQ = 10
FEATS = 63
S = 64
K = 4
NB = 8
CAP = 64
ZONES = 128
RG = 512
OWN = 4
ROWS = 32
SEL = 72
COLS = CAP * S
TILE = 4
CHUNK = 88
F32 = jnp.float32
BF16 = jnp.bfloat16


def iota(shape, dim):
    return lax.broadcasted_iota(jnp.int32, shape, dim)


def split3(x):
    high = x.astype(BF16)
    rest = x - high.astype(F32)
    mid = rest.astype(BF16)
    low = (rest - mid.astype(F32)).astype(BF16)
    return high, mid, low


def dot(a, b):
    return jnp.dot(a, b, preferred_element_type=F32)


def dot_nt(a, b):
    return lax.dot_general(a, b, (((1,), (1,)), ((), ())), preferred_element_type=F32)


def split_dot(x, exact):
    return sum(dot(part, exact) for part in split3(x))


def halves(column):
    lane = iota((ROWS, 2 * S), 1)
    return jnp.where(lane < S, column[0:ROWS], column[ROWS : 2 * ROWS])


def sin_cos(x):
    turns = jnp.floor(x * 0.6366197723675814 + 0.5)
    r = ((x - turns * 1.5703125) - turns * 4.837512969970703e-4) - turns * 7.54978995489188e-8
    z = r * r
    s = ((-1.9515295891e-4 * z + 8.3321608736e-3) * z - 1.6666654611e-1) * z * r + r
    c = ((2.443315711809948e-5 * z - 1.388731625493765e-3) * z + 4.166664568298827e-2) * z * z - 0.5 * z + 1.0
    quadrant = turns.astype(jnp.int32)
    swap = (quadrant & 1) == 1
    sin_r = jnp.where(swap, c, s)
    cos_r = jnp.where(swap, s, c)
    sin_r = jnp.where((quadrant & 2) == 2, -sin_r, sin_r)
    cos_r = jnp.where(((quadrant + 1) & 2) == 2, -cos_r, cos_r)
    return sin_r, cos_r


def shade(raw, step_d, count_d):
    lane = iota((ROWS, 2 * S), 1)
    index = lane & (S - 1)
    scale = jnp.where(index.astype(F32) < count_d, step_d, 0.0)
    decay = jnp.exp(-jnp.abs(raw[0]))
    density = jnp.maximum(raw[0], 0.0) + jnp.log1p(decay)
    optical = density * scale
    source, target = iota((2 * S, 2 * S), 0), iota((2 * S, 2 * S), 1)
    upto = ((source <= target) & ((source < S) == (target < S))).astype(F32).astype(BF16)
    reached = split_dot(optical, upto)
    entering = jnp.exp(optical - reached)
    weight = entering - jnp.exp(-reached)
    albedo = [1.0 / (1.0 + jnp.exp(-raw[c])) for c in (1, 2, 3)]
    return scale, optical, entering, weight, albedo


def forward_kernel(
    part_ref, anchor_ref, direct_ref, entry_ref, step_ref, counts_ref, crossing_ref, target_ref,
    w_in_ref, w_mid_ref, w_out_ref,
    send_ref, enc_ref, one_ref, two_ref, raw_ref, reals_ref, whole_ref,
    vals, ints, ranks, feats, win,
):
    part = part_ref[0]
    zone = iota((ZONES, RG), 0)
    crossing = crossing_ref[0]
    names = [zone == crossing[k : k + 1] for k in range(K)]
    member = names[0] | names[1] | names[2] | names[3]
    earlier = (iota((RG, RG), 0) < iota((RG, RG), 1)).astype(F32).astype(BF16)
    ranks[...] = dot(member.astype(F32).astype(BF16), earlier)
    place_all = ranks[...]
    own = crossing == part
    crossed = own[0:1] | own[1:2] | own[2:3] | own[3:4]

    def of_own(ref):
        return jnp.sum(jnp.where(own, ref[0].astype(F32), 0.0), axis=0, keepdims=True)

    vals[...] = jnp.zeros_like(vals)
    for d in range(3):
        vals[d : d + 1] = anchor_ref[d]
        vals[3 + d : 4 + d] = direct_ref[d]
        vals[8 + d : 9 + d] = target_ref[d]
    vals[6:7] = of_own(entry_ref)
    vals[7:8] = of_own(step_ref)
    ints[...] = jnp.zeros_like(ints)
    ints[0:4] = crossing.astype(F32)
    for k in range(K):
        ints[4 + k : 5 + k] = jnp.sum(jnp.where(names[k], place_all, 0.0), axis=0, keepdims=True)
    ray = iota((1, RG), 1)
    ints[8:9] = of_own(counts_ref)
    ints[9:10] = (ray // (RG // NB)).astype(F32)
    ints[10:11] = jnp.ones((1, RG), F32)

    row = iota((SEL, RG), 0)
    place_own = ranks[pl.ds(part, 1), :].astype(jnp.int32)
    place_own = jnp.where(crossed, place_own, -1)
    in_slot = (row < CAP) & (place_own == row)
    own_ray = (row >= CAP) & (row < CAP + OWN) & (ray == part * OWN + (row - CAP))
    selector = (in_slot | own_ray).astype(F32).astype(BF16)
    reals = sum(dot_nt(selector, piece) for piece in split3(vals[...]))
    whole = dot_nt(selector, ints[...].astype(BF16))
    reals_ref[...] = reals
    whole_ref[...] = whole

    columns = [halves(reals[0:CAP, j : j + 1]) for j in range(8)]
    count_d = halves(whole[0:CAP, 8:9])
    step_d = columns[7]
    index = (iota((ROWS, 2 * S), 1) & (S - 1)).astype(F32)
    depth = columns[6] + (index + 0.5) * step_d
    feats[FEATS * ROWS : (FEATS + 1) * ROWS] = jnp.zeros((ROWS, 2 * S), F32)
    for d in range(3):
        point = columns[d] + depth * columns[3 + d]
        feats[d * ROWS : (d + 1) * ROWS] = point
        sin_x, cos_x = sin_cos(point)
        for level in range(NFREQ):
            at = 3 + 6 * level + d
            feats[at * ROWS : (at + 1) * ROWS] = sin_x
            feats[(at + 3) * ROWS : (at + 4) * ROWS] = cos_x
            sin_x, cos_x = 2.0 * sin_x * cos_x, 1.0 - 2.0 * sin_x * sin_x

    win[...] = jnp.zeros_like(win)
    win[0:FEATS] = w_in_ref[...].astype(F32)
    w_in = win[...].T.astype(BF16)
    w_mid = w_mid_ref[...]
    w_out = w_out_ref[...]
    for tile in range(ROWS // TILE):
        span = slice(tile * TILE * 128, (tile + 1) * TILE * 128)
        encoded = jnp.concatenate(
            [feats[pl.ds(tile * TILE + j, FEATS + 1, stride=ROWS), :].astype(BF16) for j in range(TILE)], axis=1
        )
        enc_ref[:, span] = encoded
        one = jnp.maximum(dot(w_in, encoded), 0.0).astype(BF16)
        one_ref[:, span] = one
        two = jnp.maximum(dot(w_mid, one), 0.0).astype(BF16)
        two_ref[:, span] = two
        raw = dot(w_out, two)
        for j in range(TILE):
            raw_ref[pl.ds(tile * TILE + j, 4, stride=ROWS), :] = raw[:, j * 128 : (j + 1) * 128]

    raw = [raw_ref[c * ROWS : (c + 1) * ROWS] for c in range(4)]
    _, optical, _, weight, albedo = shade(raw, step_d, count_d)
    sums = jnp.concatenate([weight * albedo[0], weight * albedo[1], weight * albedo[2], -optical], axis=0)
    half = (iota((8, 2 * S), 0) == iota((8, 2 * S), 1) // S).astype(F32).astype(BF16)
    sent = sum(dot_nt(half, piece) for piece in split3(sums))
    send_ref[...] = jnp.broadcast_to(sent[None, 0:2], send_ref.shape)


def backward_kernel(
    part_ref, got_ref, order_ref, reals_ref, whole_ref, raw_ref, enc_ref, one_ref, two_ref, w_mid_ref, w_out_ref,
    rendered_ref, grads_ref,
    draw, wout,
):
    part = part_ref[0]
    reals, whole = reals_ref[...], whole_ref[...]
    bundle = (whole[:, 9:10].astype(jnp.int32) == iota((SEL, NB), 1)).astype(F32).astype(BF16)
    order = dot(bundle, order_ref[0].astype(F32).astype(BF16))
    lane = iota((SEL, ZONES), 1)
    position = lane.astype(F32)
    named = [whole[:, k : k + 1] for k in range(K)]
    rank = [jnp.sum(jnp.where(order == named[k], position, 0.0), axis=1, keepdims=True) for k in range(K)]
    pick = jnp.concatenate([(named[k] == position).astype(F32).astype(BF16) for k in range(K)], axis=0)
    place = jnp.concatenate([whole[:, 4 + k : 5 + k] for k in range(K)], axis=0).astype(jnp.int32)
    pieces = [split3(got_ref[:, h, :]) for h in range(2)]
    wanted = (iota((K * SEL, ZONES), 1) % ROWS) == (place % ROWS)
    gather = (iota((ZONES, 8), 0) // ROWS == iota((ZONES, 8), 1)).astype(F32).astype(BF16)
    values = jnp.zeros((K * SEL, 8), F32)
    for piece in range(3):
        low, high = dot(pick, pieces[0][piece]), dot(pick, pieces[1][piece])
        found = jnp.where(wanted, jnp.where(place < ROWS, low, high), 0.0)
        values = values + dot(found.astype(BF16), gather)

    mine = [values[k * SEL : (k + 1) * SEL] for k in range(K)]
    log = [mine[k][:, 3:4] for k in range(K)]
    color = [[mine[k][:, c : c + 1] for c in range(3)] for k in range(K)]
    ahead = [[rank[j] < rank[k] for j in range(K)] for k in range(K)]
    fade = [jnp.exp(sum(jnp.where(ahead[k][j], log[j], 0.0) for j in range(K) if j != k)) for k in range(K)]
    clear = jnp.exp(log[0] + log[1] + log[2] + log[3])
    rendered = [sum(fade[k] * color[k][c] for k in range(K)) + clear for c in range(3)]
    residual = [rendered[c] - reals[:, 8 + c : 9 + c] for c in range(3)]
    share = [fade[k] * sum(residual[c] * color[k][c] for c in range(3)) for k in range(K)]
    owned = [named[k] == part.astype(F32) for k in range(K)]
    own_rank = sum(jnp.where(owned[k], rank[k], 0.0) for k in range(K))
    own_fade = sum(jnp.where(owned[k], fade[k], 0.0) for k in range(K))
    dlog = sum(jnp.where(rank[k] > own_rank, share[k], 0.0) for k in range(K))
    dlog = dlog + clear * (residual[0] + residual[1] + residual[2])
    used = whole[:, 10:11] > 0.5
    dlog = jnp.where(used, dlog, 0.0)
    dcolor = [jnp.where(used, own_fade * residual[c], 0.0) for c in range(3)]
    diagonal = iota((8, 8), 0) == iota((8, 8), 1)
    for c in range(3):
        line = jnp.sum(jnp.where(diagonal, rendered[c][CAP:SEL], 0.0), axis=0, keepdims=True)
        rendered_ref[c] = line[:, 0:OWN]

    raw = [raw_ref[c * ROWS : (c + 1) * ROWS] for c in range(4)]
    step_d = halves(reals[0:CAP, 7:8])
    count_d = halves(whole[0:CAP, 8:9])
    scale, _, entering, weight, albedo = shade(raw, step_d, count_d)
    dcolor_d = [halves(dcolor[c][0:CAP]) for c in range(3)]
    gain = sum(dcolor_d[c] * albedo[c] for c in range(3))
    source, target = iota((2 * S, 2 * S), 0), iota((2 * S, 2 * S), 1)
    since = ((source >= target) & ((source < S) == (target < S))).astype(F32).astype(BF16)
    behind = split_dot(gain * weight, since)
    d_optical = gain * entering - behind - halves(dlog[0:CAP])
    draw[0:ROWS] = d_optical * scale / (1.0 + jnp.exp(-raw[0]))
    for c in range(3):
        draw[(c + 1) * ROWS : (c + 2) * ROWS] = weight * dcolor_d[c] * albedo[c] * (1.0 - albedo[c])
    draw[4 * ROWS :] = jnp.zeros((12 * ROWS, 2 * S), F32)

    wout[...] = jnp.zeros_like(wout)
    wout[0:4] = w_out_ref[...].astype(F32)
    w_out_t = wout[...].T.astype(BF16)
    w_mid_t = w_mid_ref[...].astype(F32).T.astype(BF16)
    grad_out = jnp.zeros((16, 256), F32)
    grad_mid = jnp.zeros((256, 256), F32)
    grad_in = jnp.zeros((64, 256), F32)
    for tile in range(ROWS // TILE):
        span = slice(tile * TILE * 128, (tile + 1) * TILE * 128)
        low = jnp.concatenate(
            [draw[pl.ds(tile * TILE + j, 16, stride=ROWS), :].astype(BF16) for j in range(TILE)], axis=1
        )
        two, one = two_ref[:, span], one_ref[:, span]
        grad_out = grad_out + dot_nt(low, two)
        d_two = jnp.where(two > 0, dot(w_out_t, low), 0.0).astype(BF16)
        grad_mid = grad_mid + dot_nt(d_two, one)
        d_one = jnp.where(one > 0, dot(w_mid_t, d_two), 0.0).astype(BF16)
        grad_in = grad_in + dot_nt(enc_ref[:, span], d_one)
    for q in range(4):
        grads_ref[q, 0:64] = grad_mid[64 * q : 64 * q + 64]
        grads_ref[q, 64:80] = grad_in[16 * q : 16 * q + 16]
        grads_ref[q, 80:88] = jnp.broadcast_to(grad_out[q : q + 1], (8, 256))


def unpack_kernel(all_ref, in_ref, mid_ref, out_ref):
    for q in range(4):
        mid_ref[64 * q : 64 * q + 64] = all_ref[q, 0:64]
        rows = min(16, FEATS - 16 * q)
        in_ref[16 * q : 16 * q + rows, 0, :] = all_ref[q, 64 : 64 + rows]
        out_ref[q : q + 1] = all_ref[q, 80:81]


def vmem(count):
    return [pl.BlockSpec(memory_space=pltpu.VMEM)] * count


def local(anchor, direct, entry, step, counts, crossing, order, target, w_in, w_mid, w_out):
    part = lax.axis_index("dom").astype(jnp.int32).reshape(1)
    entry, step, counts, crossing = (jnp.swapaxes(a, 1, 2) for a in (entry, step, counts, crossing))
    w_in_t = jnp.swapaxes(w_in, 1, 2)[0]
    scalar = pl.BlockSpec(memory_space=pltpu.SMEM)
    params = pltpu.CompilerParams(vmem_limit_bytes=40 * 1024 * 1024)
    shape = jax.ShapeDtypeStruct
    send, enc, one, two, raw, reals, whole = pl.pallas_call(
        forward_kernel,
        out_shape=(
            shape((ZONES, 2, 128), F32),
            shape((64, COLS), BF16),
            shape((256, COLS), BF16),
            shape((256, COLS), BF16),
            shape((4 * ROWS, 128), F32),
            shape((SEL, 16), F32),
            shape((SEL, 16), F32),
        ),
        in_specs=[scalar] + vmem(10),
        out_specs=vmem(7),
        scratch_shapes=[
            pltpu.VMEM((16, RG), F32),
            pltpu.VMEM((16, RG), F32),
            pltpu.VMEM((ZONES, RG), F32),
            pltpu.VMEM((64 * ROWS, 128), F32),
            pltpu.VMEM((64, 256), F32),
        ],
        compiler_params=params,
        name="forward",
    )(part, anchor, direct, entry, step, counts, crossing, target, w_in_t, w_mid[0], w_out[0])
    got = lax.all_to_all(send, "dom", 0, 0)
    rendered, grads = pl.pallas_call(
        backward_kernel,
        out_shape=(shape((3, 1, OWN), F32), shape((4, CHUNK, 256), F32)),
        in_specs=[scalar] + vmem(10),
        out_specs=vmem(2),
        scratch_shapes=[pltpu.VMEM((16 * ROWS, 128), F32), pltpu.VMEM((16, 256), F32)],
        compiler_params=params,
        name="backward",
    )(part, got, order, reals, whole, raw, enc, one, two, w_mid[0], w_out[0])
    shares = lax.all_to_all(grads, "ray", 0, 0)
    total = jnp.sum(shares, axis=0)
    everything = lax.all_to_all(jnp.broadcast_to(total[None], grads.shape), "ray", 0, 0)
    grad_i, grad_m, grad_o = pl.pallas_call(
        unpack_kernel,
        out_shape=(shape((FEATS, 1, 256), F32), shape((256, 256), F32), shape((4, 256), F32)),
        in_specs=vmem(1),
        out_specs=vmem(3),
        compiler_params=params,
        name="unpack",
    )(everything)
    return rendered, jnp.transpose(grad_i, (1, 2, 0)), grad_m[None], grad_o[None]


def solution(mesh):
    in_specs = (
        P(None, "ray", None),
        P(None, "ray", None),
        P("ray", None, None),
        P("ray", None, None),
        P("ray", None, None),
        P("ray", None, None),
        P("ray", None, None),
        P(None, "ray", None),
        P("dom", None, None),
        P("dom", None, None),
        P("dom", None, None),
    )
    out_specs = (
        P(None, "ray", "dom"),
        P("dom", None, None),
        P("dom", None, None),
        P("dom", None, None),
    )
    return jax.shard_map(local, mesh=mesh, in_specs=in_specs, out_specs=out_specs, check_vma=False)
```

```python
import functools

import jax
import jax.numpy as jnp
from jax import lax
from jax.experimental import pallas as pl
from jax.experimental.pallas import tpu as pltpu
from jax.sharding import PartitionSpec as P

NFREQ = 10
FEATS = 63
S = 64
K = 4
NB = 8
CAP = 64
ZONES = 128
RG = 512
OWN = 4
ROWS = 32
SEL = 72
COLS = CAP * S
TILE = 4
CHUNK = 88
F32 = jnp.float32
BF16 = jnp.bfloat16


def iota(shape, dim):
    return lax.broadcasted_iota(jnp.int32, shape, dim)


def split3(x):
    high = x.astype(BF16)
    rest = x - high.astype(F32)
    mid = rest.astype(BF16)
    low = (rest - mid.astype(F32)).astype(BF16)
    return high, mid, low


def dot(a, b):
    return jnp.dot(a, b, preferred_element_type=F32)


def dot_nt(a, b):
    return lax.dot_general(a, b, (((1,), (1,)), ((), ())), preferred_element_type=F32)


def split_dot(x, exact):
    return sum(dot(part, exact) for part in split3(x))


def halves(column):
    lane = iota((ROWS, 2 * S), 1)
    return jnp.where(lane < S, column[0:ROWS], column[ROWS : 2 * ROWS])


def sin_cos(x):
    turns = jnp.floor(x * 0.6366197723675814 + 0.5)
    r = ((x - turns * 1.5703125) - turns * 4.837512969970703e-4) - turns * 7.54978995489188e-8
    z = r * r
    s = ((-1.9515295891e-4 * z + 8.3321608736e-3) * z - 1.6666654611e-1) * z * r + r
    c = ((2.443315711809948e-5 * z - 1.388731625493765e-3) * z + 4.166664568298827e-2) * z * z - 0.5 * z + 1.0
    quadrant = turns.astype(jnp.int32)
    swap = (quadrant & 1) == 1
    sin_r = jnp.where(swap, c, s)
    cos_r = jnp.where(swap, s, c)
    sin_r = jnp.where((quadrant & 2) == 2, -sin_r, sin_r)
    cos_r = jnp.where(((quadrant + 1) & 2) == 2, -cos_r, cos_r)
    return sin_r, cos_r


def shade(raw, step_d, count_d):
    lane = iota((ROWS, 2 * S), 1)
    index = lane & (S - 1)
    scale = jnp.where(index.astype(F32) < count_d, step_d, 0.0)
    decay = jnp.exp(-jnp.abs(raw[0]))
    density = jnp.maximum(raw[0], 0.0) + jnp.log1p(decay)
    optical = density * scale
    source, target = iota((2 * S, 2 * S), 0), iota((2 * S, 2 * S), 1)
    upto = ((source <= target) & ((source < S) == (target < S))).astype(F32).astype(BF16)
    reached = split_dot(optical, upto)
    entering = jnp.exp(optical - reached)
    weight = entering - jnp.exp(-reached)
    albedo = [1.0 / (1.0 + jnp.exp(-raw[c])) for c in (1, 2, 3)]
    return scale, optical, entering, weight, albedo


def forward_kernel(
    part_ref, anchor_hbm, direct_hbm, entry_hbm, step_hbm, counts_hbm, crossing_hbm, target_hbm, order_hbm,
    w_in_hbm, w_mid_hbm, w_out_hbm,
    send_ref, enc_ref, one_ref, two_ref, raw_ref, reals_ref, whole_ref, order_ref, w_mid_ref, w_out_ref,
    anchor_ref, direct_ref, entry_ref, step_ref, counts_ref, crossing_ref, target_ref, w_in_ref,
    vals, ints, ranks, feats, win, sems,
):
    copies = [
        pltpu.make_async_copy(source, target, sems.at[i])
        for i, (source, target) in enumerate((
            (crossing_hbm, crossing_ref), (entry_hbm, entry_ref), (step_hbm, step_ref), (counts_hbm, counts_ref),
            (anchor_hbm, anchor_ref), (direct_hbm, direct_ref), (target_hbm, target_ref), (w_in_hbm, w_in_ref),
            (w_mid_hbm, w_mid_ref), (w_out_hbm, w_out_ref), (order_hbm, order_ref),
        ))
    ]
    for copy in copies:
        copy.start()
    part = part_ref[0]
    copies[0].wait()
    zone = iota((ZONES, RG), 0)
    crossing = crossing_ref[0]
    names = [zone == crossing[k : k + 1] for k in range(K)]
    member = names[0] | names[1] | names[2] | names[3]
    earlier = (iota((RG, RG), 0) < iota((RG, RG), 1)).astype(F32).astype(BF16)
    ranks[...] = dot(member.astype(F32).astype(BF16), earlier)
    place_all = ranks[...]
    own = crossing == part
    crossed = own[0:1] | own[1:2] | own[2:3] | own[3:4]

    def of_own(ref):
        return jnp.sum(jnp.where(own, ref[0].astype(F32), 0.0), axis=0, keepdims=True)

    for copy in copies[1:7]:
        copy.wait()
    vals[...] = jnp.zeros_like(vals)
    for d in range(3):
        vals[d : d + 1] = anchor_ref[d]
        vals[3 + d : 4 + d] = direct_ref[d]
        vals[8 + d : 9 + d] = target_ref[d]
    vals[6:7] = of_own(entry_ref)
    vals[7:8] = of_own(step_ref)
    ints[...] = jnp.zeros_like(ints)
    ints[0:4] = crossing.astype(F32)
    for k in range(K):
        ints[4 + k : 5 + k] = jnp.sum(jnp.where(names[k], place_all, 0.0), axis=0, keepdims=True)
    ray = iota((1, RG), 1)
    ints[8:9] = of_own(counts_ref)
    ints[9:10] = (ray // (RG // NB)).astype(F32)
    ints[10:11] = jnp.ones((1, RG), F32)

    row = iota((SEL, RG), 0)
    place_own = ranks[pl.ds(part, 1), :].astype(jnp.int32)
    place_own = jnp.where(crossed, place_own, -1)
    in_slot = (row < CAP) & (place_own == row)
    own_ray = (row >= CAP) & (row < CAP + OWN) & (ray == part * OWN + (row - CAP))
    selector = (in_slot | own_ray).astype(F32).astype(BF16)
    reals = sum(dot_nt(selector, piece) for piece in split3(vals[...]))
    whole = dot_nt(selector, ints[...].astype(BF16))
    reals_ref[...] = reals
    whole_ref[...] = whole

    columns = [halves(reals[0:CAP, j : j + 1]) for j in range(8)]
    count_d = halves(whole[0:CAP, 8:9])
    step_d = columns[7]
    index = (iota((ROWS, 2 * S), 1) & (S - 1)).astype(F32)
    depth = columns[6] + (index + 0.5) * step_d
    feats[FEATS * ROWS : (FEATS + 1) * ROWS] = jnp.zeros((ROWS, 2 * S), F32)
    for d in range(3):
        point = columns[d] + depth * columns[3 + d]
        feats[d * ROWS : (d + 1) * ROWS] = point
        sin_x, cos_x = sin_cos(point)
        for level in range(NFREQ):
            at = 3 + 6 * level + d
            feats[at * ROWS : (at + 1) * ROWS] = sin_x
            feats[(at + 3) * ROWS : (at + 4) * ROWS] = cos_x
            sin_x, cos_x = 2.0 * sin_x * cos_x, 1.0 - 2.0 * sin_x * sin_x

    for copy in copies[7:]:
        copy.wait()
    win[...] = jnp.zeros_like(win)
    win[0:FEATS] = w_in_ref[...].astype(F32)
    w_in = win[...].T.astype(BF16)
    w_mid = w_mid_ref[...]
    w_out = w_out_ref[...]
    for tile in range(ROWS // TILE):
        span = slice(tile * TILE * 128, (tile + 1) * TILE * 128)
        encoded = jnp.concatenate(
            [feats[pl.ds(tile * TILE + j, FEATS + 1, stride=ROWS), :].astype(BF16) for j in range(TILE)], axis=1
        )
        enc_ref[:, span] = encoded
        one = jnp.maximum(dot(w_in, encoded), 0.0).astype(BF16)
        one_ref[:, span] = one
        two = jnp.maximum(dot(w_mid, one), 0.0).astype(BF16)
        two_ref[:, span] = two
        raw = dot(w_out, two)
        for j in range(TILE):
            raw_ref[pl.ds(tile * TILE + j, 4, stride=ROWS), :] = raw[:, j * 128 : (j + 1) * 128]

    raw = [raw_ref[c * ROWS : (c + 1) * ROWS] for c in range(4)]
    _, optical, _, weight, albedo = shade(raw, step_d, count_d)
    sums = jnp.concatenate([weight * albedo[0], weight * albedo[1], weight * albedo[2], -optical], axis=0)
    half = (iota((8, 2 * S), 0) == iota((8, 2 * S), 1) // S).astype(F32).astype(BF16)
    sent = sum(dot_nt(half, piece) for piece in split3(sums))
    send_ref[...] = jnp.broadcast_to(sent[None, 0:2], send_ref.shape)


def backward_kernel(
    part_ref, got_ref, order_ref, reals_ref, whole_ref, raw_ref, enc_ref, one_ref, two_ref, w_mid_ref, w_out_ref,
    rendered_ref, grads_ref,
    draw, wout,
):
    part = part_ref[0]
    reals, whole = reals_ref[...], whole_ref[...]
    bundle = (whole[:, 9:10].astype(jnp.int32) == iota((SEL, NB), 1)).astype(F32).astype(BF16)
    order = dot(bundle, order_ref[0].astype(F32).astype(BF16))
    lane = iota((SEL, ZONES), 1)
    position = lane.astype(F32)
    named = [whole[:, k : k + 1] for k in range(K)]
    rank = [jnp.sum(jnp.where(order == named[k], position, 0.0), axis=1, keepdims=True) for k in range(K)]
    pick = jnp.concatenate([(named[k] == position).astype(F32).astype(BF16) for k in range(K)], axis=0)
    place = jnp.concatenate([whole[:, 4 + k : 5 + k] for k in range(K)], axis=0).astype(jnp.int32)
    pieces = [split3(got_ref[:, h, :]) for h in range(2)]
    wanted = (iota((K * SEL, ZONES), 1) % ROWS) == (place % ROWS)
    gather = (iota((ZONES, 8), 0) // ROWS == iota((ZONES, 8), 1)).astype(F32).astype(BF16)
    values = jnp.zeros((K * SEL, 8), F32)
    for piece in range(3):
        low, high = dot(pick, pieces[0][piece]), dot(pick, pieces[1][piece])
        found = jnp.where(wanted, jnp.where(place < ROWS, low, high), 0.0)
        values = values + dot(found.astype(BF16), gather)

    mine = [values[k * SEL : (k + 1) * SEL] for k in range(K)]
    log = [mine[k][:, 3:4] for k in range(K)]
    color = [[mine[k][:, c : c + 1] for c in range(3)] for k in range(K)]
    ahead = [[rank[j] < rank[k] for j in range(K)] for k in range(K)]
    fade = [jnp.exp(sum(jnp.where(ahead[k][j], log[j], 0.0) for j in range(K) if j != k)) for k in range(K)]
    clear = jnp.exp(log[0] + log[1] + log[2] + log[3])
    rendered = [sum(fade[k] * color[k][c] for k in range(K)) + clear for c in range(3)]
    residual = [rendered[c] - reals[:, 8 + c : 9 + c] for c in range(3)]
    share = [fade[k] * sum(residual[c] * color[k][c] for c in range(3)) for k in range(K)]
    owned = [named[k] == part.astype(F32) for k in range(K)]
    own_rank = sum(jnp.where(owned[k], rank[k], 0.0) for k in range(K))
    own_fade = sum(jnp.where(owned[k], fade[k], 0.0) for k in range(K))
    dlog = sum(jnp.where(rank[k] > own_rank, share[k], 0.0) for k in range(K))
    dlog = dlog + clear * (residual[0] + residual[1] + residual[2])
    used = whole[:, 10:11] > 0.5
    dlog = jnp.where(used, dlog, 0.0)
    dcolor = [jnp.where(used, own_fade * residual[c], 0.0) for c in range(3)]
    diagonal = iota((8, 8), 0) == iota((8, 8), 1)
    for c in range(3):
        line = jnp.sum(jnp.where(diagonal, rendered[c][CAP:SEL], 0.0), axis=0, keepdims=True)
        rendered_ref[c] = line[:, 0:OWN]

    raw = [raw_ref[c * ROWS : (c + 1) * ROWS] for c in range(4)]
    step_d = halves(reals[0:CAP, 7:8])
    count_d = halves(whole[0:CAP, 8:9])
    scale, _, entering, weight, albedo = shade(raw, step_d, count_d)
    dcolor_d = [halves(dcolor[c][0:CAP]) for c in range(3)]
    gain = sum(dcolor_d[c] * albedo[c] for c in range(3))
    source, target = iota((2 * S, 2 * S), 0), iota((2 * S, 2 * S), 1)
    since = ((source >= target) & ((source < S) == (target < S))).astype(F32).astype(BF16)
    behind = split_dot(gain * weight, since)
    d_optical = gain * entering - behind - halves(dlog[0:CAP])
    draw[0:ROWS] = d_optical * scale / (1.0 + jnp.exp(-raw[0]))
    for c in range(3):
        draw[(c + 1) * ROWS : (c + 2) * ROWS] = weight * dcolor_d[c] * albedo[c] * (1.0 - albedo[c])
    draw[4 * ROWS :] = jnp.zeros((12 * ROWS, 2 * S), F32)

    wout[...] = jnp.zeros_like(wout)
    wout[0:4] = w_out_ref[...].astype(F32)
    w_out_t = wout[...].T.astype(BF16)
    w_mid_t = w_mid_ref[...].astype(F32).T.astype(BF16)
    grad_out = jnp.zeros((16, 256), F32)
    grad_mid = jnp.zeros((256, 256), F32)
    grad_in = jnp.zeros((64, 256), F32)
    for tile in range(ROWS // TILE):
        span = slice(tile * TILE * 128, (tile + 1) * TILE * 128)
        low = jnp.concatenate(
            [draw[pl.ds(tile * TILE + j, 16, stride=ROWS), :].astype(BF16) for j in range(TILE)], axis=1
        )
        two, one = two_ref[:, span], one_ref[:, span]
        grad_out = grad_out + dot_nt(low, two)
        d_two = jnp.where(two > 0, dot(w_out_t, low), 0.0).astype(BF16)
        grad_mid = grad_mid + dot_nt(d_two, one)
        d_one = jnp.where(one > 0, dot(w_mid_t, d_two), 0.0).astype(BF16)
        grad_in = grad_in + dot_nt(enc_ref[:, span], d_one)
    for q in range(4):
        grads_ref[q, 0:64] = grad_mid[64 * q : 64 * q + 64]
        grads_ref[q, 64:80] = grad_in[16 * q : 16 * q + 16]
        grads_ref[q, 80:88] = jnp.broadcast_to(grad_out[q : q + 1], (8, 256))


def unpack_kernel(all_ref, in_ref, mid_ref, out_ref):
    for q in range(4):
        mid_ref[64 * q : 64 * q + 64] = all_ref[q, 0:64]
        rows = min(16, FEATS - 16 * q)
        in_ref[16 * q : 16 * q + rows, 0, :] = all_ref[q, 64 : 64 + rows]
        out_ref[q : q + 1] = all_ref[q, 80:81]


def vmem(count):
    return [pl.BlockSpec(memory_space=pltpu.VMEM)] * count


def in_hbm(array):
    return pltpu.with_memory_space_constraint(array, pltpu.HBM)


def local(anchor, direct, entry, step, counts, crossing, order, target, w_in, w_mid, w_out):
    part = lax.axis_index("dom").astype(jnp.int32).reshape(1)
    entry, step, counts, crossing = (jnp.swapaxes(a, 1, 2) for a in (entry, step, counts, crossing))
    w_in_t = jnp.swapaxes(w_in, 1, 2)[0]
    scalar = pl.BlockSpec(memory_space=pltpu.SMEM)
    params = pltpu.CompilerParams(vmem_limit_bytes=40 * 1024 * 1024)
    shape = jax.ShapeDtypeStruct
    send, enc, one, two, raw, reals, whole, order_v, w_mid_v, w_out_v = pl.pallas_call(
        forward_kernel,
        out_shape=(
            shape((ZONES, 2, 128), F32),
            shape((64, COLS), BF16),
            shape((256, COLS), BF16),
            shape((256, COLS), BF16),
            shape((4 * ROWS, 128), F32),
            shape((SEL, 16), F32),
            shape((SEL, 16), F32),
            shape((1, NB, ZONES), jnp.int32),
            shape((256, 256), BF16),
            shape((4, 256), BF16),
        ),
        in_specs=[scalar] + [pl.BlockSpec(memory_space=pltpu.HBM)] * 11,
        out_specs=vmem(10),
        scratch_shapes=[
            pltpu.VMEM((3, 1, RG), F32),
            pltpu.VMEM((3, 1, RG), F32),
            pltpu.VMEM((1, K, RG), F32),
            pltpu.VMEM((1, K, RG), F32),
            pltpu.VMEM((1, K, RG), jnp.int32),
            pltpu.VMEM((1, K, RG), jnp.int32),
            pltpu.VMEM((3, 1, RG), F32),
            pltpu.VMEM((FEATS, 256), BF16),
            pltpu.VMEM((16, RG), F32),
            pltpu.VMEM((16, RG), F32),
            pltpu.VMEM((ZONES, RG), F32),
            pltpu.VMEM((64 * ROWS, 128), F32),
            pltpu.VMEM((64, 256), F32),
            pltpu.SemaphoreType.DMA((11,)),
        ],
        compiler_params=params,
        name="forward",
    )(part, *(in_hbm(a) for a in (
        anchor, direct, entry, step, counts, crossing, target, order, w_in_t, w_mid[0], w_out[0]
    )))
    got = lax.all_to_all(send, "dom", 0, 0)
    rendered, grads = pl.pallas_call(
        backward_kernel,
        out_shape=(shape((3, 1, OWN), F32), shape((4, CHUNK, 256), F32)),
        in_specs=[scalar] + vmem(10),
        out_specs=vmem(2),
        scratch_shapes=[pltpu.VMEM((16 * ROWS, 128), F32), pltpu.VMEM((16, 256), F32)],
        compiler_params=params,
        name="backward",
    )(part, got, order_v, reals, whole, raw, enc, one, two, w_mid_v, w_out_v)
    shares = lax.all_to_all(grads, "ray", 0, 0)
    total = jnp.sum(shares, axis=0)
    everything = lax.all_to_all(jnp.broadcast_to(total[None], grads.shape), "ray", 0, 0)
    grad_i, grad_m, grad_o = pl.pallas_call(
        unpack_kernel,
        out_shape=(shape((FEATS, 1, 256), F32), shape((256, 256), F32), shape((4, 256), F32)),
        in_specs=vmem(1),
        out_specs=vmem(3),
        compiler_params=params,
        name="unpack",
    )(everything)
    return rendered, jnp.transpose(grad_i, (1, 2, 0)), grad_m[None], grad_o[None]


def solution(mesh):
    in_specs = (
        P(None, "ray", None),
        P(None, "ray", None),
        P("ray", None, None),
        P("ray", None, None),
        P("ray", None, None),
        P("ray", None, None),
        P("ray", None, None),
        P(None, "ray", None),
        P("dom", None, None),
        P("dom", None, None),
        P("dom", None, None),
    )
    out_specs = (
        P(None, "ray", "dom"),
        P("dom", None, None),
        P("dom", None, None),
        P("dom", None, None),
    )
    return jax.shard_map(local, mesh=mesh, in_specs=in_specs, out_specs=out_specs, check_vma=False)
```

```python
import functools

import jax
import jax.numpy as jnp
from jax import lax
from jax.experimental import pallas as pl
from jax.experimental.pallas import tpu as pltpu
from jax.sharding import PartitionSpec as P

NFREQ = 10
FEATS = 63
S = 64
K = 4
NB = 8
CAP = 64
ZONES = 128
RG = 512
OWN = 4
ROWS = 32
SEL = 72
FIRST = 84
COLS = CAP * S
TILE = 16
CHUNK = 88
F32 = jnp.float32
BF16 = jnp.bfloat16


def iota(shape, dim):
    return lax.broadcasted_iota(jnp.int32, shape, dim)


def one_hot(mask):
    return mask.astype(F32).astype(BF16)


def split(x, terms):
    parts = []
    for _ in range(terms):
        parts.append(x.astype(BF16))
        x = x - parts[-1].astype(F32)
    return parts


def dot(a, b):
    return jnp.dot(a, b, preferred_element_type=F32)


def dot_nt(a, b):
    return lax.dot_general(a, b, (((1,), (1,)), ((), ())), preferred_element_type=F32)


def split_dot(x, exact):
    return sum(dot(part, exact) for part in split(x, 2))


def halves(column):
    lane = iota((ROWS, 2 * S), 1)
    return jnp.where(lane < S, column[0:ROWS], column[ROWS : 2 * ROWS])


def sin_cos(x):
    turns = jnp.floor(x * 0.6366197723675814 + 0.5)
    r = ((x - turns * 1.5703125) - turns * 4.837512969970703e-4) - turns * 7.54978995489188e-8
    z = r * r
    s = ((-1.9515295891e-4 * z + 8.3321608736e-3) * z - 1.6666654611e-1) * z * r + r
    c = ((2.443315711809948e-5 * z - 1.388731625493765e-3) * z + 4.166664568298827e-2) * z * z - 0.5 * z + 1.0
    quadrant = turns.astype(jnp.int32)
    swap = (quadrant & 1) == 1
    sin_r = jnp.where(swap, c, s)
    cos_r = jnp.where(swap, s, c)
    sin_r = jnp.where((quadrant & 2) == 2, -sin_r, sin_r)
    cos_r = jnp.where(((quadrant + 1) & 2) == 2, -cos_r, cos_r)
    return sin_r, cos_r


def shade(raw, step_d, count_d):
    index = iota(step_d.shape, 1) & (S - 1)
    scale = jnp.where(index.astype(F32) < count_d, step_d, 0.0)
    decay = jnp.exp(-jnp.abs(raw[0]))
    density = jnp.maximum(raw[0], 0.0) + jnp.log1p(decay)
    optical = density * scale
    source, target = iota((2 * S, 2 * S), 0), iota((2 * S, 2 * S), 1)
    upto = one_hot((source <= target) & ((source < S) == (target < S)))
    reached = split_dot(optical, upto)
    entering = jnp.exp(optical - reached)
    weight = entering - jnp.exp(-reached)
    albedo = [1.0 / (1.0 + jnp.exp(-raw[c])) for c in (1, 2, 3)]
    return scale, optical, entering, weight, albedo


def forward_kernel(
    part_ref, anchor_hbm, direct_hbm, entry_hbm, step_hbm, counts_hbm, crossing_hbm, target_hbm, order_hbm,
    w_in_hbm, w_mid_hbm, w_out_hbm,
    send_ref, enc_ref, one_ref, two_ref, pick_ref, low_ref, high_ref, info_ref, shade_ref, w_mid_t_ref, w_out_t_ref,
    anchor_ref, direct_ref, entry_ref, step_ref, counts_ref, crossing_ref, target_ref, order_ref,
    w_in_ref, w_mid_ref, w_out_ref, vals, ints, ranks, feats, raws, win, wout, sems,
):
    copies = [
        pltpu.make_async_copy(source, target, sems.at[i])
        for i, (source, target) in enumerate((
            (crossing_hbm, crossing_ref), (entry_hbm, entry_ref), (step_hbm, step_ref), (counts_hbm, counts_ref),
            (anchor_hbm, anchor_ref), (direct_hbm, direct_ref), (w_in_hbm, w_in_ref), (w_mid_hbm, w_mid_ref),
            (w_out_hbm, w_out_ref), (target_hbm, target_ref), (order_hbm, order_ref),
        ))
    ]
    for copy in copies:
        copy.start()
    part = part_ref[0]
    earlier = one_hot(iota((RG, RG), 0) < iota((RG, RG), 1))
    vals[...] = jnp.zeros_like(vals)
    ints[...] = jnp.zeros_like(ints)
    win[...] = jnp.zeros_like(win)
    wout[...] = jnp.zeros_like(wout)
    feats[FEATS * ROWS : (FEATS + 1) * ROWS] = jnp.zeros((ROWS, 2 * S), F32)
    for copy in copies:
        copy.wait()

    crossing = crossing_ref[0]
    own = crossing == part
    crossed = own[0:1] | own[1:2] | own[2:3] | own[3:4]
    place_own = dot(one_hot(jnp.broadcast_to(crossed, (16, RG))), earlier)[0:1]
    place_own = jnp.where(crossed, place_own.astype(jnp.int32), -1)
    row, ray = iota((SEL, RG), 0), iota((1, RG), 1)
    in_slot = (row < CAP) & (place_own == row)
    own_ray = (row >= CAP) & (row < CAP + OWN) & (ray == part * OWN + (row - CAP))
    selector = one_hot(in_slot | own_ray)

    def of_own(ref):
        return jnp.sum(jnp.where(own, ref[0].astype(F32), 0.0), axis=0, keepdims=True)

    for d in range(3):
        vals[d : d + 1] = anchor_ref[d]
        vals[3 + d : 4 + d] = direct_ref[d]
        vals[16 + d : 17 + d] = target_ref[d]
    vals[6:7] = of_own(entry_ref)
    vals[7:8] = of_own(step_ref)
    vals[8:9] = of_own(counts_ref)
    reals = sum(dot_nt(selector, piece) for piece in split(vals[0:16], 3))

    columns = [halves(reals[0:CAP, j : j + 1]) for j in range(9)]
    step_d, count_d = columns[7], columns[8]
    index = (iota((ROWS, 2 * S), 1) & (S - 1)).astype(F32)
    depth = columns[6] + (index + 0.5) * step_d
    for d in range(3):
        point = columns[d] + depth * columns[3 + d]
        feats[d * ROWS : (d + 1) * ROWS] = point
        sin_x, cos_x = sin_cos(point)
        for level in range(NFREQ):
            at = 3 + 6 * level + d
            feats[at * ROWS : (at + 1) * ROWS] = sin_x
            feats[(at + 3) * ROWS : (at + 4) * ROWS] = cos_x
            sin_x, cos_x = 2.0 * sin_x * cos_x, 1.0 - 2.0 * sin_x * sin_x

    win[0:FEATS] = w_in_ref[...].astype(F32)
    w_in = win[...].T.astype(BF16)
    w_mid = w_mid_ref[...]
    w_out = w_out_ref[...]
    half = one_hot(iota((8, 2 * S), 0) == iota((8, 2 * S), 1) // S)
    sent = []
    for tile in range(ROWS // TILE):
        span = slice(tile * TILE * 128, (tile + 1) * TILE * 128)
        encoded = jnp.concatenate(
            [feats[pl.ds(tile * TILE + j, FEATS + 1, stride=ROWS), :].astype(BF16) for j in range(TILE)], axis=1
        )
        enc_ref[:, span] = encoded
        one = jnp.maximum(dot(w_in, encoded), 0.0).astype(BF16)
        one_ref[:, span] = one
        two = jnp.maximum(dot(w_mid, one), 0.0).astype(BF16)
        two_ref[:, span] = two
        raw = dot(w_out, two)
        for j in range(TILE):
            raws[pl.ds(tile * TILE + j, 4, stride=ROWS), :] = raw[:, j * 128 : (j + 1) * 128]
        rows = slice(tile * TILE, (tile + 1) * TILE)
        raw = [raws[c * ROWS + tile * TILE : c * ROWS + (tile + 1) * TILE] for c in range(4)]
        scale, optical, entering, weight, albedo = shade(raw, step_d[rows], count_d[rows])
        sums = jnp.concatenate([weight * albedo[0], weight * albedo[1], weight * albedo[2], -optical], axis=0)
        sent.append(sum(dot_nt(half, piece) for piece in split(sums, 2)))
        kept = [entering, weight, scale / (1.0 + jnp.exp(-raw[0]))] + albedo
        kept = kept + [weight * a * (1.0 - a) for a in albedo]
        for i, value in enumerate(kept):
            shade_ref[i * ROWS + tile * TILE : i * ROWS + (tile + 1) * TILE] = value
    sent = jnp.concatenate(sent, axis=1)
    send_ref[...] = jnp.broadcast_to(sent[None, 0:2], send_ref.shape)

    zone = iota((ZONES, RG), 0)
    names = [zone == crossing[k : k + 1] for k in range(K)]
    ranks[...] = dot(one_hot(names[0] | names[1] | names[2] | names[3]), earlier)
    place_all = ranks[...]
    ints[0:4] = crossing.astype(F32)
    for k in range(K):
        ints[4 + k : 5 + k] = jnp.sum(jnp.where(names[k], place_all, 0.0), axis=0, keepdims=True)
    ints[8:9] = (ray // (RG // NB)).astype(F32)
    ints[9:10] = jnp.ones((1, RG), F32)
    whole = ints[...].astype(BF16)
    table = dot_nt(selector, whole)
    info_ref[0:16] = dot_nt(whole, selector)
    info_ref[16:24] = sum(dot_nt(piece, selector) for piece in split(vals[16:24], 3))
    bundle = one_hot(table[:, 8:9].astype(jnp.int32) == iota((SEL, NB), 1))
    order = dot(bundle, order_ref[0].astype(F32).astype(BF16))
    lane = iota((SEL, ZONES), 1)
    lister = ((lane + FIRST) & (ZONES - 1)).astype(F32)
    positions = iota((8, ZONES), 1).astype(F32).astype(BF16)
    for k in range(K):
        named = table[:, k : k + 1]
        place = table[:, 4 + k : 5 + k].astype(jnp.int32)
        pick_ref[k * SEL : (k + 1) * SEL] = one_hot(named == lister)
        wanted = ((lane & 15) == (place & 15)) & ((lane >> 6) == ((place >> 4) & 1))
        low_ref[k * SEL : (k + 1) * SEL] = (wanted & (place < ROWS)).astype(F32)
        high_ref[k * SEL : (k + 1) * SEL] = (wanted & (place >= ROWS)).astype(F32)
        info_ref[24 + k : 25 + k] = dot_nt(positions, one_hot(order == named))[0:1]
    info_ref[28:32] = jnp.zeros((4, SEL), F32)
    wout[0:4] = w_out.astype(F32)
    w_out_t_ref[...] = wout[...].T.astype(BF16)
    w_mid_t_ref[...] = w_mid.astype(F32).T.astype(BF16)


def backward_kernel(
    part_ref, got_ref, pick_ref, low_ref, high_ref, info_ref, shade_ref, enc_ref, one_ref, two_ref,
    w_mid_t_ref, w_out_t_ref,
    rendered_ref, grads_ref,
    draw,
):
    part = part_ref[0].astype(F32)
    pieces = split(jnp.concatenate([got_ref[:, 0, :], got_ref[:, 1, :]], axis=1), 2)
    gather = one_hot(iota((8, ZONES), 0) == ((iota((8, ZONES), 1) >> 4) & 3))
    pick = pick_ref[...]
    low, high = low_ref[...] > 0.5, high_ref[...] > 0.5
    values = jnp.zeros((8, K * SEL), F32)
    for piece in pieces:
        both = dot(pick, piece)
        found = jnp.where(low, both[:, 0:128], jnp.where(high, both[:, 128:256], 0.0))
        values = values + dot_nt(gather, found.astype(BF16))

    mine = [values[:, k * SEL : (k + 1) * SEL] for k in range(K)]
    log = [mine[k][3:4] for k in range(K)]
    color = [mine[k][0:3] for k in range(K)]
    named = [info_ref[k : k + 1] for k in range(K)]
    used = info_ref[9:10] > 0.5
    goal = info_ref[16:19]
    rank = [info_ref[24 + k : 25 + k] for k in range(K)]
    fade = [
        jnp.exp(sum(jnp.where(rank[j] < rank[k], log[j], 0.0) for j in range(K) if j != k)) for k in range(K)
    ]
    clear = jnp.exp(log[0] + log[1] + log[2] + log[3])
    rendered = sum(fade[k] * color[k] for k in range(K)) + clear
    residual = rendered - goal
    share = [fade[k] * jnp.sum(residual * color[k], axis=0, keepdims=True) for k in range(K)]
    owned = [named[k] == part for k in range(K)]
    own_rank = sum(jnp.where(owned[k], rank[k], 0.0) for k in range(K))
    own_fade = sum(jnp.where(owned[k], fade[k], 0.0) for k in range(K))
    dlog = sum(jnp.where(rank[k] > own_rank, share[k], 0.0) for k in range(K))
    dlog = dlog + clear * jnp.sum(residual, axis=0, keepdims=True)
    dcolor = own_fade * residual
    for c in range(3):
        rendered_ref[c] = rendered[c : c + 1, CAP : CAP + OWN]
    slots = jnp.concatenate([dcolor, dlog, jnp.zeros((4, SEL), F32)], axis=0)
    slots = jnp.where(used, slots, 0.0)
    slots = jnp.concatenate([slots, jnp.zeros((8, 128 - SEL), F32)], axis=1).T

    entering, weight, slope, *rest = [shade_ref[i * ROWS : (i + 1) * ROWS] for i in range(9)]
    dcolor_d = [halves(slots[0:CAP, c : c + 1]) for c in range(3)]
    gain = sum(dcolor_d[c] * rest[c] for c in range(3))
    source, target = iota((2 * S, 2 * S), 0), iota((2 * S, 2 * S), 1)
    since = one_hot((source >= target) & ((source < S) == (target < S)))
    behind = split_dot(gain * weight, since)
    draw[0:ROWS] = (gain * entering - behind - halves(slots[0:CAP, 3:4])) * slope
    for c in range(3):
        draw[(c + 1) * ROWS : (c + 2) * ROWS] = dcolor_d[c] * rest[3 + c]
    draw[4 * ROWS :] = jnp.zeros((12 * ROWS, 2 * S), F32)

    w_out_t, w_mid_t = w_out_t_ref[...], w_mid_t_ref[...]
    grad_out = jnp.zeros((16, 256), F32)
    grad_mid = jnp.zeros((256, 256), F32)
    grad_in = jnp.zeros((256, 64), F32)
    zero = jnp.zeros((), BF16)
    for tile in range(ROWS // TILE):
        span = slice(tile * TILE * 128, (tile + 1) * TILE * 128)
        low = jnp.concatenate(
            [draw[pl.ds(tile * TILE + j, 16, stride=ROWS), :].astype(BF16) for j in range(TILE)], axis=1
        )
        two, one = two_ref[:, span], one_ref[:, span]
        grad_out = grad_out + dot_nt(low, two)
        d_two = jnp.where(two > 0, dot(w_out_t, low).astype(BF16), zero)
        grad_mid = grad_mid + dot_nt(d_two, one)
        d_one = jnp.where(one > 0, dot(w_mid_t, d_two).astype(BF16), zero)
        grad_in = grad_in + dot_nt(d_one, enc_ref[:, span])
    grad_in = grad_in.T
    for q in range(4):
        grads_ref[q, 0:64] = grad_mid[64 * q : 64 * q + 64]
        grads_ref[q, 64:80] = grad_in[16 * q : 16 * q + 16]
        grads_ref[q, 80:88] = jnp.broadcast_to(grad_out[q : q + 1], (8, 256))


def unpack_kernel(all_ref, in_ref, mid_ref, out_ref):
    for q in range(4):
        mid_ref[64 * q : 64 * q + 64] = all_ref[q, 0:64]
        rows = min(16, FEATS - 16 * q)
        in_ref[16 * q : 16 * q + rows, 0, :] = all_ref[q, 64 : 64 + rows]
        out_ref[q : q + 1] = all_ref[q, 80:81]


def vmem(count):
    return [pl.BlockSpec(memory_space=pltpu.VMEM)] * count


def in_hbm(array):
    return pltpu.with_memory_space_constraint(array, pltpu.HBM)


def local(anchor, direct, entry, step, counts, crossing, order, target, w_in, w_mid, w_out):
    part = lax.axis_index("dom").astype(jnp.int32).reshape(1)
    entry, step, counts, crossing = (jnp.swapaxes(a, 1, 2) for a in (entry, step, counts, crossing))
    w_in_t = jnp.swapaxes(w_in, 1, 2)[0]
    scalar = pl.BlockSpec(memory_space=pltpu.SMEM)
    params = pltpu.CompilerParams(vmem_limit_bytes=40 * 1024 * 1024)
    shape = jax.ShapeDtypeStruct
    arguments = [in_hbm(a) for a in (
        anchor, direct, entry, step, counts, crossing, target, order, w_in_t, w_mid[0], w_out[0]
    )]
    send, *kept = pl.pallas_call(
        forward_kernel,
        out_shape=(
            shape((ZONES, 2, 128), F32),
            shape((64, COLS), BF16),
            shape((256, COLS), BF16),
            shape((256, COLS), BF16),
            shape((K * SEL, ZONES), BF16),
            shape((K * SEL, ZONES), F32),
            shape((K * SEL, ZONES), F32),
            shape((32, SEL), F32),
            shape((9 * ROWS, 128), F32),
            shape((256, 256), BF16),
            shape((256, 16), BF16),
        ),
        in_specs=[scalar] + [pl.BlockSpec(memory_space=pltpu.HBM)] * 11,
        out_specs=vmem(11),
        scratch_shapes=[pltpu.VMEM(a.shape, a.dtype) for a in arguments]
        + [
            pltpu.VMEM((24, RG), F32),
            pltpu.VMEM((16, RG), F32),
            pltpu.VMEM((ZONES, RG), F32),
            pltpu.VMEM((64 * ROWS, 128), F32),
            pltpu.VMEM((4 * ROWS, 128), F32),
            pltpu.VMEM((64, 256), F32),
            pltpu.VMEM((16, 256), F32),
            pltpu.SemaphoreType.DMA((11,)),
        ],
        compiler_params=params,
        name="forward",
    )(part, *arguments)
    listed = [[(i + FIRST) % ZONES for i in range(ZONES)]]
    got = lax.all_to_all(send, "dom", 0, 0, axis_index_groups=listed)
    enc, one, two, pick, low, high, info, shaded, w_mid_t, w_out_t = kept
    rendered, grads = pl.pallas_call(
        backward_kernel,
        out_shape=(shape((3, 1, OWN), F32), shape((4, CHUNK, 256), F32)),
        in_specs=[scalar] + vmem(11),
        out_specs=vmem(2),
        scratch_shapes=[pltpu.VMEM((16 * ROWS, 128), F32)],
        compiler_params=params,
        name="backward",
    )(part, got, pick, low, high, info, shaded, enc, one, two, w_mid_t, w_out_t)
    shares = lax.all_to_all(grads, "ray", 0, 0)
    total = jnp.sum(shares, axis=0)
    everything = lax.all_to_all(jnp.broadcast_to(total[None], grads.shape), "ray", 0, 0)
    grad_i, grad_m, grad_o = pl.pallas_call(
        unpack_kernel,
        out_shape=(shape((FEATS, 1, 256), F32), shape((256, 256), F32), shape((4, 256), F32)),
        in_specs=vmem(1),
        out_specs=vmem(3),
        compiler_params=params,
        name="unpack",
    )(everything)
    return rendered, jnp.transpose(grad_i, (1, 2, 0)), grad_m[None], grad_o[None]


def solution(mesh):
    in_specs = (
        P(None, "ray", None),
        P(None, "ray", None),
        P("ray", None, None),
        P("ray", None, None),
        P("ray", None, None),
        P("ray", None, None),
        P("ray", None, None),
        P(None, "ray", None),
        P("dom", None, None),
        P("dom", None, None),
        P("dom", None, None),
    )
    out_specs = (
        P(None, "ray", "dom"),
        P("dom", None, None),
        P("dom", None, None),
        P("dom", None, None),
    )
    return jax.shard_map(local, mesh=mesh, in_specs=in_specs, out_specs=out_specs, check_vma=False)
```

```python
import functools

import jax
import jax.numpy as jnp
from jax import lax
from jax.experimental import pallas as pl
from jax.experimental.pallas import tpu as pltpu
from jax.sharding import PartitionSpec as P

NFREQ = 10
FEATS = 63
S = 64
K = 4
NB = 8
CAP = 64
ZONES = 128
RG = 512
OWN = 4
ROWS = 32
SEL = 72
FIRST = 84
COLS = CAP * S
TILE = 16
CHUNK = 88
F32 = jnp.float32
BF16 = jnp.bfloat16


def iota(shape, dim):
    return lax.broadcasted_iota(jnp.int32, shape, dim)


def one_hot(mask):
    return mask.astype(F32).astype(BF16)


def split(x, terms):
    parts = []
    for _ in range(terms):
        parts.append(x.astype(BF16))
        x = x - parts[-1].astype(F32)
    return parts


def dot(a, b):
    return jnp.dot(a, b, preferred_element_type=F32)


def dot_nt(a, b):
    return lax.dot_general(a, b, (((1,), (1,)), ((), ())), preferred_element_type=F32)


def split_dot(x, exact):
    return sum(dot(part, exact) for part in split(x, 2))


def halves(column):
    lane = iota((ROWS, 2 * S), 1)
    return jnp.where(lane < S, column[0:ROWS], column[ROWS : 2 * ROWS])


def sin_cos(x):
    turns = jnp.floor(x * 0.6366197723675814 + 0.5)
    r = ((x - turns * 1.5703125) - turns * 4.837512969970703e-4) - turns * 7.54978995489188e-8
    z = r * r
    s = ((-1.9515295891e-4 * z + 8.3321608736e-3) * z - 1.6666654611e-1) * z * r + r
    c = ((2.443315711809948e-5 * z - 1.388731625493765e-3) * z + 4.166664568298827e-2) * z * z - 0.5 * z + 1.0
    quadrant = turns.astype(jnp.int32)
    swap = (quadrant & 1) == 1
    sin_r = jnp.where(swap, c, s)
    cos_r = jnp.where(swap, s, c)
    sin_r = jnp.where((quadrant & 2) == 2, -sin_r, sin_r)
    cos_r = jnp.where(((quadrant + 1) & 2) == 2, -cos_r, cos_r)
    return sin_r, cos_r


def shade(raw, step_d, count_d):
    index = iota(step_d.shape, 1) & (S - 1)
    scale = jnp.where(index.astype(F32) < count_d, step_d, 0.0)
    decay = jnp.exp(-jnp.abs(raw[0]))
    density = jnp.maximum(raw[0], 0.0) + jnp.log1p(decay)
    optical = density * scale
    source, target = iota((2 * S, 2 * S), 0), iota((2 * S, 2 * S), 1)
    upto = one_hot((source <= target) & ((source < S) == (target < S)))
    reached = split_dot(optical, upto)
    entering = jnp.exp(optical - reached)
    weight = entering - jnp.exp(-reached)
    albedo = [1.0 / (1.0 + jnp.exp(-raw[c])) for c in (1, 2, 3)]
    return scale, optical, entering, weight, albedo


def forward_kernel(
    part_ref, anchor_hbm, direct_hbm, entry_hbm, step_hbm, counts_hbm, crossing_hbm, target_hbm, order_hbm,
    w_in_hbm, w_mid_hbm, w_out_hbm,
    send_ref, enc_ref, one_ref, two_ref, pick_ref, low_ref, high_ref, info_ref, shade_ref, w_mid_t_ref, w_out_t_ref,
    anchor_ref, direct_ref, entry_ref, step_ref, counts_ref, crossing_ref, target_ref, order_ref,
    w_in_ref, w_mid_ref, w_out_ref, vals, ints, ranks, feats, raws, win, wout, sems,
):
    copies = [
        pltpu.make_async_copy(source, target, sems.at[i])
        for i, (source, target) in enumerate((
            (crossing_hbm, crossing_ref), (entry_hbm, entry_ref), (step_hbm, step_ref), (counts_hbm, counts_ref),
            (anchor_hbm, anchor_ref), (direct_hbm, direct_ref), (w_in_hbm, w_in_ref), (w_mid_hbm, w_mid_ref),
            (w_out_hbm, w_out_ref), (target_hbm, target_ref), (order_hbm, order_ref),
        ))
    ]
    for copy in copies:
        copy.start()
    part = part_ref[0]
    earlier = one_hot(iota((RG, RG), 0) < iota((RG, RG), 1))
    vals[...] = jnp.zeros_like(vals)
    ints[...] = jnp.zeros_like(ints)
    win[...] = jnp.zeros_like(win)
    wout[...] = jnp.zeros_like(wout)
    feats[FEATS * ROWS : (FEATS + 1) * ROWS] = jnp.zeros((ROWS, 2 * S), F32)
    for copy in copies:
        copy.wait()

    crossing = crossing_ref[0]
    own = crossing == part
    crossed = own[0:1] | own[1:2] | own[2:3] | own[3:4]
    place_own = dot(one_hot(jnp.broadcast_to(crossed, (16, RG))), earlier)[0:1]
    place_own = jnp.where(crossed, place_own.astype(jnp.int32), -1)
    row, ray = iota((SEL, RG), 0), iota((1, RG), 1)
    in_slot = (row < CAP) & (place_own == row)
    own_ray = (row >= CAP) & (row < CAP + OWN) & (ray == part * OWN + (row - CAP))
    selector = one_hot(in_slot | own_ray)

    def of_own(ref):
        return jnp.sum(jnp.where(own, ref[0].astype(F32), 0.0), axis=0, keepdims=True)

    for d in range(3):
        vals[d : d + 1] = anchor_ref[d]
        vals[3 + d : 4 + d] = direct_ref[d]
        vals[16 + d : 17 + d] = target_ref[d]
    vals[6:7] = of_own(entry_ref)
    vals[7:8] = of_own(step_ref)
    vals[8:9] = of_own(counts_ref)
    reals = sum(dot_nt(selector, piece) for piece in split(vals[0:16], 3))

    columns = [halves(reals[0:CAP, j : j + 1]) for j in range(9)]
    step_d, count_d = columns[7], columns[8]
    index = (iota((ROWS, 2 * S), 1) & (S - 1)).astype(F32)
    depth = columns[6] + (index + 0.5) * step_d
    for d in range(3):
        point = columns[d] + depth * columns[3 + d]
        feats[d * ROWS : (d + 1) * ROWS] = point
        sin_x, cos_x = sin_cos(point)
        for level in range(NFREQ):
            at = 3 + 6 * level + d
            feats[at * ROWS : (at + 1) * ROWS] = sin_x
            feats[(at + 3) * ROWS : (at + 4) * ROWS] = cos_x
            sin_x, cos_x = 2.0 * sin_x * cos_x, 1.0 - 2.0 * sin_x * sin_x

    win[0:FEATS] = w_in_ref[...].astype(F32)
    w_in = win[...].T.astype(BF16)
    w_mid = w_mid_ref[...]
    w_out = w_out_ref[...]
    half = one_hot(iota((8, 2 * S), 0) == iota((8, 2 * S), 1) // S)
    sent = []
    for tile in range(ROWS // TILE):
        span = slice(tile * TILE * 128, (tile + 1) * TILE * 128)
        encoded = jnp.concatenate(
            [feats[pl.ds(tile * TILE + j, FEATS + 1, stride=ROWS), :].astype(BF16) for j in range(TILE)], axis=1
        )
        enc_ref[:, span] = encoded
        one = jnp.maximum(dot(w_in, encoded), 0.0).astype(BF16)
        one_ref[:, span] = one
        two = jnp.maximum(dot(w_mid, one), 0.0).astype(BF16)
        two_ref[:, span] = two
        raw = dot(w_out, two)
        for j in range(TILE):
            raws[pl.ds(tile * TILE + j, 4, stride=ROWS), :] = raw[:, j * 128 : (j + 1) * 128]
        rows = slice(tile * TILE, (tile + 1) * TILE)
        raw = [raws[c * ROWS + tile * TILE : c * ROWS + (tile + 1) * TILE] for c in range(4)]
        scale, optical, entering, weight, albedo = shade(raw, step_d[rows], count_d[rows])
        sums = jnp.concatenate([weight * albedo[0], weight * albedo[1], weight * albedo[2], -optical], axis=0)
        sent.append(sum(dot_nt(half, piece) for piece in split(sums, 2)))
        kept = [entering, weight, scale / (1.0 + jnp.exp(-raw[0]))] + albedo
        kept = kept + [weight * a * (1.0 - a) for a in albedo]
        for i, value in enumerate(kept):
            shade_ref[i * ROWS + tile * TILE : i * ROWS + (tile + 1) * TILE] = value
    sent = jnp.concatenate(sent, axis=1)
    send_ref[...] = jnp.broadcast_to(sent[None, 0:2], send_ref.shape)

    zone = iota((ZONES, RG), 0)
    names = [zone == crossing[k : k + 1] for k in range(K)]
    ranks[...] = dot(one_hot(names[0] | names[1] | names[2] | names[3]), earlier)
    place_all = ranks[...]
    ints[0:4] = crossing.astype(F32)
    for k in range(K):
        ints[4 + k : 5 + k] = jnp.sum(jnp.where(names[k], place_all, 0.0), axis=0, keepdims=True)
    ints[8:9] = (ray // (RG // NB)).astype(F32)
    ints[9:10] = jnp.ones((1, RG), F32)
    whole = ints[...].astype(BF16)
    table = dot_nt(selector, whole)
    info_ref[0:16] = dot_nt(whole, selector)
    info_ref[16:24] = sum(dot_nt(piece, selector) for piece in split(vals[16:24], 3))
    bundle = one_hot(table[:, 8:9].astype(jnp.int32) == iota((SEL, NB), 1))
    order = dot(bundle, order_ref[0].astype(F32).astype(BF16))
    lane = iota((SEL, ZONES), 1)
    lister = ((2 * lane + FIRST) & (ZONES - 1)) + jnp.where(lane < ZONES // 2, part & 1, 1 - (part & 1))
    lister = lister.astype(F32)
    positions = iota((8, ZONES), 1).astype(F32).astype(BF16)
    for k in range(K):
        named = table[:, k : k + 1]
        place = table[:, 4 + k : 5 + k].astype(jnp.int32)
        pick_ref[k * SEL : (k + 1) * SEL] = one_hot(named == lister)
        wanted = ((lane & 15) == (place & 15)) & ((lane >> 6) == ((place >> 4) & 1))
        low_ref[k * SEL : (k + 1) * SEL] = (wanted & (place < ROWS)).astype(F32)
        high_ref[k * SEL : (k + 1) * SEL] = (wanted & (place >= ROWS)).astype(F32)
        info_ref[24 + k : 25 + k] = dot_nt(positions, one_hot(order == named))[0:1]
    info_ref[28:32] = jnp.zeros((4, SEL), F32)
    wout[0:4] = w_out.astype(F32)
    w_out_t_ref[...] = wout[...].T.astype(BF16)
    w_mid_t_ref[...] = w_mid.astype(F32).T.astype(BF16)


def backward_kernel(
    part_ref, near_ref, other_ref, pick_ref, low_ref, high_ref, info_ref, shade_ref, enc_ref, one_ref, two_ref,
    w_mid_t_ref, w_out_t_ref,
    rendered_ref, grads_ref,
    draw,
):
    part = part_ref[0].astype(F32)
    got = [jnp.concatenate([near_ref[:, h, :], other_ref[:, h, :]], axis=0) for h in range(2)]
    pieces = split(jnp.concatenate(got, axis=1), 2)
    gather = one_hot(iota((8, ZONES), 0) == ((iota((8, ZONES), 1) >> 4) & 3))
    pick = pick_ref[...]
    low, high = low_ref[...] > 0.5, high_ref[...] > 0.5
    values = jnp.zeros((8, K * SEL), F32)
    for piece in pieces:
        both = dot(pick, piece)
        found = jnp.where(low, both[:, 0:128], jnp.where(high, both[:, 128:256], 0.0))
        values = values + dot_nt(gather, found.astype(BF16))

    mine = [values[:, k * SEL : (k + 1) * SEL] for k in range(K)]
    log = [mine[k][3:4] for k in range(K)]
    color = [mine[k][0:3] for k in range(K)]
    named = [info_ref[k : k + 1] for k in range(K)]
    used = info_ref[9:10] > 0.5
    goal = info_ref[16:19]
    rank = [info_ref[24 + k : 25 + k] for k in range(K)]
    fade = [
        jnp.exp(sum(jnp.where(rank[j] < rank[k], log[j], 0.0) for j in range(K) if j != k)) for k in range(K)
    ]
    clear = jnp.exp(log[0] + log[1] + log[2] + log[3])
    rendered = sum(fade[k] * color[k] for k in range(K)) + clear
    residual = rendered - goal
    share = [fade[k] * jnp.sum(residual * color[k], axis=0, keepdims=True) for k in range(K)]
    owned = [named[k] == part for k in range(K)]
    own_rank = sum(jnp.where(owned[k], rank[k], 0.0) for k in range(K))
    own_fade = sum(jnp.where(owned[k], fade[k], 0.0) for k in range(K))
    dlog = sum(jnp.where(rank[k] > own_rank, share[k], 0.0) for k in range(K))
    dlog = dlog + clear * jnp.sum(residual, axis=0, keepdims=True)
    dcolor = own_fade * residual
    for c in range(3):
        rendered_ref[c] = rendered[c : c + 1, CAP : CAP + OWN]
    slots = jnp.concatenate([dcolor, dlog, jnp.zeros((4, SEL), F32)], axis=0)
    slots = jnp.where(used, slots, 0.0)
    slots = jnp.concatenate([slots, jnp.zeros((8, 128 - SEL), F32)], axis=1).T

    entering, weight, slope, *rest = [shade_ref[i * ROWS : (i + 1) * ROWS] for i in range(9)]
    dcolor_d = [halves(slots[0:CAP, c : c + 1]) for c in range(3)]
    gain = sum(dcolor_d[c] * rest[c] for c in range(3))
    source, target = iota((2 * S, 2 * S), 0), iota((2 * S, 2 * S), 1)
    since = one_hot((source >= target) & ((source < S) == (target < S)))
    behind = split_dot(gain * weight, since)
    draw[0:ROWS] = (gain * entering - behind - halves(slots[0:CAP, 3:4])) * slope
    for c in range(3):
        draw[(c + 1) * ROWS : (c + 2) * ROWS] = dcolor_d[c] * rest[3 + c]
    draw[4 * ROWS :] = jnp.zeros((12 * ROWS, 2 * S), F32)

    w_out_t, w_mid_t = w_out_t_ref[...], w_mid_t_ref[...]
    grad_out = jnp.zeros((16, 256), F32)
    grad_mid = jnp.zeros((256, 256), F32)
    grad_in = jnp.zeros((256, 64), F32)
    zero = jnp.zeros((), BF16)
    for tile in range(ROWS // TILE):
        span = slice(tile * TILE * 128, (tile + 1) * TILE * 128)
        low = jnp.concatenate(
            [draw[pl.ds(tile * TILE + j, 16, stride=ROWS), :].astype(BF16) for j in range(TILE)], axis=1
        )
        two, one = two_ref[:, span], one_ref[:, span]
        grad_out = grad_out + dot_nt(low, two)
        d_two = jnp.where(two > 0, dot(w_out_t, low).astype(BF16), zero)
        grad_mid = grad_mid + dot_nt(d_two, one)
        d_one = jnp.where(one > 0, dot(w_mid_t, d_two).astype(BF16), zero)
        grad_in = grad_in + dot_nt(d_one, enc_ref[:, span])
    grad_in = grad_in.T
    for q in range(4):
        grads_ref[q, 0:64] = grad_mid[64 * q : 64 * q + 64]
        grads_ref[q, 64:80] = grad_in[16 * q : 16 * q + 16]
        grads_ref[q, 80:88] = jnp.broadcast_to(grad_out[q : q + 1], (8, 256))


def unpack_kernel(all_ref, in_ref, mid_ref, out_ref):
    for q in range(4):
        mid_ref[64 * q : 64 * q + 64] = all_ref[q, 0:64]
        rows = min(16, FEATS - 16 * q)
        in_ref[16 * q : 16 * q + rows, 0, :] = all_ref[q, 64 : 64 + rows]
        out_ref[q : q + 1] = all_ref[q, 80:81]


def vmem(count):
    return [pl.BlockSpec(memory_space=pltpu.VMEM)] * count


def in_hbm(array):
    return pltpu.with_memory_space_constraint(array, pltpu.HBM)


def local(anchor, direct, entry, step, counts, crossing, order, target, w_in, w_mid, w_out):
    part = lax.axis_index("dom").astype(jnp.int32).reshape(1)
    entry, step, counts, crossing = (jnp.swapaxes(a, 1, 2) for a in (entry, step, counts, crossing))
    w_in_t = jnp.swapaxes(w_in, 1, 2)[0]
    scalar = pl.BlockSpec(memory_space=pltpu.SMEM)
    params = pltpu.CompilerParams(vmem_limit_bytes=40 * 1024 * 1024)
    shape = jax.ShapeDtypeStruct
    arguments = [in_hbm(a) for a in (
        anchor, direct, entry, step, counts, crossing, target, order, w_in_t, w_mid[0], w_out[0]
    )]
    send, *kept = pl.pallas_call(
        forward_kernel,
        out_shape=(
            shape((ZONES // 2, 2, 128), F32),
            shape((64, COLS), BF16),
            shape((256, COLS), BF16),
            shape((256, COLS), BF16),
            shape((K * SEL, ZONES), BF16),
            shape((K * SEL, ZONES), F32),
            shape((K * SEL, ZONES), F32),
            shape((32, SEL), F32),
            shape((9 * ROWS, 128), F32),
            shape((256, 256), BF16),
            shape((256, 16), BF16),
        ),
        in_specs=[scalar] + [pl.BlockSpec(memory_space=pltpu.HBM)] * 11,
        out_specs=vmem(11),
        scratch_shapes=[pltpu.VMEM(a.shape, a.dtype) for a in arguments]
        + [
            pltpu.VMEM((24, RG), F32),
            pltpu.VMEM((16, RG), F32),
            pltpu.VMEM((ZONES, RG), F32),
            pltpu.VMEM((64 * ROWS, 128), F32),
            pltpu.VMEM((4 * ROWS, 128), F32),
            pltpu.VMEM((64, 256), F32),
            pltpu.VMEM((16, 256), F32),
            pltpu.SemaphoreType.DMA((11,)),
        ],
        compiler_params=params,
        name="forward",
    )(part, *arguments)
    listed = [[(2 * i + FIRST) % ZONES + core for i in range(ZONES // 2)] for core in range(2)]
    near = lax.all_to_all(send, "dom", 0, 0, axis_index_groups=listed)
    other = lax.ppermute(near, "dom", [(i, i ^ 1) for i in range(ZONES)])
    enc, one, two, pick, low, high, info, shaded, w_mid_t, w_out_t = kept
    rendered, grads = pl.pallas_call(
        backward_kernel,
        out_shape=(shape((3, 1, OWN), F32), shape((4, CHUNK, 256), F32)),
        in_specs=[scalar] + vmem(12),
        out_specs=vmem(2),
        scratch_shapes=[pltpu.VMEM((16 * ROWS, 128), F32)],
        compiler_params=params,
        name="backward",
    )(part, near, other, pick, low, high, info, shaded, enc, one, two, w_mid_t, w_out_t)
    shares = lax.all_to_all(grads, "ray", 0, 0, axis_index_groups=[[2, 1, 0, 3]])
    total = jnp.sum(shares, axis=0)
    everything = lax.all_to_all(jnp.broadcast_to(total[None], grads.shape), "ray", 0, 0, axis_index_groups=[[2, 1, 0, 3]])
    grad_i, grad_m, grad_o = pl.pallas_call(
        unpack_kernel,
        out_shape=(shape((FEATS, 1, 256), F32), shape((256, 256), F32), shape((4, 256), F32)),
        in_specs=vmem(1),
        out_specs=vmem(3),
        compiler_params=params,
        name="unpack",
    )(everything)
    return rendered, jnp.transpose(grad_i, (1, 2, 0)), grad_m[None], grad_o[None]


def solution(mesh):
    in_specs = (
        P(None, "ray", None),
        P(None, "ray", None),
        P("ray", None, None),
        P("ray", None, None),
        P("ray", None, None),
        P("ray", None, None),
        P("ray", None, None),
        P(None, "ray", None),
        P("dom", None, None),
        P("dom", None, None),
        P("dom", None, None),
    )
    out_specs = (
        P(None, "ray", "dom"),
        P("dom", None, None),
        P("dom", None, None),
        P("dom", None, None),
    )
    return jax.shard_map(local, mesh=mesh, in_specs=in_specs, out_specs=out_specs, check_vma=False)
```

```python
import functools

import jax
import jax.numpy as jnp
import numpy as np
from jax import lax
from jax.experimental import pallas as pl
from jax.experimental.pallas import tpu as pltpu
from jax.sharding import PartitionSpec as P

NFREQ = 10
FEATS = 63
S = 64
K = 4
NB = 8
CAP = 64
ZONES = 128
RG = 512
OWN = 4
ROWS = 32
SEL = 72
FIRST = 84
EARLY = 48
SPAN = (16, 4)
COLS = CAP * S
TILE = 16
CHUNK = 88
F32 = jnp.float32
BF16 = jnp.bfloat16


def listing():
    def far(index):
        hops = 0
        for place, first, length in zip(divmod(index // 2, SPAN[1]), divmod(FIRST // 2, SPAN[1]), SPAN):
            hops += min((place - first) % length, (first - place) % length)
        return index // 2 != FIRST // 2, -hops

    return [sorted(range(core, ZONES, 2), key=far) for core in range(2)]


def iota(shape, dim):
    return lax.broadcasted_iota(jnp.int32, shape, dim)


def one_hot(mask):
    return mask.astype(F32).astype(BF16)


def split(x, terms):
    parts = []
    for _ in range(terms):
        parts.append(x.astype(BF16))
        x = x - parts[-1].astype(F32)
    return parts


def dot(a, b):
    return jnp.dot(a, b, preferred_element_type=F32)


def dot_nt(a, b):
    return lax.dot_general(a, b, (((1,), (1,)), ((), ())), preferred_element_type=F32)


def split_dot(x, exact):
    return sum(dot(part, exact) for part in split(x, 2))


def halves(column):
    lane = iota((ROWS, 2 * S), 1)
    return jnp.where(lane < S, column[0:ROWS], column[ROWS : 2 * ROWS])


def sin_cos(x):
    turns = jnp.floor(x * 0.6366197723675814 + 0.5)
    r = ((x - turns * 1.5703125) - turns * 4.837512969970703e-4) - turns * 7.54978995489188e-8
    z = r * r
    s = ((-1.9515295891e-4 * z + 8.3321608736e-3) * z - 1.6666654611e-1) * z * r + r
    c = ((2.443315711809948e-5 * z - 1.388731625493765e-3) * z + 4.166664568298827e-2) * z * z - 0.5 * z + 1.0
    quadrant = turns.astype(jnp.int32)
    swap = (quadrant & 1) == 1
    sin_r = jnp.where(swap, c, s)
    cos_r = jnp.where(swap, s, c)
    sin_r = jnp.where((quadrant & 2) == 2, -sin_r, sin_r)
    cos_r = jnp.where(((quadrant + 1) & 2) == 2, -cos_r, cos_r)
    return sin_r, cos_r


def shade(raw, step_d, count_d):
    index = iota(step_d.shape, 1) & (S - 1)
    scale = jnp.where(index.astype(F32) < count_d, step_d, 0.0)
    decay = jnp.exp(-jnp.abs(raw[0]))
    density = jnp.maximum(raw[0], 0.0) + jnp.log1p(decay)
    optical = density * scale
    source, target = iota((2 * S, 2 * S), 0), iota((2 * S, 2 * S), 1)
    upto = one_hot((source <= target) & ((source < S) == (target < S)))
    reached = split_dot(optical, upto)
    entering = jnp.exp(optical - reached)
    weight = entering - jnp.exp(-reached)
    albedo = [1.0 / (1.0 + jnp.exp(-raw[c])) for c in (1, 2, 3)]
    return scale, optical, entering, weight, albedo


def select(part, crossing):
    earlier = one_hot(iota((RG, RG), 0) < iota((RG, RG), 1))
    own = crossing == part
    crossed = own[0:1] | own[1:2] | own[2:3] | own[3:4]
    place_own = dot(one_hot(jnp.broadcast_to(crossed, (16, RG))), earlier)[0:1]
    place_own = jnp.where(crossed, place_own.astype(jnp.int32), -1)
    row, ray = iota((SEL, RG), 0), iota((1, RG), 1)
    in_slot = (row < CAP) & (place_own == row)
    own_ray = (row >= CAP) & (row < CAP + OWN) & (ray == part * OWN + (row - CAP))
    return own, one_hot(in_slot | own_ray), earlier


def prepare(
    part, crossing_ref, target_ref, order_ref, lists_ref, w_mid_ref, w_out_ref,
    pick_ref, low_ref, high_ref, info_ref, w_mid_t_ref, w_out_t_ref, ints, goals, ranks, wout,
):
    crossing = crossing_ref[0]
    _, selector, earlier = select(part, crossing)
    ray = iota((1, RG), 1)
    ints[...] = jnp.zeros_like(ints)
    goals[...] = jnp.zeros_like(goals)
    for d in range(3):
        goals[d : d + 1] = target_ref[d]
    zone = iota((ZONES, RG), 0)
    names = [zone == crossing[k : k + 1] for k in range(K)]
    ranks[...] = dot(one_hot(names[0] | names[1] | names[2] | names[3]), earlier)
    place_all = ranks[...]
    ints[0:4] = crossing.astype(F32)
    for k in range(K):
        ints[4 + k : 5 + k] = jnp.sum(jnp.where(names[k], place_all, 0.0), axis=0, keepdims=True)
    ints[8:9] = (ray // (RG // NB)).astype(F32)
    ints[9:10] = jnp.ones((1, RG), F32)
    whole = ints[...].astype(BF16)
    table = dot_nt(selector, whole)
    info_ref[0:16] = dot_nt(whole, selector)
    info_ref[16:24] = sum(dot_nt(piece, selector) for piece in split(goals[...], 3))
    bundle = one_hot(table[:, 8:9].astype(jnp.int32) == iota((SEL, NB), 1))
    order = dot(bundle, order_ref[0].astype(F32).astype(BF16))
    lane = iota((SEL, ZONES), 1)
    lister = jnp.where((part & 1) == 0, lists_ref[0:1], lists_ref[1:2])
    positions = iota((8, ZONES), 1).astype(F32).astype(BF16)
    for k in range(K):
        named = table[:, k : k + 1]
        place = table[:, 4 + k : 5 + k].astype(jnp.int32)
        pick_ref[k * SEL : (k + 1) * SEL] = one_hot(named == lister)
        wanted = (lane & (ROWS - 1)) == (place & (ROWS - 1))
        low_ref[k * SEL : (k + 1) * SEL] = (wanted & (place < ROWS)).astype(F32)
        high_ref[k * SEL : (k + 1) * SEL] = (wanted & (place >= ROWS)).astype(F32)
        info_ref[24 + k : 25 + k] = dot_nt(positions, one_hot(order == named))[0:1]
    info_ref[28:32] = jnp.zeros((4, SEL), F32)
    wout[...] = jnp.zeros_like(wout)
    wout[0:4] = w_out_ref[...].astype(F32)
    w_out_t_ref[...] = wout[...].T.astype(BF16)
    w_mid_t_ref[...] = w_mid_ref[...].astype(F32).T.astype(BF16)


def forward_kernel(
    part_ref, anchor_hbm, direct_hbm, entry_hbm, step_hbm, counts_hbm, crossing_hbm, target_hbm, order_hbm,
    w_in_hbm, w_mid_hbm, w_out_hbm, lists_hbm,
    send_ref, enc_ref, one_ref, two_ref, shade_ref, crossing_ref, target_ref, order_ref, lists_ref, w_mid_ref, w_out_ref,
    pick_ref, low_ref, high_ref, info_ref, w_mid_t_ref, w_out_t_ref,
    anchor_ref, direct_ref, entry_ref, step_ref, counts_ref, w_in_ref, vals, feats, raws, win,
    ints, goals, ranks, wout, sems,
):
    copies = [
        pltpu.make_async_copy(source, target, sems.at[i])
        for i, (source, target) in enumerate((
            (crossing_hbm, crossing_ref), (entry_hbm, entry_ref), (step_hbm, step_ref), (counts_hbm, counts_ref),
            (anchor_hbm, anchor_ref), (direct_hbm, direct_ref), (w_in_hbm, w_in_ref), (w_mid_hbm, w_mid_ref),
            (w_out_hbm, w_out_ref), (target_hbm, target_ref), (order_hbm, order_ref),
            (lists_hbm, lists_ref),
        ))
    ]
    for copy in copies:
        copy.start()
    part = part_ref[0]
    vals[...] = jnp.zeros_like(vals)
    win[...] = jnp.zeros_like(win)
    wout[...] = jnp.zeros_like(wout)
    feats[FEATS * ROWS : (FEATS + 1) * ROWS] = jnp.zeros((ROWS, 2 * S), F32)
    copies[0].wait()

    crossing = crossing_ref[0]
    own, selector, _ = select(part, crossing)
    for copy in copies[1:]:
        copy.wait()

    def of_own(ref):
        return jnp.sum(jnp.where(own, ref[0].astype(F32), 0.0), axis=0, keepdims=True)

    for d in range(3):
        vals[d : d + 1] = anchor_ref[d]
        vals[3 + d : 4 + d] = direct_ref[d]
    vals[6:7] = of_own(entry_ref)
    vals[7:8] = of_own(step_ref)
    vals[8:9] = of_own(counts_ref)
    reals = sum(dot_nt(selector, piece) for piece in split(vals[...], 3))

    columns = [halves(reals[0:CAP, j : j + 1]) for j in range(9)]
    step_d, count_d = columns[7], columns[8]
    index = (iota((ROWS, 2 * S), 1) & (S - 1)).astype(F32)
    depth = columns[6] + (index + 0.5) * step_d
    for d in range(3):
        point = columns[d] + depth * columns[3 + d]
        feats[d * ROWS : (d + 1) * ROWS] = point
        sin_x, cos_x = sin_cos(point)
        for level in range(NFREQ):
            at = 3 + 6 * level + d
            feats[at * ROWS : (at + 1) * ROWS] = sin_x
            feats[(at + 3) * ROWS : (at + 4) * ROWS] = cos_x
            sin_x, cos_x = 2.0 * sin_x * cos_x, 1.0 - 2.0 * sin_x * sin_x

    win[0:FEATS] = w_in_ref[...].astype(F32)
    w_in = win[...].T.astype(BF16)
    w_mid = w_mid_ref[...]
    wout[0:4] = w_out_ref[...].astype(F32)
    w_out = wout[...].astype(BF16)
    half = one_hot(iota((8, 2 * S), 0) == iota((8, 2 * S), 1) // S)
    for tile in range(ROWS // TILE):
        span = slice(tile * TILE * 128, (tile + 1) * TILE * 128)
        encoded = jnp.concatenate(
            [feats[pl.ds(tile * TILE + j, FEATS + 1, stride=ROWS), :].astype(BF16) for j in range(TILE)], axis=1
        )
        enc_ref[:, span] = encoded
        one = jnp.maximum(dot(w_in, encoded), 0.0).astype(BF16)
        one_ref[:, span] = one
        two = jnp.maximum(dot(w_mid, one), 0.0).astype(BF16)
        two_ref[:, span] = two
        raw = dot(w_out, two)
        for j in range(TILE):
            raws[pl.ds(tile * TILE + j, 4, stride=ROWS), :] = raw[0:4, j * 128 : (j + 1) * 128]
    raw = [raws[c * ROWS : (c + 1) * ROWS] for c in range(4)]
    scale, optical, entering, weight, albedo = shade(raw, step_d, count_d)
    sums = jnp.concatenate([weight * albedo[0], weight * albedo[1], weight * albedo[2], -optical], axis=0)
    sent = sum(dot_nt(half, piece) for piece in split(sums, 2))
    send_ref[...] = jnp.broadcast_to(sent[None, 0:2], send_ref.shape)
    kept = [entering, weight, scale / (1.0 + jnp.exp(-raw[0]))] + albedo + [weight * a * (1.0 - a) for a in albedo]
    for i, value in enumerate(kept):
        shade_ref[i * ROWS : (i + 1) * ROWS] = value

    @pl.when(part < EARLY)
    def _():
        prepare(
            part, crossing_ref, target_ref, order_ref, lists_ref, w_mid_ref, w_out_ref,
            pick_ref, low_ref, high_ref, info_ref, w_mid_t_ref, w_out_t_ref, ints, goals, ranks, wout,
        )


def backward_kernel(
    part_ref, near_ref, other_ref, enc_ref, one_ref, two_ref, shade_ref,
    crossing_ref, target_ref, order_ref, lists_ref, w_mid_ref, w_out_ref, *refs,
):
    ready, (rendered_ref, grads_ref), work, (draw, *room) = refs[0:6], refs[6:8], refs[8:14], refs[14:]
    pick_ref, low_ref, high_ref, info_ref, w_mid_t_ref, w_out_t_ref = work

    @pl.when(part_ref[0] < EARLY)
    def _():
        for source, target in zip(ready, work):
            target[...] = source[...]

    @pl.when(part_ref[0] >= EARLY)
    def _():
        prepare(
            part_ref[0], crossing_ref, target_ref, order_ref, lists_ref, w_mid_ref, w_out_ref, *work, *room
        )

    part = part_ref[0].astype(F32)
    got = [jnp.concatenate([near_ref[:, h, :], other_ref[:, h, :]], axis=0) for h in range(2)]
    pieces = split(jnp.concatenate(got, axis=1), 2)
    gather = one_hot(iota((8, ZONES), 0) == iota((8, ZONES), 1) // ROWS)
    pick = pick_ref[...]
    low, high = low_ref[...] > 0.5, high_ref[...] > 0.5
    values = jnp.zeros((8, K * SEL), F32)
    for piece in pieces:
        both = dot(pick, piece)
        found = jnp.where(low, both[:, 0:128], jnp.where(high, both[:, 128:256], 0.0))
        values = values + dot_nt(gather, found.astype(BF16))

    mine = [values[:, k * SEL : (k + 1) * SEL] for k in range(K)]
    log = [mine[k][3:4] for k in range(K)]
    color = [mine[k][0:3] for k in range(K)]
    named = [info_ref[k : k + 1] for k in range(K)]
    used = info_ref[9:10] > 0.5
    goal = info_ref[16:19]
    rank = [info_ref[24 + k : 25 + k] for k in range(K)]
    fade = [
        jnp.exp(sum(jnp.where(rank[j] < rank[k], log[j], 0.0) for j in range(K) if j != k)) for k in range(K)
    ]
    clear = jnp.exp(log[0] + log[1] + log[2] + log[3])
    rendered = sum(fade[k] * color[k] for k in range(K)) + clear
    residual = rendered - goal
    share = [fade[k] * jnp.sum(residual * color[k], axis=0, keepdims=True) for k in range(K)]
    owned = [named[k] == part for k in range(K)]
    own_rank = sum(jnp.where(owned[k], rank[k], 0.0) for k in range(K))
    own_fade = sum(jnp.where(owned[k], fade[k], 0.0) for k in range(K))
    dlog = sum(jnp.where(rank[k] > own_rank, share[k], 0.0) for k in range(K))
    dlog = dlog + clear * jnp.sum(residual, axis=0, keepdims=True)
    dcolor = own_fade * residual
    for c in range(3):
        rendered_ref[c] = rendered[c : c + 1, CAP : CAP + OWN]
    slots = jnp.concatenate([dcolor, dlog, jnp.zeros((4, SEL), F32)], axis=0)
    slots = jnp.where(used, slots, 0.0)
    slots = jnp.concatenate([slots, jnp.zeros((8, 128 - SEL), F32)], axis=1).T

    entering, weight, slope, *rest = [shade_ref[i * ROWS : (i + 1) * ROWS] for i in range(9)]
    dcolor_d = [halves(slots[0:CAP, c : c + 1]) for c in range(3)]
    gain = sum(dcolor_d[c] * rest[c] for c in range(3))
    source, target = iota((2 * S, 2 * S), 0), iota((2 * S, 2 * S), 1)
    since = one_hot((source >= target) & ((source < S) == (target < S)))
    behind = split_dot(gain * weight, since)
    draw[0:ROWS] = (gain * entering - behind - halves(slots[0:CAP, 3:4])) * slope
    for c in range(3):
        draw[(c + 1) * ROWS : (c + 2) * ROWS] = dcolor_d[c] * rest[3 + c]
    draw[4 * ROWS :] = jnp.zeros((12 * ROWS, 2 * S), F32)

    w_out_t, w_mid_t = w_out_t_ref[...], w_mid_t_ref[...]
    grad_out = jnp.zeros((16, 256), F32)
    grad_mid = jnp.zeros((256, 256), F32)
    grad_in = jnp.zeros((256, 64), F32)
    zero = jnp.zeros((), BF16)
    for tile in range(ROWS // TILE):
        span = slice(tile * TILE * 128, (tile + 1) * TILE * 128)
        low = jnp.concatenate(
            [draw[pl.ds(tile * TILE + j, 16, stride=ROWS), :].astype(BF16) for j in range(TILE)], axis=1
        )
        two, one = two_ref[:, span], one_ref[:, span]
        grad_out = grad_out + dot_nt(low, two)
        d_two = jnp.where(two > 0, dot(w_out_t, low).astype(BF16), zero)
        grad_mid = grad_mid + dot_nt(d_two, one)
        d_one = jnp.where(one > 0, dot(w_mid_t, d_two).astype(BF16), zero)
        grad_in = grad_in + dot_nt(d_one, enc_ref[:, span])
    grad_in = grad_in.T
    for q in range(4):
        grads_ref[q, 0:64] = grad_mid[64 * q : 64 * q + 64]
        grads_ref[q, 64:80] = grad_in[16 * q : 16 * q + 16]
        grads_ref[q, 80:88] = jnp.broadcast_to(grad_out[q : q + 1], (8, 256))


def unpack_kernel(all_ref, in_ref, mid_ref, out_ref):
    for q in range(4):
        mid_ref[64 * q : 64 * q + 64] = all_ref[q, 0:64]
        rows = min(16, FEATS - 16 * q)
        in_ref[16 * q : 16 * q + rows, 0, :] = all_ref[q, 64 : 64 + rows]
        out_ref[q : q + 1] = all_ref[q, 80:81]


def vmem(count):
    return [pl.BlockSpec(memory_space=pltpu.VMEM)] * count


def in_hbm(array):
    return pltpu.with_memory_space_constraint(array, pltpu.HBM)


def local(anchor, direct, entry, step, counts, crossing, order, target, w_in, w_mid, w_out):
    part = lax.axis_index("dom").astype(jnp.int32).reshape(1)
    entry, step, counts, crossing = (jnp.swapaxes(a, 1, 2) for a in (entry, step, counts, crossing))
    w_in_t = jnp.swapaxes(w_in, 1, 2)[0]
    scalar = pl.BlockSpec(memory_space=pltpu.SMEM)
    params = pltpu.CompilerParams(vmem_limit_bytes=40 * 1024 * 1024)
    shape = jax.ShapeDtypeStruct
    listed = listing()
    lists = jnp.asarray(np.array([listed[0] + listed[1], listed[1] + listed[0]], np.float32))
    arguments = [in_hbm(a) for a in (
        anchor, direct, entry, step, counts, crossing, target, order, w_in_t, w_mid[0], w_out[0], lists
    )]
    prepared = (
        shape((K * SEL, ZONES), BF16),
        shape((K * SEL, ZONES), F32),
        shape((K * SEL, ZONES), F32),
        shape((32, SEL), F32),
        shape((256, 256), BF16),
        shape((256, 16), BF16),
    )
    room = [
        pltpu.VMEM((16, RG), F32),
        pltpu.VMEM((8, RG), F32),
        pltpu.VMEM((ZONES, RG), F32),
        pltpu.VMEM((16, 256), F32),
    ]
    send, *kept = pl.pallas_call(
        forward_kernel,
        out_shape=(
            shape((ZONES // 2, 2, 128), F32),
            shape((64, COLS), BF16),
            shape((256, COLS), BF16),
            shape((256, COLS), BF16),
            shape((9 * ROWS, 128), F32),
            *(shape(a.shape, a.dtype) for a in (crossing, target, order, lists, w_mid[0], w_out[0])),
            *prepared,
        ),
        in_specs=[scalar] + [pl.BlockSpec(memory_space=pltpu.HBM)] * len(arguments),
        out_specs=vmem(17),
        scratch_shapes=[pltpu.VMEM(a.shape, a.dtype) for a in (anchor, direct, entry, step, counts, w_in_t)]
        + [
            pltpu.VMEM((16, RG), F32),
            pltpu.VMEM((64 * ROWS, 128), F32),
            pltpu.VMEM((4 * ROWS, 128), F32),
            pltpu.VMEM((64, 256), F32),
            *room,
            pltpu.SemaphoreType.DMA((len(arguments),)),
        ],
        compiler_params=params,
        name="forward",
    )(part, *arguments)
    near = lax.all_to_all(send, "dom", 0, 0, axis_index_groups=listed)
    other = lax.ppermute(near, "dom", [(i, i ^ 1) for i in range(ZONES)])
    rendered, grads = pl.pallas_call(
        backward_kernel,
        out_shape=(shape((3, 1, OWN), F32), shape((4, CHUNK, 256), F32)),
        in_specs=[scalar] + vmem(2 + len(kept)),
        out_specs=vmem(2),
        scratch_shapes=[pltpu.VMEM(a.shape, a.dtype) for a in prepared] + [pltpu.VMEM((16 * ROWS, 128), F32), *room],
        compiler_params=params,
        name="backward",
    )(part, near, other, *kept)
    shares = lax.all_to_all(grads, "ray", 0, 0, axis_index_groups=[[2, 1, 0, 3]])
    total = jnp.sum(shares, axis=0)
    everything = lax.all_to_all(jnp.broadcast_to(total[None], grads.shape), "ray", 0, 0, axis_index_groups=[[2, 1, 0, 3]])
    grad_i, grad_m, grad_o = pl.pallas_call(
        unpack_kernel,
        out_shape=(shape((FEATS, 1, 256), F32), shape((256, 256), F32), shape((4, 256), F32)),
        in_specs=vmem(1),
        out_specs=vmem(3),
        compiler_params=params,
        name="unpack",
    )(everything)
    return rendered, jnp.transpose(grad_i, (1, 2, 0)), grad_m[None], grad_o[None]


def solution(mesh):
    in_specs = (
        P(None, "ray", None),
        P(None, "ray", None),
        P("ray", None, None),
        P("ray", None, None),
        P("ray", None, None),
        P("ray", None, None),
        P("ray", None, None),
        P(None, "ray", None),
        P("dom", None, None),
        P("dom", None, None),
        P("dom", None, None),
    )
    out_specs = (
        P(None, "ray", "dom"),
        P("dom", None, None),
        P("dom", None, None),
        P("dom", None, None),
    )
    return jax.shard_map(local, mesh=mesh, in_specs=in_specs, out_specs=out_specs, check_vma=False)
```

```python
import functools

import jax
import jax.numpy as jnp
import numpy as np
from jax import lax
from jax.experimental import pallas as pl
from jax.experimental.pallas import tpu as pltpu
from jax.sharding import PartitionSpec as P

NFREQ = 10
FEATS = 63
S = 64
K = 4
NB = 8
CAP = 64
ZONES = 128
RG = 512
OWN = 4
ROWS = 32
SEL = 72
FIRST = 84
EARLY = 48
SPAN = (16, 4)
COLS = CAP * S
TILE = 16
CHUNK = 168
F32 = jnp.float32
BF16 = jnp.bfloat16


def listing():
    def far(index):
        hops = 0
        for place, first, length in zip(divmod(index // 2, SPAN[1]), divmod(FIRST // 2, SPAN[1]), SPAN):
            hops += min((place - first) % length, (first - place) % length)
        return index // 2 != FIRST // 2, -hops

    return [sorted(range(core, ZONES, 2), key=far) for core in range(2)]


def iota(shape, dim):
    return lax.broadcasted_iota(jnp.int32, shape, dim)


def one_hot(mask):
    return mask.astype(F32).astype(BF16)


def split(x, terms):
    parts = []
    for _ in range(terms):
        parts.append(x.astype(BF16))
        x = x - parts[-1].astype(F32)
    return parts


def dot(a, b):
    return jnp.dot(a, b, preferred_element_type=F32)


def dot_nt(a, b):
    return lax.dot_general(a, b, (((1,), (1,)), ((), ())), preferred_element_type=F32)


def split_dot(x, exact):
    return sum(dot(part, exact) for part in split(x, 2))


def halves(column):
    lane = iota((ROWS, 2 * S), 1)
    return jnp.where(lane < S, column[0:ROWS], column[ROWS : 2 * ROWS])


def sin_cos(x):
    turns = jnp.floor(x * 0.6366197723675814 + 0.5)
    r = ((x - turns * 1.5703125) - turns * 4.837512969970703e-4) - turns * 7.54978995489188e-8
    z = r * r
    s = ((-1.9515295891e-4 * z + 8.3321608736e-3) * z - 1.6666654611e-1) * z * r + r
    c = ((2.443315711809948e-5 * z - 1.388731625493765e-3) * z + 4.166664568298827e-2) * z * z - 0.5 * z + 1.0
    quadrant = turns.astype(jnp.int32)
    swap = (quadrant & 1) == 1
    sin_r = jnp.where(swap, c, s)
    cos_r = jnp.where(swap, s, c)
    sin_r = jnp.where((quadrant & 2) == 2, -sin_r, sin_r)
    cos_r = jnp.where(((quadrant + 1) & 2) == 2, -cos_r, cos_r)
    return sin_r, cos_r


def shade(raw, step_d, count_d):
    index = iota(step_d.shape, 1) & (S - 1)
    scale = jnp.where(index.astype(F32) < count_d, step_d, 0.0)
    decay = jnp.exp(-jnp.abs(raw[0]))
    density = jnp.maximum(raw[0], 0.0) + jnp.log1p(decay)
    optical = density * scale
    source, target = iota((2 * S, 2 * S), 0), iota((2 * S, 2 * S), 1)
    upto = one_hot((source <= target) & ((source < S) == (target < S)))
    reached = split_dot(optical, upto)
    entering = jnp.exp(optical - reached)
    weight = entering - jnp.exp(-reached)
    albedo = [1.0 / (1.0 + jnp.exp(-raw[c])) for c in (1, 2, 3)]
    return scale, optical, entering, weight, albedo


def select(part, crossing):
    earlier = one_hot(iota((RG, RG), 0) < iota((RG, RG), 1))
    own = crossing == part
    crossed = own[0:1] | own[1:2] | own[2:3] | own[3:4]
    place_own = dot(one_hot(jnp.broadcast_to(crossed, (16, RG))), earlier)[0:1]
    place_own = jnp.where(crossed, place_own.astype(jnp.int32), -1)
    row, ray = iota((SEL, RG), 0), iota((1, RG), 1)
    in_slot = (row < CAP) & (place_own == row)
    own_ray = (row >= CAP) & (row < CAP + OWN) & (ray == part * OWN + (row - CAP))
    return own, one_hot(in_slot | own_ray), earlier


def prepare(
    part, crossing_ref, target_ref, order_ref, lists_ref, w_mid_ref, w_out_ref,
    pick_ref, low_ref, high_ref, info_ref, w_mid_t_ref, w_out_t_ref, ints, goals, ranks, wout,
):
    crossing = crossing_ref[0]
    _, selector, earlier = select(part, crossing)
    ray = iota((1, RG), 1)
    ints[...] = jnp.zeros_like(ints)
    goals[...] = jnp.zeros_like(goals)
    for d in range(3):
        goals[d : d + 1] = target_ref[d]
    zone = iota((ZONES, RG), 0)
    names = [zone == crossing[k : k + 1] for k in range(K)]
    ranks[...] = dot(one_hot(names[0] | names[1] | names[2] | names[3]), earlier)
    place_all = ranks[...]
    ints[0:4] = crossing.astype(F32)
    for k in range(K):
        ints[4 + k : 5 + k] = jnp.sum(jnp.where(names[k], place_all, 0.0), axis=0, keepdims=True)
    ints[8:9] = (ray // (RG // NB)).astype(F32)
    ints[9:10] = jnp.ones((1, RG), F32)
    whole = ints[...].astype(BF16)
    table = dot_nt(selector, whole)
    info_ref[0:16] = dot_nt(whole, selector)
    info_ref[16:24] = sum(dot_nt(piece, selector) for piece in split(goals[...], 3))
    bundle = one_hot(table[:, 8:9].astype(jnp.int32) == iota((SEL, NB), 1))
    order = dot(bundle, order_ref[0].astype(F32).astype(BF16))
    lane = iota((SEL, ZONES), 1)
    lister = jnp.where((part & 1) == 0, lists_ref[0:1], lists_ref[1:2])
    positions = iota((8, ZONES), 1).astype(F32).astype(BF16)
    for k in range(K):
        named = table[:, k : k + 1]
        place = table[:, 4 + k : 5 + k].astype(jnp.int32)
        pick_ref[k * SEL : (k + 1) * SEL] = one_hot(named == lister)
        wanted = (lane & (ROWS - 1)) == (place & (ROWS - 1))
        low_ref[k * SEL : (k + 1) * SEL] = (wanted & (place < ROWS)).astype(F32)
        high_ref[k * SEL : (k + 1) * SEL] = (wanted & (place >= ROWS)).astype(F32)
        info_ref[24 + k : 25 + k] = dot_nt(positions, one_hot(order == named))[0:1]
    info_ref[28:32] = jnp.zeros((4, SEL), F32)
    wout[...] = jnp.zeros_like(wout)
    wout[0:4] = w_out_ref[...].astype(F32)
    w_out_t_ref[...] = wout[...].T.astype(BF16)
    w_mid_t_ref[...] = w_mid_ref[...].astype(F32).T.astype(BF16)


def forward_kernel(
    part_ref, anchor_hbm, direct_hbm, entry_hbm, step_hbm, counts_hbm, crossing_hbm, target_hbm, order_hbm,
    w_in_hbm, w_mid_hbm, w_out_hbm, lists_hbm,
    send_ref, enc_ref, one_ref, two_ref, shade_ref, crossing_ref, target_ref, order_ref, lists_ref, w_mid_ref, w_out_ref,
    pick_ref, low_ref, high_ref, info_ref, w_mid_t_ref, w_out_t_ref,
    anchor_ref, direct_ref, entry_ref, step_ref, counts_ref, w_in_ref, vals, feats, raws, win,
    ints, goals, ranks, wout, sems,
):
    copies = [
        pltpu.make_async_copy(source, target, sems.at[i])
        for i, (source, target) in enumerate((
            (crossing_hbm, crossing_ref), (entry_hbm, entry_ref), (step_hbm, step_ref), (counts_hbm, counts_ref),
            (anchor_hbm, anchor_ref), (direct_hbm, direct_ref), (w_in_hbm, w_in_ref), (w_mid_hbm, w_mid_ref),
            (w_out_hbm, w_out_ref), (target_hbm, target_ref), (order_hbm, order_ref),
            (lists_hbm, lists_ref),
        ))
    ]
    for copy in copies:
        copy.start()
    part = part_ref[0]
    vals[...] = jnp.zeros_like(vals)
    win[...] = jnp.zeros_like(win)
    wout[...] = jnp.zeros_like(wout)
    feats[FEATS * ROWS : (FEATS + 1) * ROWS] = jnp.zeros((ROWS, 2 * S), F32)
    copies[0].wait()

    crossing = crossing_ref[0]
    own, selector, _ = select(part, crossing)
    for copy in copies[1:]:
        copy.wait()

    def of_own(ref):
        return jnp.sum(jnp.where(own, ref[0].astype(F32), 0.0), axis=0, keepdims=True)

    for d in range(3):
        vals[d : d + 1] = anchor_ref[d]
        vals[3 + d : 4 + d] = direct_ref[d]
    vals[6:7] = of_own(entry_ref)
    vals[7:8] = of_own(step_ref)
    vals[8:9] = of_own(counts_ref)
    reals = sum(dot_nt(selector, piece) for piece in split(vals[...], 3))

    columns = [halves(reals[0:CAP, j : j + 1]) for j in range(9)]
    step_d, count_d = columns[7], columns[8]
    index = (iota((ROWS, 2 * S), 1) & (S - 1)).astype(F32)
    depth = columns[6] + (index + 0.5) * step_d
    for d in range(3):
        point = columns[d] + depth * columns[3 + d]
        feats[d * ROWS : (d + 1) * ROWS] = point
        sin_x, cos_x = sin_cos(point)
        for level in range(NFREQ):
            at = 3 + 6 * level + d
            feats[at * ROWS : (at + 1) * ROWS] = sin_x
            feats[(at + 3) * ROWS : (at + 4) * ROWS] = cos_x
            sin_x, cos_x = 2.0 * sin_x * cos_x, 1.0 - 2.0 * sin_x * sin_x

    win[0:FEATS] = w_in_ref[...].astype(F32)
    w_in = win[...].T.astype(BF16)
    w_mid = w_mid_ref[...]
    wout[0:4] = w_out_ref[...].astype(F32)
    w_out = wout[...].astype(BF16)
    half = one_hot(iota((8, 2 * S), 0) == iota((8, 2 * S), 1) // S)
    for tile in range(ROWS // TILE):
        span = slice(tile * TILE * 128, (tile + 1) * TILE * 128)
        encoded = jnp.concatenate(
            [feats[pl.ds(tile * TILE + j, FEATS + 1, stride=ROWS), :].astype(BF16) for j in range(TILE)], axis=1
        )
        enc_ref[:, span] = encoded
        one = jnp.maximum(dot(w_in, encoded), 0.0).astype(BF16)
        one_ref[:, span] = one
        two = jnp.maximum(dot(w_mid, one), 0.0).astype(BF16)
        two_ref[:, span] = two
        raw = dot(w_out, two)
        for j in range(TILE):
            raws[pl.ds(tile * TILE + j, 4, stride=ROWS), :] = raw[0:4, j * 128 : (j + 1) * 128]
    raw = [raws[c * ROWS : (c + 1) * ROWS] for c in range(4)]
    scale, optical, entering, weight, albedo = shade(raw, step_d, count_d)
    sums = jnp.concatenate([weight * albedo[0], weight * albedo[1], weight * albedo[2], -optical], axis=0)
    sent = sum(dot_nt(half, piece) for piece in split(sums, 2))
    send_ref[...] = jnp.broadcast_to(sent[None, 0:2], send_ref.shape)
    kept = [entering, weight, scale / (1.0 + jnp.exp(-raw[0]))] + albedo + [weight * a * (1.0 - a) for a in albedo]
    for i, value in enumerate(kept):
        shade_ref[i * ROWS : (i + 1) * ROWS] = value

    @pl.when(part < EARLY)
    def _():
        prepare(
            part, crossing_ref, target_ref, order_ref, lists_ref, w_mid_ref, w_out_ref,
            pick_ref, low_ref, high_ref, info_ref, w_mid_t_ref, w_out_t_ref, ints, goals, ranks, wout,
        )


def backward_kernel(
    part_ref, near_ref, other_ref, enc_ref, one_ref, two_ref, shade_ref,
    crossing_ref, target_ref, order_ref, lists_ref, w_mid_ref, w_out_ref, *refs,
):
    ready, (rendered_ref, grads_ref), work, (draw, *room) = refs[0:6], refs[6:8], refs[8:14], refs[14:]
    pick_ref, low_ref, high_ref, info_ref, w_mid_t_ref, w_out_t_ref = work

    @pl.when(part_ref[0] < EARLY)
    def _():
        for source, target in zip(ready, work):
            target[...] = source[...]

    @pl.when(part_ref[0] >= EARLY)
    def _():
        prepare(
            part_ref[0], crossing_ref, target_ref, order_ref, lists_ref, w_mid_ref, w_out_ref, *work, *room
        )

    part = part_ref[0].astype(F32)
    got = [jnp.concatenate([near_ref[:, h, :], other_ref[:, h, :]], axis=0) for h in range(2)]
    pieces = split(jnp.concatenate(got, axis=1), 2)
    gather = one_hot(iota((8, ZONES), 0) == iota((8, ZONES), 1) // ROWS)
    pick = pick_ref[...]
    low, high = low_ref[...] > 0.5, high_ref[...] > 0.5
    values = jnp.zeros((8, K * SEL), F32)
    for piece in pieces:
        both = dot(pick, piece)
        found = jnp.where(low, both[:, 0:128], jnp.where(high, both[:, 128:256], 0.0))
        values = values + dot_nt(gather, found.astype(BF16))

    mine = [values[:, k * SEL : (k + 1) * SEL] for k in range(K)]
    log = [mine[k][3:4] for k in range(K)]
    color = [mine[k][0:3] for k in range(K)]
    named = [info_ref[k : k + 1] for k in range(K)]
    used = info_ref[9:10] > 0.5
    goal = info_ref[16:19]
    rank = [info_ref[24 + k : 25 + k] for k in range(K)]
    fade = [
        jnp.exp(sum(jnp.where(rank[j] < rank[k], log[j], 0.0) for j in range(K) if j != k)) for k in range(K)
    ]
    clear = jnp.exp(log[0] + log[1] + log[2] + log[3])
    rendered = sum(fade[k] * color[k] for k in range(K)) + clear
    residual = rendered - goal
    share = [fade[k] * jnp.sum(residual * color[k], axis=0, keepdims=True) for k in range(K)]
    owned = [named[k] == part for k in range(K)]
    own_rank = sum(jnp.where(owned[k], rank[k], 0.0) for k in range(K))
    own_fade = sum(jnp.where(owned[k], fade[k], 0.0) for k in range(K))
    dlog = sum(jnp.where(rank[k] > own_rank, share[k], 0.0) for k in range(K))
    dlog = dlog + clear * jnp.sum(residual, axis=0, keepdims=True)
    dcolor = own_fade * residual
    for c in range(3):
        rendered_ref[c] = rendered[c : c + 1, CAP : CAP + OWN]
    slots = jnp.concatenate([dcolor, dlog, jnp.zeros((4, SEL), F32)], axis=0)
    slots = jnp.where(used, slots, 0.0)
    slots = jnp.concatenate([slots, jnp.zeros((8, 128 - SEL), F32)], axis=1).T

    entering, weight, slope, *rest = [shade_ref[i * ROWS : (i + 1) * ROWS] for i in range(9)]
    dcolor_d = [halves(slots[0:CAP, c : c + 1]) for c in range(3)]
    gain = sum(dcolor_d[c] * rest[c] for c in range(3))
    source, target = iota((2 * S, 2 * S), 0), iota((2 * S, 2 * S), 1)
    since = one_hot((source >= target) & ((source < S) == (target < S)))
    behind = split_dot(gain * weight, since)
    draw[0:ROWS] = (gain * entering - behind - halves(slots[0:CAP, 3:4])) * slope
    for c in range(3):
        draw[(c + 1) * ROWS : (c + 2) * ROWS] = dcolor_d[c] * rest[3 + c]
    draw[4 * ROWS :] = jnp.zeros((12 * ROWS, 2 * S), F32)

    w_out_t, w_mid_t = w_out_t_ref[...], w_mid_t_ref[...]
    grad_out = jnp.zeros((16, 256), F32)
    grad_mid = jnp.zeros((256, 256), F32)
    grad_in = jnp.zeros((256, 64), F32)
    zero = jnp.zeros((), BF16)
    for tile in range(ROWS // TILE):
        span = slice(tile * TILE * 128, (tile + 1) * TILE * 128)
        low = jnp.concatenate(
            [draw[pl.ds(tile * TILE + j, 16, stride=ROWS), :].astype(BF16) for j in range(TILE)], axis=1
        )
        two, one = two_ref[:, span], one_ref[:, span]
        grad_out = grad_out + dot_nt(low, two)
        d_two = jnp.where(two > 0, dot(w_out_t, low).astype(BF16), zero)
        grad_mid = grad_mid + dot_nt(d_two, one)
        d_one = jnp.where(one > 0, dot(w_mid_t, d_two).astype(BF16), zero)
        grad_in = grad_in + dot_nt(d_one, enc_ref[:, span])
    grad_in = grad_in.T
    for q in range(4):
        for h in range(2):
            half = slice(128 * h, 128 * h + 128)
            grads_ref[q, 64 * h : 64 * h + 64] = grad_mid[64 * q : 64 * q + 64, half]
            grads_ref[q, 128 + 16 * h : 144 + 16 * h] = grad_in[16 * q : 16 * q + 16, half]
            grads_ref[q, 160 + 4 * h : 164 + 4 * h] = jnp.broadcast_to(grad_out[q : q + 1, half], (4, 128))


def unpack_kernel(all_ref, in_ref, mid_ref, out_ref):
    for q in range(4):
        rows = min(16, FEATS - 16 * q)
        for h in range(2):
            half = slice(128 * h, 128 * h + 128)
            mid_ref[64 * q : 64 * q + 64, half] = all_ref[q, 64 * h : 64 * h + 64]
            in_ref[16 * q : 16 * q + rows, 0, half] = all_ref[q, 128 + 16 * h : 128 + 16 * h + rows]
            out_ref[q : q + 1, half] = all_ref[q, 160 + 4 * h : 161 + 4 * h]


def vmem(count):
    return [pl.BlockSpec(memory_space=pltpu.VMEM)] * count


def in_hbm(array):
    return pltpu.with_memory_space_constraint(array, pltpu.HBM)


def local(anchor, direct, entry, step, counts, crossing, order, target, w_in, w_mid, w_out):
    part = lax.axis_index("dom").astype(jnp.int32).reshape(1)
    entry, step, counts, crossing = (jnp.swapaxes(a, 1, 2) for a in (entry, step, counts, crossing))
    w_in_t = jnp.swapaxes(w_in, 1, 2)[0]
    scalar = pl.BlockSpec(memory_space=pltpu.SMEM)
    params = pltpu.CompilerParams(vmem_limit_bytes=40 * 1024 * 1024)
    shape = jax.ShapeDtypeStruct
    listed = listing()
    lists = jnp.asarray(np.array([listed[0] + listed[1], listed[1] + listed[0]], np.float32))
    arguments = [in_hbm(a) for a in (
        anchor, direct, entry, step, counts, crossing, target, order, w_in_t, w_mid[0], w_out[0], lists
    )]
    prepared = (
        shape((K * SEL, ZONES), BF16),
        shape((K * SEL, ZONES), F32),
        shape((K * SEL, ZONES), F32),
        shape((32, SEL), F32),
        shape((256, 256), BF16),
        shape((256, 16), BF16),
    )
    room = [
        pltpu.VMEM((16, RG), F32),
        pltpu.VMEM((8, RG), F32),
        pltpu.VMEM((ZONES, RG), F32),
        pltpu.VMEM((16, 256), F32),
    ]
    send, *kept = pl.pallas_call(
        forward_kernel,
        out_shape=(
            shape((ZONES // 2, 2, 128), F32),
            shape((64, COLS), BF16),
            shape((256, COLS), BF16),
            shape((256, COLS), BF16),
            shape((9 * ROWS, 128), F32),
            *(shape(a.shape, a.dtype) for a in (crossing, target, order, lists, w_mid[0], w_out[0])),
            *prepared,
        ),
        in_specs=[scalar] + [pl.BlockSpec(memory_space=pltpu.HBM)] * len(arguments),
        out_specs=vmem(17),
        scratch_shapes=[pltpu.VMEM(a.shape, a.dtype) for a in (anchor, direct, entry, step, counts, w_in_t)]
        + [
            pltpu.VMEM((16, RG), F32),
            pltpu.VMEM((64 * ROWS, 128), F32),
            pltpu.VMEM((4 * ROWS, 128), F32),
            pltpu.VMEM((64, 256), F32),
            *room,
            pltpu.SemaphoreType.DMA((len(arguments),)),
        ],
        compiler_params=params,
        name="forward",
    )(part, *arguments)
    near = lax.all_to_all(send, "dom", 0, 0, axis_index_groups=listed)
    other = lax.ppermute(near, "dom", [(i, i ^ 1) for i in range(ZONES)])
    rendered, grads = pl.pallas_call(
        backward_kernel,
        out_shape=(shape((3, 1, OWN), F32), shape((4, CHUNK, 128), F32)),
        in_specs=[scalar] + vmem(2 + len(kept)),
        out_specs=vmem(2),
        scratch_shapes=[pltpu.VMEM(a.shape, a.dtype) for a in prepared] + [pltpu.VMEM((16 * ROWS, 128), F32), *room],
        compiler_params=params,
        name="backward",
    )(part, near, other, *kept)
    shares = lax.all_to_all(grads, "ray", 0, 0, axis_index_groups=[[2, 1, 0, 3]])
    total = jnp.sum(shares, axis=0)
    everything = lax.all_to_all(jnp.broadcast_to(total[None], grads.shape), "ray", 0, 0, axis_index_groups=[[2, 1, 0, 3]])
    grad_i, grad_m, grad_o = pl.pallas_call(
        unpack_kernel,
        out_shape=(shape((FEATS, 1, 256), F32), shape((256, 256), F32), shape((4, 256), F32)),
        in_specs=vmem(1),
        out_specs=vmem(3),
        compiler_params=params,
        name="unpack",
    )(everything)
    return rendered, jnp.transpose(grad_i, (1, 2, 0)), grad_m[None], grad_o[None]


def solution(mesh):
    in_specs = (
        P(None, "ray", None),
        P(None, "ray", None),
        P("ray", None, None),
        P("ray", None, None),
        P("ray", None, None),
        P("ray", None, None),
        P("ray", None, None),
        P(None, "ray", None),
        P("dom", None, None),
        P("dom", None, None),
        P("dom", None, None),
    )
    out_specs = (
        P(None, "ray", "dom"),
        P("dom", None, None),
        P("dom", None, None),
        P("dom", None, None),
    )
    return jax.shard_map(local, mesh=mesh, in_specs=in_specs, out_specs=out_specs, check_vma=False)
```

```python
import functools

import jax
import jax.numpy as jnp
import numpy as np
from jax import lax
from jax.experimental import pallas as pl
from jax.experimental.pallas import tpu as pltpu
from jax.sharding import PartitionSpec as P

NFREQ = 10
FEATS = 63
S = 64
K = 4
NB = 8
CAP = 64
ZONES = 128
RG = 512
OWN = 4
ROWS = 32
SEL = 72
FIRST = 84
EARLY = 48
SPAN = (16, 4)
COLS = CAP * S
TILE = 16
CHUNK = 168
F32 = jnp.float32
BF16 = jnp.bfloat16


def listing():
    def far(index):
        hops = 0
        for place, first, length in zip(divmod(index // 2, SPAN[1]), divmod(FIRST // 2, SPAN[1]), SPAN):
            hops += min((place - first) % length, (first - place) % length)
        return index // 2 != FIRST // 2, -hops

    return [sorted(range(core, ZONES, 2), key=far) for core in range(2)]


def iota(shape, dim):
    return lax.broadcasted_iota(jnp.int32, shape, dim)


def one_hot(mask):
    return mask.astype(F32).astype(BF16)


def split(x, terms):
    parts = []
    for _ in range(terms):
        parts.append(x.astype(BF16))
        x = x - parts[-1].astype(F32)
    return parts


def dot(a, b):
    return jnp.dot(a, b, preferred_element_type=F32)


def dot_nt(a, b):
    return lax.dot_general(a, b, (((1,), (1,)), ((), ())), preferred_element_type=F32)


def split_dot(x, exact, terms):
    return sum(dot(part, exact) for part in split(x, terms))


def halves(column):
    lane = iota((ROWS, 2 * S), 1)
    return jnp.where(lane < S, column[0:ROWS], column[ROWS : 2 * ROWS])


def sin_cos(x):
    turns = jnp.floor(x * 0.6366197723675814 + 0.5)
    r = ((x - turns * 1.5703125) - turns * 4.837512969970703e-4) - turns * 7.54978995489188e-8
    z = r * r
    s = ((-1.9515295891e-4 * z + 8.3321608736e-3) * z - 1.6666654611e-1) * z * r + r
    c = ((2.443315711809948e-5 * z - 1.388731625493765e-3) * z + 4.166664568298827e-2) * z * z - 0.5 * z + 1.0
    quadrant = turns.astype(jnp.int32)
    swap = (quadrant & 1) == 1
    sin_r = jnp.where(swap, c, s)
    cos_r = jnp.where(swap, s, c)
    sin_r = jnp.where((quadrant & 2) == 2, -sin_r, sin_r)
    cos_r = jnp.where(((quadrant + 1) & 2) == 2, -cos_r, cos_r)
    return sin_r, cos_r


def shade(raw, step_d, count_d):
    index = iota(step_d.shape, 1) & (S - 1)
    scale = jnp.where(index.astype(F32) < count_d, step_d, 0.0)
    decay = jnp.exp(-jnp.abs(raw[0]))
    density = jnp.maximum(raw[0], 0.0) + jnp.log1p(decay)
    optical = density * scale
    source, target = iota((2 * S, 2 * S), 0), iota((2 * S, 2 * S), 1)
    ahead = one_hot((source < target) & ((source < S) == (target < S)))
    passed = split_dot(optical, ahead, 2)
    entering = jnp.exp(-passed)
    weight = entering - jnp.exp(-(passed + optical))
    albedo = [1.0 / (1.0 + jnp.exp(-raw[c])) for c in (1, 2, 3)]
    return scale, optical, entering, weight, albedo


def select(part, crossing):
    earlier = one_hot(iota((RG, RG), 0) < iota((RG, RG), 1))
    own = crossing == part
    crossed = own[0:1] | own[1:2] | own[2:3] | own[3:4]
    place_own = dot(one_hot(jnp.broadcast_to(crossed, (16, RG))), earlier)[0:1]
    place_own = jnp.where(crossed, place_own.astype(jnp.int32), -1)
    row, ray = iota((SEL, RG), 0), iota((1, RG), 1)
    in_slot = (row < CAP) & (place_own == row)
    own_ray = (row >= CAP) & (row < CAP + OWN) & (ray == part * OWN + (row - CAP))
    return own, one_hot(in_slot | own_ray), earlier


def prepare(
    part, crossing_ref, target_ref, order_ref, lists_ref, w_mid_ref, w_out_ref,
    pick_ref, low_ref, high_ref, info_ref, w_mid_t_ref, w_out_t_ref, ints, goals, ranks, wout,
):
    crossing = crossing_ref[0]
    _, selector, earlier = select(part, crossing)
    ray = iota((1, RG), 1)
    ints[...] = jnp.zeros_like(ints)
    goals[...] = jnp.zeros_like(goals)
    for d in range(3):
        goals[d : d + 1] = target_ref[d]
    zone = iota((ZONES, RG), 0)
    names = [zone == crossing[k : k + 1] for k in range(K)]
    ranks[...] = dot(one_hot(names[0] | names[1] | names[2] | names[3]), earlier)
    place_all = ranks[...]
    ints[0:4] = crossing.astype(F32)
    for k in range(K):
        ints[4 + k : 5 + k] = jnp.sum(jnp.where(names[k], place_all, 0.0), axis=0, keepdims=True)
    ints[8:9] = (ray // (RG // NB)).astype(F32)
    ints[9:10] = jnp.ones((1, RG), F32)
    whole = ints[...].astype(BF16)
    table = dot_nt(selector, whole)
    info_ref[0:16] = dot_nt(whole, selector)
    info_ref[16:24] = sum(dot_nt(piece, selector) for piece in split(goals[...], 3))
    bundle = one_hot(table[:, 8:9].astype(jnp.int32) == iota((SEL, NB), 1))
    order = dot(bundle, order_ref[0].astype(F32).astype(BF16))
    lane = iota((SEL, ZONES), 1)
    lister = jnp.where((part & 1) == 0, lists_ref[0:1], lists_ref[1:2])
    positions = iota((8, ZONES), 1).astype(F32).astype(BF16)
    for k in range(K):
        named = table[:, k : k + 1]
        place = table[:, 4 + k : 5 + k].astype(jnp.int32)
        pick_ref[k * SEL : (k + 1) * SEL] = one_hot(named == lister)
        wanted = (lane & (ROWS - 1)) == (place & (ROWS - 1))
        low_ref[k * SEL : (k + 1) * SEL] = (wanted & (place < ROWS)).astype(F32)
        high_ref[k * SEL : (k + 1) * SEL] = (wanted & (place >= ROWS)).astype(F32)
        info_ref[24 + k : 25 + k] = dot_nt(positions, one_hot(order == named))[0:1]
    info_ref[28:32] = jnp.zeros((4, SEL), F32)
    wout[...] = jnp.zeros_like(wout)
    wout[0:4] = w_out_ref[...].astype(F32)
    w_out_t_ref[...] = wout[...].T.astype(BF16)
    w_mid_t_ref[...] = w_mid_ref[...].astype(F32).T.astype(BF16)


def forward_kernel(
    part_ref, anchor_hbm, direct_hbm, entry_hbm, step_hbm, counts_hbm, crossing_hbm, target_hbm, order_hbm,
    w_in_hbm, w_mid_hbm, w_out_hbm, lists_hbm,
    send_ref, enc_ref, one_ref, two_ref, shade_ref, crossing_ref, target_ref, order_ref, lists_ref, w_mid_ref, w_out_ref,
    pick_ref, low_ref, high_ref, info_ref, w_mid_t_ref, w_out_t_ref,
    anchor_ref, direct_ref, entry_ref, step_ref, counts_ref, w_in_ref, vals, feats, raws, win,
    ints, goals, ranks, wout, sems,
):
    copies = [
        pltpu.make_async_copy(source, target, sems.at[i])
        for i, (source, target) in enumerate((
            (crossing_hbm, crossing_ref), (entry_hbm, entry_ref), (step_hbm, step_ref), (counts_hbm, counts_ref),
            (anchor_hbm, anchor_ref), (direct_hbm, direct_ref), (w_in_hbm, w_in_ref), (w_mid_hbm, w_mid_ref),
            (w_out_hbm, w_out_ref), (target_hbm, target_ref), (order_hbm, order_ref),
            (lists_hbm, lists_ref),
        ))
    ]
    for copy in copies:
        copy.start()
    part = part_ref[0]
    vals[...] = jnp.zeros_like(vals)
    win[...] = jnp.zeros_like(win)
    wout[...] = jnp.zeros_like(wout)
    feats[FEATS * ROWS : (FEATS + 1) * ROWS] = jnp.zeros((ROWS, 2 * S), F32)
    copies[0].wait()

    crossing = crossing_ref[0]
    own, selector, _ = select(part, crossing)
    for copy in copies[1:]:
        copy.wait()

    def of_own(ref):
        return jnp.sum(jnp.where(own, ref[0].astype(F32), 0.0), axis=0, keepdims=True)

    for d in range(3):
        vals[d : d + 1] = anchor_ref[d]
        vals[3 + d : 4 + d] = direct_ref[d]
    vals[6:7] = of_own(entry_ref)
    vals[7:8] = of_own(step_ref)
    vals[8:9] = of_own(counts_ref)
    reals = sum(dot_nt(selector, piece) for piece in split(vals[...], 3))

    columns = [halves(reals[0:CAP, j : j + 1]) for j in range(9)]
    step_d, count_d = columns[7], columns[8]
    index = (iota((ROWS, 2 * S), 1) & (S - 1)).astype(F32)
    depth = columns[6] + (index + 0.5) * step_d
    for d in range(3):
        point = columns[d] + depth * columns[3 + d]
        feats[d * ROWS : (d + 1) * ROWS] = point
        sin_x, cos_x = sin_cos(point)
        for level in range(NFREQ):
            at = 3 + 6 * level + d
            feats[at * ROWS : (at + 1) * ROWS] = sin_x
            feats[(at + 3) * ROWS : (at + 4) * ROWS] = cos_x
            sin_x, cos_x = 2.0 * sin_x * cos_x, 1.0 - 2.0 * sin_x * sin_x

    win[0:FEATS] = w_in_ref[...].astype(F32)
    w_in = win[...].T.astype(BF16)
    w_mid = w_mid_ref[...]
    wout[0:4] = w_out_ref[...].astype(F32)
    w_out = wout[...].astype(BF16)
    half = one_hot(iota((8, 2 * S), 0) == iota((8, 2 * S), 1) // S)
    for tile in range(ROWS // TILE):
        span = slice(tile * TILE * 128, (tile + 1) * TILE * 128)
        encoded = jnp.concatenate(
            [feats[pl.ds(tile * TILE + j, FEATS + 1, stride=ROWS), :].astype(BF16) for j in range(TILE)], axis=1
        )
        enc_ref[:, span] = encoded
        one = jnp.maximum(dot(w_in, encoded), 0.0).astype(BF16)
        one_ref[:, span] = one
        two = jnp.maximum(dot(w_mid, one), 0.0).astype(BF16)
        two_ref[:, span] = two
        raw = dot(w_out, two)
        for j in range(TILE):
            raws[pl.ds(tile * TILE + j, 4, stride=ROWS), :] = raw[0:4, j * 128 : (j + 1) * 128]
    raw = [raws[c * ROWS : (c + 1) * ROWS] for c in range(4)]
    scale, optical, entering, weight, albedo = shade(raw, step_d, count_d)
    sums = jnp.concatenate([weight * albedo[0], weight * albedo[1], weight * albedo[2], -optical], axis=0)
    sent = sum(dot_nt(half, piece) for piece in split(sums, 2))
    send_ref[...] = jnp.broadcast_to(sent[None, 0:2], send_ref.shape)
    kept = [entering, weight, scale / (1.0 + jnp.exp(-raw[0]))] + albedo + [weight * a * (1.0 - a) for a in albedo]
    for i, value in enumerate(kept):
        shade_ref[i * ROWS : (i + 1) * ROWS] = value

    @pl.when(part < EARLY)
    def _():
        prepare(
            part, crossing_ref, target_ref, order_ref, lists_ref, w_mid_ref, w_out_ref,
            pick_ref, low_ref, high_ref, info_ref, w_mid_t_ref, w_out_t_ref, ints, goals, ranks, wout,
        )


def backward_kernel(
    part_ref, near_ref, other_ref, enc_ref, one_ref, two_ref, shade_ref,
    crossing_ref, target_ref, order_ref, lists_ref, w_mid_ref, w_out_ref, *refs,
):
    ready, (rendered_ref, grads_ref), work, (draw, *room) = refs[0:6], refs[6:8], refs[8:14], refs[14:]
    pick_ref, low_ref, high_ref, info_ref, w_mid_t_ref, w_out_t_ref = work

    @pl.when(part_ref[0] < EARLY)
    def _():
        for source, target in zip(ready, work):
            target[...] = source[...]

    @pl.when(part_ref[0] >= EARLY)
    def _():
        prepare(
            part_ref[0], crossing_ref, target_ref, order_ref, lists_ref, w_mid_ref, w_out_ref, *work, *room
        )

    part = part_ref[0].astype(F32)
    got = [jnp.concatenate([near_ref[:, h, :], other_ref[:, h, :]], axis=0) for h in range(2)]
    pieces = split(jnp.concatenate(got, axis=1), 2)
    gather = one_hot(iota((8, ZONES), 0) == iota((8, ZONES), 1) // ROWS)
    pick = pick_ref[...]
    low, high = low_ref[...] > 0.5, high_ref[...] > 0.5
    values = jnp.zeros((8, K * SEL), F32)
    for piece in pieces:
        both = dot(pick, piece)
        found = jnp.where(low, both[:, 0:128], jnp.where(high, both[:, 128:256], 0.0))
        values = values + dot_nt(gather, found.astype(BF16))

    mine = [values[:, k * SEL : (k + 1) * SEL] for k in range(K)]
    log = [mine[k][3:4] for k in range(K)]
    color = [mine[k][0:3] for k in range(K)]
    named = [info_ref[k : k + 1] for k in range(K)]
    used = info_ref[9:10] > 0.5
    goal = info_ref[16:19]
    rank = [info_ref[24 + k : 25 + k] for k in range(K)]
    fade = [
        jnp.exp(sum(jnp.where(rank[j] < rank[k], log[j], 0.0) for j in range(K) if j != k)) for k in range(K)
    ]
    clear = jnp.exp(log[0] + log[1] + log[2] + log[3])
    rendered = sum(fade[k] * color[k] for k in range(K)) + clear
    residual = rendered - goal
    share = [fade[k] * jnp.sum(residual * color[k], axis=0, keepdims=True) for k in range(K)]
    owned = [named[k] == part for k in range(K)]
    own_rank = sum(jnp.where(owned[k], rank[k], 0.0) for k in range(K))
    own_fade = sum(jnp.where(owned[k], fade[k], 0.0) for k in range(K))
    dlog = sum(jnp.where(rank[k] > own_rank, share[k], 0.0) for k in range(K))
    dlog = dlog + clear * jnp.sum(residual, axis=0, keepdims=True)
    dcolor = own_fade * residual
    for c in range(3):
        rendered_ref[c] = rendered[c : c + 1, CAP : CAP + OWN]
    slots = jnp.concatenate([dcolor, dlog, jnp.zeros((4, SEL), F32)], axis=0)
    slots = jnp.where(used, slots, 0.0)
    slots = jnp.concatenate([slots, jnp.zeros((8, 128 - SEL), F32)], axis=1).T

    entering, weight, slope, *rest = [shade_ref[i * ROWS : (i + 1) * ROWS] for i in range(9)]
    dcolor_d = [halves(slots[0:CAP, c : c + 1]) for c in range(3)]
    gain = sum(dcolor_d[c] * rest[c] for c in range(3))
    source, target = iota((2 * S, 2 * S), 0), iota((2 * S, 2 * S), 1)
    since = one_hot((source >= target) & ((source < S) == (target < S)))
    behind = split_dot(gain * weight, since, 3)
    draw[0:ROWS] = (gain * entering - behind - halves(slots[0:CAP, 3:4])) * slope
    for c in range(3):
        draw[(c + 1) * ROWS : (c + 2) * ROWS] = dcolor_d[c] * rest[3 + c]
    draw[4 * ROWS : 16 * ROWS] = jnp.zeros((12 * ROWS, 2 * S), F32)

    w_out_t, w_mid_t = w_out_t_ref[...], w_mid_t_ref[...]
    grad_out = jnp.zeros((16, 256), F32)
    grad_mid = jnp.zeros((256, 256), F32)
    grad_in = jnp.zeros((256, 64), F32)
    zero = jnp.zeros((), BF16)
    for tile in range(ROWS // TILE):
        span = slice(tile * TILE * 128, (tile + 1) * TILE * 128)
        low = jnp.concatenate(
            [draw[pl.ds(tile * TILE + j, 16, stride=ROWS), :].astype(BF16) for j in range(TILE)], axis=1
        )
        two, one = two_ref[:, span], one_ref[:, span]
        grad_out = grad_out + dot_nt(low, two)
        d_two = jnp.where(two > 0, dot(w_out_t, low).astype(BF16), zero)
        grad_mid = grad_mid + dot_nt(d_two, one)
        d_one = jnp.where(one > 0, dot(w_mid_t, d_two).astype(BF16), zero)
        grad_in = grad_in + dot_nt(d_one, enc_ref[:, span])
    grad_in = grad_in.T
    for q in range(4):
        for h in range(2):
            half = slice(128 * h, 128 * h + 128)
            grads_ref[q, 64 * h : 64 * h + 64] = grad_mid[64 * q : 64 * q + 64, half]
            grads_ref[q, 128 + 16 * h : 144 + 16 * h] = grad_in[16 * q : 16 * q + 16, half]
            grads_ref[q, 160 + 4 * h : 164 + 4 * h] = jnp.broadcast_to(grad_out[q : q + 1, half], (4, 128))


def unpack_kernel(all_ref, in_ref, mid_ref, out_ref):
    for q in range(4):
        rows = min(16, FEATS - 16 * q)
        for h in range(2):
            half = slice(128 * h, 128 * h + 128)
            mid_ref[64 * q : 64 * q + 64, half] = all_ref[q, 64 * h : 64 * h + 64]
            in_ref[16 * q : 16 * q + rows, 0, half] = all_ref[q, 128 + 16 * h : 128 + 16 * h + rows]
            out_ref[q : q + 1, half] = all_ref[q, 160 + 4 * h : 161 + 4 * h]


def vmem(count):
    return [pl.BlockSpec(memory_space=pltpu.VMEM)] * count


def in_hbm(array):
    return pltpu.with_memory_space_constraint(array, pltpu.HBM)


def local(anchor, direct, entry, step, counts, crossing, order, target, w_in, w_mid, w_out):
    part = lax.axis_index("dom").astype(jnp.int32).reshape(1)
    entry, step, counts, crossing = (jnp.swapaxes(a, 1, 2) for a in (entry, step, counts, crossing))
    w_in_t = jnp.swapaxes(w_in, 1, 2)[0]
    scalar = pl.BlockSpec(memory_space=pltpu.SMEM)
    params = pltpu.CompilerParams(vmem_limit_bytes=40 * 1024 * 1024)
    shape = jax.ShapeDtypeStruct
    listed = listing()
    lists = jnp.asarray(np.array([listed[0] + listed[1], listed[1] + listed[0]], np.float32))
    arguments = [in_hbm(a) for a in (
        anchor, direct, entry, step, counts, crossing, target, order, w_in_t, w_mid[0], w_out[0], lists
    )]
    prepared = (
        shape((K * SEL, ZONES), BF16),
        shape((K * SEL, ZONES), F32),
        shape((K * SEL, ZONES), F32),
        shape((32, SEL), F32),
        shape((256, 256), BF16),
        shape((256, 16), BF16),
    )
    room = [
        pltpu.VMEM((16, RG), F32),
        pltpu.VMEM((8, RG), F32),
        pltpu.VMEM((ZONES, RG), F32),
        pltpu.VMEM((16, 256), F32),
    ]
    send, *kept = pl.pallas_call(
        forward_kernel,
        out_shape=(
            shape((ZONES // 2, 2, 128), F32),
            shape((64, COLS), BF16),
            shape((256, COLS), BF16),
            shape((256, COLS), BF16),
            shape((9 * ROWS, 128), F32),
            *(shape(a.shape, a.dtype) for a in (crossing, target, order, lists, w_mid[0], w_out[0])),
            *prepared,
        ),
        in_specs=[scalar] + [pl.BlockSpec(memory_space=pltpu.HBM)] * len(arguments),
        out_specs=vmem(17),
        scratch_shapes=[pltpu.VMEM(a.shape, a.dtype) for a in (anchor, direct, entry, step, counts, w_in_t)]
        + [
            pltpu.VMEM((16, RG), F32),
            pltpu.VMEM((65 * ROWS, 128), F32),
            pltpu.VMEM((5 * ROWS, 128), F32),
            pltpu.VMEM((64, 256), F32),
            *room,
            pltpu.SemaphoreType.DMA((len(arguments),)),
        ],
        compiler_params=params,
        name="forward",
    )(part, *arguments)
    near = lax.all_to_all(send, "dom", 0, 0, axis_index_groups=listed)
    other = lax.ppermute(near, "dom", [(i, i ^ 1) for i in range(ZONES)])
    rendered, grads = pl.pallas_call(
        backward_kernel,
        out_shape=(shape((3, 1, OWN), F32), shape((4, CHUNK, 128), F32)),
        in_specs=[scalar] + vmem(2 + len(kept)),
        out_specs=vmem(2),
        scratch_shapes=[pltpu.VMEM(a.shape, a.dtype) for a in prepared] + [pltpu.VMEM((17 * ROWS, 128), F32), *room],
        compiler_params=params,
        name="backward",
    )(part, near, other, *kept)
    shares = lax.all_to_all(grads, "ray", 0, 0, axis_index_groups=[[2, 1, 0, 3]])
    total = jnp.sum(shares, axis=0)
    everything = lax.all_to_all(jnp.broadcast_to(total[None], grads.shape), "ray", 0, 0, axis_index_groups=[[2, 1, 0, 3]])
    grad_i, grad_m, grad_o = pl.pallas_call(
        unpack_kernel,
        out_shape=(shape((FEATS, 1, 256), F32), shape((256, 256), F32), shape((4, 256), F32)),
        in_specs=vmem(1),
        out_specs=vmem(3),
        compiler_params=params,
        name="unpack",
    )(everything)
    return rendered, jnp.transpose(grad_i, (1, 2, 0)), grad_m[None], grad_o[None]


def solution(mesh):
    in_specs = (
        P(None, "ray", None),
        P(None, "ray", None),
        P("ray", None, None),
        P("ray", None, None),
        P("ray", None, None),
        P("ray", None, None),
        P("ray", None, None),
        P(None, "ray", None),
        P("dom", None, None),
        P("dom", None, None),
        P("dom", None, None),
    )
    out_specs = (
        P(None, "ray", "dom"),
        P("dom", None, None),
        P("dom", None, None),
        P("dom", None, None),
    )
    return jax.shard_map(local, mesh=mesh, in_specs=in_specs, out_specs=out_specs, check_vma=False)
```

```python
import functools

import jax
import jax.numpy as jnp
import numpy as np
from jax import lax
from jax.experimental import pallas as pl
from jax.experimental.pallas import tpu as pltpu
from jax.sharding import PartitionSpec as P

NFREQ = 10
FEATS = 63
S = 64
K = 4
NB = 8
CAP = 64
ZONES = 128
RG = 512
OWN = 4
ROWS = 32
SEL = 72
FIRST = 84
EARLY = 48
SPAN = (16, 4)
COLS = CAP * S
TILE = 16
CHUNK = 168
F32 = jnp.float32
BF16 = jnp.bfloat16


def listing():
    def far(index):
        hops = 0
        for place, first, length in zip(divmod(index // 2, SPAN[1]), divmod(FIRST // 2, SPAN[1]), SPAN):
            hops += min((place - first) % length, (first - place) % length)
        return index // 2 != FIRST // 2, -hops

    return [sorted(range(core, ZONES, 2), key=far) for core in range(2)]


def iota(shape, dim):
    return lax.broadcasted_iota(jnp.int32, shape, dim)


def one_hot(mask):
    return mask.astype(F32).astype(BF16)


def split(x, terms):
    parts = []
    for _ in range(terms):
        parts.append(x.astype(BF16))
        x = x - parts[-1].astype(F32)
    return parts


def dot(a, b):
    return jnp.dot(a, b, preferred_element_type=F32)


def dot_nt(a, b):
    return lax.dot_general(a, b, (((1,), (1,)), ((), ())), preferred_element_type=F32)


def split_dot(x, exact, terms):
    return sum(dot(part, exact) for part in split(x, terms))


def halves(column):
    lane = iota((ROWS, 2 * S), 1)
    return jnp.where(lane < S, column[0:ROWS], column[ROWS : 2 * ROWS])


def sin_cos(x):
    turns = jnp.floor(x * 0.6366197723675814 + 0.5)
    r = ((x - turns * 1.5703125) - turns * 4.837512969970703e-4) - turns * 7.54978995489188e-8
    z = r * r
    s = ((-1.9515295891e-4 * z + 8.3321608736e-3) * z - 1.6666654611e-1) * z * r + r
    c = ((2.443315711809948e-5 * z - 1.388731625493765e-3) * z + 4.166664568298827e-2) * z * z - 0.5 * z + 1.0
    quadrant = turns.astype(jnp.int32)
    swap = (quadrant & 1) == 1
    sin_r = jnp.where(swap, c, s)
    cos_r = jnp.where(swap, s, c)
    sin_r = jnp.where((quadrant & 2) == 2, -sin_r, sin_r)
    cos_r = jnp.where(((quadrant + 1) & 2) == 2, -cos_r, cos_r)
    return sin_r, cos_r


def shade(raw, step_d, count_d):
    index = iota(step_d.shape, 1) & (S - 1)
    scale = jnp.where(index.astype(F32) < count_d, step_d, 0.0)
    decay = jnp.exp(-jnp.abs(raw[0]))
    density = jnp.maximum(raw[0], 0.0) + jnp.log1p(decay)
    optical = density * scale
    source, target = iota((2 * S, 2 * S), 0), iota((2 * S, 2 * S), 1)
    ahead = one_hot((source < target) & ((source < S) == (target < S)))
    passed = split_dot(optical, ahead, 2)
    entering = jnp.exp(-passed)
    weight = entering - jnp.exp(-(passed + optical))
    albedo = [1.0 / (1.0 + jnp.exp(-raw[c])) for c in (1, 2, 3)]
    return scale, optical, entering, weight, albedo


def select(part, crossing):
    earlier = one_hot(iota((RG, RG), 0) < iota((RG, RG), 1))
    own = crossing == part
    crossed = own[0:1] | own[1:2] | own[2:3] | own[3:4]
    place_own = dot(one_hot(jnp.broadcast_to(crossed, (16, RG))), earlier)[0:1]
    place_own = jnp.where(crossed, place_own.astype(jnp.int32), -1)
    row, ray = iota((SEL, RG), 0), iota((1, RG), 1)
    in_slot = (row < CAP) & (place_own == row)
    own_ray = (row >= CAP) & (row < CAP + OWN) & (ray == part * OWN + (row - CAP))
    return own, one_hot(in_slot | own_ray), earlier


def prepare(
    part, crossing_ref, target_ref, order_ref, lists_ref, w_mid_ref, w_out_ref,
    pick_ref, low_ref, high_ref, info_ref, w_mid_t_ref, w_out_t_ref, ints, goals, ranks, wout,
):
    crossing = crossing_ref[0]
    _, selector, earlier = select(part, crossing)
    ray = iota((1, RG), 1)
    ints[...] = jnp.zeros_like(ints)
    goals[...] = jnp.zeros_like(goals)
    for d in range(3):
        goals[d : d + 1] = target_ref[d]
    zone = iota((ZONES, RG), 0)
    names = [zone == crossing[k : k + 1] for k in range(K)]
    ranks[...] = dot(one_hot(names[0] | names[1] | names[2] | names[3]), earlier)
    place_all = ranks[...]
    ints[0:4] = crossing.astype(F32)
    for k in range(K):
        ints[4 + k : 5 + k] = jnp.sum(jnp.where(names[k], place_all, 0.0), axis=0, keepdims=True)
    ints[8:9] = (ray // (RG // NB)).astype(F32)
    ints[9:10] = jnp.ones((1, RG), F32)
    whole = ints[...].astype(BF16)
    table = dot_nt(selector, whole)
    info_ref[0:16] = dot_nt(whole, selector)
    info_ref[16:24] = sum(dot_nt(piece, selector) for piece in split(goals[...], 3))
    bundle = one_hot(table[:, 8:9].astype(jnp.int32) == iota((SEL, NB), 1))
    order = dot(bundle, order_ref[0].astype(F32).astype(BF16))
    lane = iota((SEL, ZONES), 1)
    lister = jnp.where((part & 1) == 0, lists_ref[0:1], lists_ref[1:2])
    positions = iota((8, ZONES), 1).astype(F32).astype(BF16)
    for k in range(K):
        named = table[:, k : k + 1]
        place = table[:, 4 + k : 5 + k].astype(jnp.int32)
        pick_ref[k * SEL : (k + 1) * SEL] = one_hot(named == lister)
        wanted = (lane & (ROWS - 1)) == (place & (ROWS - 1))
        low_ref[k * SEL : (k + 1) * SEL] = (wanted & (place < ROWS)).astype(F32)
        high_ref[k * SEL : (k + 1) * SEL] = (wanted & (place >= ROWS)).astype(F32)
        info_ref[24 + k : 25 + k] = dot_nt(positions, one_hot(order == named))[0:1]
    info_ref[28:32] = jnp.zeros((4, SEL), F32)
    wout[...] = jnp.zeros_like(wout)
    wout[0:4] = w_out_ref[...].astype(F32)
    w_out_t_ref[...] = wout[...].T.astype(BF16)
    w_mid_t_ref[...] = w_mid_ref[...].astype(F32).T.astype(BF16)


def forward_kernel(
    part_ref, anchor_hbm, direct_hbm, entry_hbm, step_hbm, counts_hbm, crossing_hbm, target_hbm, order_hbm,
    w_in_hbm, w_mid_hbm, w_out_hbm, lists_hbm,
    send_ref, enc_ref, one_ref, two_ref, shade_ref, crossing_ref, target_ref, order_ref, lists_ref, w_mid_ref, w_out_ref,
    pick_ref, low_ref, high_ref, info_ref, w_mid_t_ref, w_out_t_ref,
    anchor_ref, direct_ref, entry_ref, step_ref, counts_ref, w_in_ref, vals, feats, raws, win,
    ints, goals, ranks, wout, sems,
):
    copies = [
        pltpu.make_async_copy(source, target, sems.at[i])
        for i, (source, target) in enumerate((
            (crossing_hbm, crossing_ref), (entry_hbm, entry_ref), (step_hbm, step_ref), (counts_hbm, counts_ref),
            (anchor_hbm, anchor_ref), (direct_hbm, direct_ref), (w_in_hbm, w_in_ref), (w_mid_hbm, w_mid_ref),
            (w_out_hbm, w_out_ref), (target_hbm, target_ref), (order_hbm, order_ref),
            (lists_hbm, lists_ref),
        ))
    ]
    for copy in copies:
        copy.start()
    part = part_ref[0]
    vals[...] = jnp.zeros_like(vals)
    win[...] = jnp.zeros_like(win)
    wout[...] = jnp.zeros_like(wout)
    feats[FEATS * ROWS : (FEATS + 1) * ROWS] = jnp.zeros((ROWS, 2 * S), F32)
    copies[0].wait()

    crossing = crossing_ref[0]
    own, selector, _ = select(part, crossing)
    for copy in copies[1:]:
        copy.wait()

    def of_own(ref):
        return jnp.sum(jnp.where(own, ref[0].astype(F32), 0.0), axis=0, keepdims=True)

    for d in range(3):
        vals[d : d + 1] = anchor_ref[d]
        vals[3 + d : 4 + d] = direct_ref[d]
    vals[6:7] = of_own(entry_ref)
    vals[7:8] = of_own(step_ref)
    vals[8:9] = of_own(counts_ref)
    reals = sum(dot_nt(selector, piece) for piece in split(vals[...], 3))

    columns = [halves(reals[0:CAP, j : j + 1]) for j in range(9)]
    step_d, count_d = columns[7], columns[8]
    index = (iota((ROWS, 2 * S), 1) & (S - 1)).astype(F32)
    depth = columns[6] + (index + 0.5) * step_d
    for d in range(3):
        point = columns[d] + depth * columns[3 + d]
        feats[d * ROWS : (d + 1) * ROWS] = point
        sin_x, cos_x = sin_cos(point)
        for level in range(NFREQ):
            at = 3 + 6 * level + d
            feats[at * ROWS : (at + 1) * ROWS] = sin_x
            feats[(at + 3) * ROWS : (at + 4) * ROWS] = cos_x
            sin_x, cos_x = 2.0 * sin_x * cos_x, 1.0 - 2.0 * sin_x * sin_x

    win[0:FEATS] = w_in_ref[...].astype(F32)
    w_in = win[...].T.astype(BF16)
    w_mid = w_mid_ref[...]
    wout[0:4] = w_out_ref[...].astype(F32)
    w_out = wout[...].astype(BF16)
    half = one_hot(iota((8, 2 * S), 0) == iota((8, 2 * S), 1) // S)
    for tile in range(ROWS // TILE):
        span = slice(tile * TILE * 128, (tile + 1) * TILE * 128)
        encoded = jnp.concatenate(
            [feats[pl.ds(tile * TILE + j, FEATS + 1, stride=ROWS), :].astype(BF16) for j in range(TILE)], axis=1
        )
        enc_ref[:, span] = encoded
        one = jnp.maximum(dot(w_in, encoded), 0.0).astype(BF16)
        one_ref[:, span] = one
        two = jnp.maximum(dot(w_mid, one), 0.0).astype(BF16)
        two_ref[:, span] = two
        raw = dot(w_out, two)
        for j in range(TILE):
            raws[pl.ds(tile * TILE + j, 4, stride=ROWS), :] = raw[0:4, j * 128 : (j + 1) * 128]
    raw = [raws[c * ROWS : (c + 1) * ROWS] for c in range(4)]
    scale, optical, entering, weight, albedo = shade(raw, step_d, count_d)
    sums = jnp.concatenate([weight * albedo[0], weight * albedo[1], weight * albedo[2], -optical], axis=0)
    sent = sum(dot_nt(half, piece) for piece in split(sums, 2))
    send_ref[...] = jnp.broadcast_to(sent[None, 0:2], send_ref.shape)
    kept = [entering, weight, scale / (1.0 + jnp.exp(-raw[0]))] + albedo + [weight * a * (1.0 - a) for a in albedo]
    for i, value in enumerate(kept):
        shade_ref[i * ROWS : (i + 1) * ROWS] = value

    @pl.when(part < EARLY)
    def _():
        prepare(
            part, crossing_ref, target_ref, order_ref, lists_ref, w_mid_ref, w_out_ref,
            pick_ref, low_ref, high_ref, info_ref, w_mid_t_ref, w_out_t_ref, ints, goals, ranks, wout,
        )


def backward_kernel(
    part_ref, near_ref, other_ref, enc_ref, one_ref, two_ref, shade_ref,
    crossing_ref, target_ref, order_ref, lists_ref, w_mid_ref, w_out_ref, *refs,
):
    ready, (rendered_ref, grads_ref), work, (draw, *room) = refs[0:6], refs[6:8], refs[8:14], refs[14:]
    pick_ref, low_ref, high_ref, info_ref, w_mid_t_ref, w_out_t_ref = work

    @pl.when(part_ref[0] < EARLY)
    def _():
        for source, target in zip(ready, work):
            target[...] = source[...]

    @pl.when(part_ref[0] >= EARLY)
    def _():
        prepare(
            part_ref[0], crossing_ref, target_ref, order_ref, lists_ref, w_mid_ref, w_out_ref, *work, *room
        )

    part = part_ref[0].astype(F32)
    got = [jnp.concatenate([near_ref[:, h, :], other_ref[:, h, :]], axis=0) for h in range(2)]
    pieces = split(jnp.concatenate(got, axis=1), 2)
    gather = one_hot(iota((8, ZONES), 0) == iota((8, ZONES), 1) // ROWS)
    pick = pick_ref[...]
    low, high = low_ref[...] > 0.5, high_ref[...] > 0.5
    values = jnp.zeros((8, K * SEL), F32)
    for piece in pieces:
        both = dot(pick, piece)
        found = jnp.where(low, both[:, 0:128], jnp.where(high, both[:, 128:256], 0.0))
        values = values + dot_nt(gather, found.astype(BF16))

    mine = [values[:, k * SEL : (k + 1) * SEL] for k in range(K)]
    log = [mine[k][3:4] for k in range(K)]
    color = [mine[k][0:3] for k in range(K)]
    named = [info_ref[k : k + 1] for k in range(K)]
    used = info_ref[9:10] > 0.5
    goal = info_ref[16:19]
    rank = [info_ref[24 + k : 25 + k] for k in range(K)]
    fade = [
        jnp.exp(sum(jnp.where(rank[j] < rank[k], log[j], 0.0) for j in range(K) if j != k)) for k in range(K)
    ]
    clear = jnp.exp(log[0] + log[1] + log[2] + log[3])
    rendered = sum(fade[k] * color[k] for k in range(K)) + clear
    residual = rendered - goal
    share = [fade[k] * jnp.sum(residual * color[k], axis=0, keepdims=True) for k in range(K)]
    owned = [named[k] == part for k in range(K)]
    own_rank = sum(jnp.where(owned[k], rank[k], 0.0) for k in range(K))
    own_fade = sum(jnp.where(owned[k], fade[k], 0.0) for k in range(K))
    dlog = sum(jnp.where(rank[k] > own_rank, share[k], 0.0) for k in range(K))
    dlog = dlog + clear * jnp.sum(residual, axis=0, keepdims=True)
    dcolor = own_fade * residual
    for c in range(3):
        rendered_ref[c] = rendered[c : c + 1, CAP : CAP + OWN]
    slots = jnp.concatenate([dcolor, dlog, jnp.zeros((4, SEL), F32)], axis=0)
    slots = jnp.where(used, slots, 0.0)
    slots = jnp.concatenate([slots, jnp.zeros((8, 128 - SEL), F32)], axis=1).T

    entering, weight, slope, *rest = [shade_ref[i * ROWS : (i + 1) * ROWS] for i in range(9)]
    dcolor_d = [halves(slots[0:CAP, c : c + 1]) for c in range(3)]
    gain = sum(dcolor_d[c] * rest[c] for c in range(3))
    source, target = iota((2 * S, 2 * S), 0), iota((2 * S, 2 * S), 1)
    since = one_hot((source >= target) & ((source < S) == (target < S)))
    behind = split_dot(gain * weight, since, 3)
    draw[0:ROWS] = (gain * entering - behind - halves(slots[0:CAP, 3:4])) * slope
    for c in range(3):
        draw[(c + 1) * ROWS : (c + 2) * ROWS] = dcolor_d[c] * rest[3 + c]
    draw[4 * ROWS : 16 * ROWS] = jnp.zeros((12 * ROWS, 2 * S), F32)

    w_out_t, w_mid_t = w_out_t_ref[...], w_mid_t_ref[...]
    grad_out = jnp.zeros((16, 256), F32)
    grad_mid = jnp.zeros((256, 256), F32)
    grad_in = jnp.zeros((256, 64), F32)
    zero = jnp.zeros((), BF16)
    for tile in range(ROWS // TILE):
        span = slice(tile * TILE * 128, (tile + 1) * TILE * 128)
        low = jnp.concatenate(
            [draw[pl.ds(tile * TILE + j, 16, stride=ROWS), :].astype(BF16) for j in range(TILE)], axis=1
        )
        two, one = two_ref[:, span], one_ref[:, span]
        grad_out = grad_out + dot_nt(low, two)
        d_two = jnp.where(two > 0, dot(w_out_t, low).astype(BF16), zero)
        grad_mid = grad_mid + dot_nt(d_two, one)
        d_one = jnp.where(one > 0, dot(w_mid_t, d_two).astype(BF16), zero)
        grad_in = grad_in + dot_nt(d_one, enc_ref[:, span])
    grad_in = grad_in.T
    for q in range(4):
        for h in range(2):
            half = slice(128 * h, 128 * h + 128)
            grads_ref[q, 64 * h : 64 * h + 64] = grad_mid[64 * q : 64 * q + 64, half]
            grads_ref[q, 128 + 16 * h : 144 + 16 * h] = grad_in[16 * q : 16 * q + 16, half]
            grads_ref[q, 160 + 4 * h : 164 + 4 * h] = jnp.broadcast_to(grad_out[q : q + 1, half], (4, 128))


def unpack_kernel(all_ref, in_ref, mid_hbm, out_ref, sems):
    copies = [
        pltpu.make_async_copy(
            all_ref.at[q, pl.ds(64 * h, 64)],
            mid_hbm.at[pl.ds(64 * q, 64), pl.ds(128 * h, 128)],
            sems.at[2 * q + h],
        )
        for q in range(4)
        for h in range(2)
    ]
    for copy in copies:
        copy.start()
    for q in range(4):
        rows = min(16, FEATS - 16 * q)
        for h in range(2):
            half = slice(128 * h, 128 * h + 128)
            in_ref[16 * q : 16 * q + rows, 0, half] = all_ref[q, 128 + 16 * h : 128 + 16 * h + rows]
            out_ref[q : q + 1, half] = all_ref[q, 160 + 4 * h : 161 + 4 * h]
    for copy in copies:
        copy.wait()


def vmem(count):
    return [pl.BlockSpec(memory_space=pltpu.VMEM)] * count


def in_hbm(array):
    return pltpu.with_memory_space_constraint(array, pltpu.HBM)


def local(anchor, direct, entry, step, counts, crossing, order, target, w_in, w_mid, w_out):
    part = lax.axis_index("dom").astype(jnp.int32).reshape(1)
    entry, step, counts, crossing = (jnp.swapaxes(a, 1, 2) for a in (entry, step, counts, crossing))
    w_in_t = jnp.swapaxes(w_in, 1, 2)[0]
    scalar = pl.BlockSpec(memory_space=pltpu.SMEM)
    params = pltpu.CompilerParams(vmem_limit_bytes=40 * 1024 * 1024)
    shape = jax.ShapeDtypeStruct
    listed = listing()
    lists = jnp.asarray(np.array([listed[0] + listed[1], listed[1] + listed[0]], np.float32))
    arguments = [in_hbm(a) for a in (
        anchor, direct, entry, step, counts, crossing, target, order, w_in_t, w_mid[0], w_out[0], lists
    )]
    prepared = (
        shape((K * SEL, ZONES), BF16),
        shape((K * SEL, ZONES), F32),
        shape((K * SEL, ZONES), F32),
        shape((32, SEL), F32),
        shape((256, 256), BF16),
        shape((256, 16), BF16),
    )
    room = [
        pltpu.VMEM((16, RG), F32),
        pltpu.VMEM((8, RG), F32),
        pltpu.VMEM((ZONES, RG), F32),
        pltpu.VMEM((16, 256), F32),
    ]
    send, *kept = pl.pallas_call(
        forward_kernel,
        out_shape=(
            shape((ZONES // 2, 2, 128), F32),
            shape((64, COLS), BF16),
            shape((256, COLS), BF16),
            shape((256, COLS), BF16),
            shape((9 * ROWS, 128), F32),
            *(shape(a.shape, a.dtype) for a in (crossing, target, order, lists, w_mid[0], w_out[0])),
            *prepared,
        ),
        in_specs=[scalar] + [pl.BlockSpec(memory_space=pltpu.HBM)] * len(arguments),
        out_specs=vmem(17),
        scratch_shapes=[pltpu.VMEM(a.shape, a.dtype) for a in (anchor, direct, entry, step, counts, w_in_t)]
        + [
            pltpu.VMEM((16, RG), F32),
            pltpu.VMEM((65 * ROWS, 128), F32),
            pltpu.VMEM((5 * ROWS, 128), F32),
            pltpu.VMEM((64, 256), F32),
            *room,
            pltpu.SemaphoreType.DMA((len(arguments),)),
        ],
        compiler_params=params,
        name="forward",
    )(part, *arguments)
    near = lax.all_to_all(send, "dom", 0, 0, axis_index_groups=listed)
    other = lax.ppermute(near, "dom", [(i, i ^ 1) for i in range(ZONES)])
    rendered, grads = pl.pallas_call(
        backward_kernel,
        out_shape=(shape((3, 1, OWN), F32), shape((4, CHUNK, 128), F32)),
        in_specs=[scalar] + vmem(2 + len(kept)),
        out_specs=vmem(2),
        scratch_shapes=[pltpu.VMEM(a.shape, a.dtype) for a in prepared] + [pltpu.VMEM((17 * ROWS, 128), F32), *room],
        compiler_params=params,
        name="backward",
    )(part, near, other, *kept)
    shares = lax.all_to_all(grads, "ray", 0, 0, axis_index_groups=[[2, 1, 0, 3]])
    total = jnp.sum(shares, axis=0)
    everything = lax.all_to_all(jnp.broadcast_to(total[None], grads.shape), "ray", 0, 0, axis_index_groups=[[2, 1, 0, 3]])
    grad_i, grad_m, grad_o = pl.pallas_call(
        unpack_kernel,
        out_shape=(shape((FEATS, 1, 256), F32), shape((256, 256), F32), shape((4, 256), F32)),
        in_specs=vmem(1),
        out_specs=[*vmem(1), pl.BlockSpec(memory_space=pltpu.HBM), *vmem(1)],
        scratch_shapes=[pltpu.SemaphoreType.DMA((8,))],
        compiler_params=params,
        name="unpack",
    )(everything)
    return rendered, jnp.transpose(grad_i, (1, 2, 0)), grad_m[None], grad_o[None]


def solution(mesh):
    in_specs = (
        P(None, "ray", None),
        P(None, "ray", None),
        P("ray", None, None),
        P("ray", None, None),
        P("ray", None, None),
        P("ray", None, None),
        P("ray", None, None),
        P(None, "ray", None),
        P("dom", None, None),
        P("dom", None, None),
        P("dom", None, None),
    )
    out_specs = (
        P(None, "ray", "dom"),
        P("dom", None, None),
        P("dom", None, None),
        P("dom", None, None),
    )
    return jax.shard_map(local, mesh=mesh, in_specs=in_specs, out_specs=out_specs, check_vma=False)
```

```python
import functools

import jax
import jax.numpy as jnp
import numpy as np
from jax import lax
from jax.experimental import pallas as pl
from jax.experimental.pallas import tpu as pltpu
from jax.sharding import PartitionSpec as P

NFREQ = 10
FEATS = 63
S = 64
K = 4
NB = 8
CAP = 64
ZONES = 128
RG = 512
OWN = 4
ROWS = 32
SEL = 72
FIRST = 92
EARLY = 48
SPAN = (16, 4)
COLS = CAP * S
TILE = 16
CHUNK = 168
F32 = jnp.float32
BF16 = jnp.bfloat16


def listing():
    def far(index):
        hops = 0
        for place, first, length in zip(divmod(index // 2, SPAN[1]), divmod(FIRST // 2, SPAN[1]), SPAN):
            hops += min((place - first) % length, (first - place) % length)
        return index // 2 != FIRST // 2, -hops

    return [sorted(range(core, ZONES, 2), key=far) for core in range(2)]


def iota(shape, dim):
    return lax.broadcasted_iota(jnp.int32, shape, dim)


def one_hot(mask):
    return mask.astype(F32).astype(BF16)


def split(x, terms):
    parts = []
    for _ in range(terms):
        parts.append(x.astype(BF16))
        x = x - parts[-1].astype(F32)
    return parts


def dot(a, b):
    return jnp.dot(a, b, preferred_element_type=F32)


def dot_nt(a, b):
    return lax.dot_general(a, b, (((1,), (1,)), ((), ())), preferred_element_type=F32)


def split_dot(x, exact, terms):
    return sum(dot(part, exact) for part in split(x, terms))


def halves(column):
    lane = iota((ROWS, 2 * S), 1)
    return jnp.where(lane < S, column[0:ROWS], column[ROWS : 2 * ROWS])


def sin_cos(x):
    turns = jnp.floor(x * 0.6366197723675814 + 0.5)
    r = ((x - turns * 1.5703125) - turns * 4.837512969970703e-4) - turns * 7.54978995489188e-8
    z = r * r
    s = ((-1.9515295891e-4 * z + 8.3321608736e-3) * z - 1.6666654611e-1) * z * r + r
    c = ((2.443315711809948e-5 * z - 1.388731625493765e-3) * z + 4.166664568298827e-2) * z * z - 0.5 * z + 1.0
    quadrant = turns.astype(jnp.int32)
    swap = (quadrant & 1) == 1
    sin_r = jnp.where(swap, c, s)
    cos_r = jnp.where(swap, s, c)
    sin_r = jnp.where((quadrant & 2) == 2, -sin_r, sin_r)
    cos_r = jnp.where(((quadrant + 1) & 2) == 2, -cos_r, cos_r)
    return sin_r, cos_r


def shade(raw, step_d, count_d):
    index = iota(step_d.shape, 1) & (S - 1)
    scale = jnp.where(index.astype(F32) < count_d, step_d, 0.0)
    decay = jnp.exp(-jnp.abs(raw[0]))
    density = jnp.maximum(raw[0], 0.0) + jnp.log1p(decay)
    optical = density * scale
    source, target = iota((2 * S, 2 * S), 0), iota((2 * S, 2 * S), 1)
    ahead = one_hot((source < target) & ((source < S) == (target < S)))
    passed = split_dot(optical, ahead, 2)
    entering = jnp.exp(-passed)
    weight = entering - jnp.exp(-(passed + optical))
    albedo = [1.0 / (1.0 + jnp.exp(-raw[c])) for c in (1, 2, 3)]
    return scale, optical, entering, weight, albedo


def select(part, crossing):
    earlier = one_hot(iota((RG, RG), 0) < iota((RG, RG), 1))
    own = crossing == part
    crossed = own[0:1] | own[1:2] | own[2:3] | own[3:4]
    place_own = dot(one_hot(jnp.broadcast_to(crossed, (16, RG))), earlier)[0:1]
    place_own = jnp.where(crossed, place_own.astype(jnp.int32), -1)
    row, ray = iota((SEL, RG), 0), iota((1, RG), 1)
    in_slot = (row < CAP) & (place_own == row)
    own_ray = (row >= CAP) & (row < CAP + OWN) & (ray == part * OWN + (row - CAP))
    return own, one_hot(in_slot | own_ray), earlier


def prepare(
    part, crossing_ref, target_ref, order_ref, lists_ref, w_mid_ref, w_out_ref,
    pick_ref, low_ref, high_ref, info_ref, w_mid_t_ref, w_out_t_ref, ints, goals, ranks, wout,
):
    crossing = crossing_ref[0]
    _, selector, earlier = select(part, crossing)
    ray = iota((1, RG), 1)
    ints[...] = jnp.zeros_like(ints)
    goals[...] = jnp.zeros_like(goals)
    for d in range(3):
        goals[d : d + 1] = target_ref[d]
    zone = iota((ZONES, RG), 0)
    names = [zone == crossing[k : k + 1] for k in range(K)]
    ranks[...] = dot(one_hot(names[0] | names[1] | names[2] | names[3]), earlier)
    place_all = ranks[...]
    ints[0:4] = crossing.astype(F32)
    for k in range(K):
        ints[4 + k : 5 + k] = jnp.sum(jnp.where(names[k], place_all, 0.0), axis=0, keepdims=True)
    ints[8:9] = (ray // (RG // NB)).astype(F32)
    ints[9:10] = jnp.ones((1, RG), F32)
    whole = ints[...].astype(BF16)
    table = dot_nt(selector, whole)
    info_ref[0:16] = dot_nt(whole, selector)
    info_ref[16:24] = sum(dot_nt(piece, selector) for piece in split(goals[...], 3))
    bundle = one_hot(table[:, 8:9].astype(jnp.int32) == iota((SEL, NB), 1))
    order = dot(bundle, order_ref[0].astype(F32).astype(BF16))
    lane = iota((SEL, ZONES), 1)
    lister = jnp.where((part & 1) == 0, lists_ref[0:1], lists_ref[1:2])
    positions = iota((8, ZONES), 1).astype(F32).astype(BF16)
    for k in range(K):
        named = table[:, k : k + 1]
        place = table[:, 4 + k : 5 + k].astype(jnp.int32)
        pick_ref[k * SEL : (k + 1) * SEL] = one_hot(named == lister)
        wanted = (lane & (ROWS - 1)) == (place & (ROWS - 1))
        low_ref[k * SEL : (k + 1) * SEL] = (wanted & (place < ROWS)).astype(F32)
        high_ref[k * SEL : (k + 1) * SEL] = (wanted & (place >= ROWS)).astype(F32)
        info_ref[24 + k : 25 + k] = dot_nt(positions, one_hot(order == named))[0:1]
    info_ref[28:32] = jnp.zeros((4, SEL), F32)
    wout[...] = jnp.zeros_like(wout)
    wout[0:4] = w_out_ref[...].astype(F32)
    w_out_t_ref[...] = wout[...].T.astype(BF16)
    w_mid_t_ref[...] = w_mid_ref[...].astype(F32).T.astype(BF16)


def forward_kernel(
    part_ref, anchor_hbm, direct_hbm, entry_hbm, step_hbm, counts_hbm, crossing_hbm, target_hbm, order_hbm,
    w_in_hbm, w_mid_hbm, w_out_hbm, lists_hbm,
    send_ref, enc_ref, one_ref, two_ref, shade_ref, crossing_ref, target_ref, order_ref, lists_ref, w_mid_ref, w_out_ref,
    pick_ref, low_ref, high_ref, info_ref, w_mid_t_ref, w_out_t_ref,
    anchor_ref, direct_ref, entry_ref, step_ref, counts_ref, w_in_ref, vals, feats, raws, win,
    ints, goals, ranks, wout, sems,
):
    copies = [
        pltpu.make_async_copy(source, target, sems.at[i])
        for i, (source, target) in enumerate((
            (crossing_hbm, crossing_ref), (entry_hbm, entry_ref), (step_hbm, step_ref), (counts_hbm, counts_ref),
            (anchor_hbm, anchor_ref), (direct_hbm, direct_ref), (w_in_hbm, w_in_ref), (w_mid_hbm, w_mid_ref),
            (w_out_hbm, w_out_ref), (target_hbm, target_ref), (order_hbm, order_ref),
            (lists_hbm, lists_ref),
        ))
    ]
    for copy in copies:
        copy.start()
    part = part_ref[0]
    vals[...] = jnp.zeros_like(vals)
    win[...] = jnp.zeros_like(win)
    wout[...] = jnp.zeros_like(wout)
    feats[FEATS * ROWS : (FEATS + 1) * ROWS] = jnp.zeros((ROWS, 2 * S), F32)
    copies[0].wait()

    crossing = crossing_ref[0]
    own, selector, _ = select(part, crossing)
    for copy in copies[1:]:
        copy.wait()

    def of_own(ref):
        return jnp.sum(jnp.where(own, ref[0].astype(F32), 0.0), axis=0, keepdims=True)

    for d in range(3):
        vals[d : d + 1] = anchor_ref[d]
        vals[3 + d : 4 + d] = direct_ref[d]
    vals[6:7] = of_own(entry_ref)
    vals[7:8] = of_own(step_ref)
    vals[8:9] = of_own(counts_ref)
    reals = sum(dot_nt(selector, piece) for piece in split(vals[...], 3))

    columns = [halves(reals[0:CAP, j : j + 1]) for j in range(9)]
    step_d, count_d = columns[7], columns[8]
    index = (iota((ROWS, 2 * S), 1) & (S - 1)).astype(F32)
    depth = columns[6] + (index + 0.5) * step_d
    for d in range(3):
        point = columns[d] + depth * columns[3 + d]
        feats[d * ROWS : (d + 1) * ROWS] = point
        sin_x, cos_x = sin_cos(point)
        for level in range(NFREQ):
            at = 3 + 6 * level + d
            feats[at * ROWS : (at + 1) * ROWS] = sin_x
            feats[(at + 3) * ROWS : (at + 4) * ROWS] = cos_x
            sin_x, cos_x = 2.0 * sin_x * cos_x, 1.0 - 2.0 * sin_x * sin_x

    win[0:FEATS] = w_in_ref[...].astype(F32)
    w_in = win[...].T.astype(BF16)
    w_mid = w_mid_ref[...]
    wout[0:4] = w_out_ref[...].astype(F32)
    w_out = wout[...].astype(BF16)
    half = one_hot(iota((8, 2 * S), 0) == iota((8, 2 * S), 1) // S)
    for tile in range(ROWS // TILE):
        span = slice(tile * TILE * 128, (tile + 1) * TILE * 128)
        encoded = jnp.concatenate(
            [feats[pl.ds(tile * TILE + j, FEATS + 1, stride=ROWS), :].astype(BF16) for j in range(TILE)], axis=1
        )
        enc_ref[:, span] = encoded
        one = jnp.maximum(dot(w_in, encoded), 0.0).astype(BF16)
        one_ref[:, span] = one
        two = jnp.maximum(dot(w_mid, one), 0.0).astype(BF16)
        two_ref[:, span] = two
        raw = dot(w_out, two)
        for j in range(TILE):
            raws[pl.ds(tile * TILE + j, 4, stride=ROWS), :] = raw[0:4, j * 128 : (j + 1) * 128]
    raw = [raws[c * ROWS : (c + 1) * ROWS] for c in range(4)]
    scale, optical, entering, weight, albedo = shade(raw, step_d, count_d)
    sums = jnp.concatenate([weight * albedo[0], weight * albedo[1], weight * albedo[2], -optical], axis=0)
    sent = sum(dot_nt(half, piece) for piece in split(sums, 2))
    send_ref[...] = jnp.broadcast_to(sent[None, 0:2], send_ref.shape)
    kept = [entering, weight, scale / (1.0 + jnp.exp(-raw[0]))] + albedo + [weight * a * (1.0 - a) for a in albedo]
    for i, value in enumerate(kept):
        shade_ref[i * ROWS : (i + 1) * ROWS] = value

    @pl.when(part < EARLY)
    def _():
        prepare(
            part, crossing_ref, target_ref, order_ref, lists_ref, w_mid_ref, w_out_ref,
            pick_ref, low_ref, high_ref, info_ref, w_mid_t_ref, w_out_t_ref, ints, goals, ranks, wout,
        )


def backward_kernel(
    part_ref, near_ref, other_ref, enc_ref, one_ref, two_ref, shade_ref,
    crossing_ref, target_ref, order_ref, lists_ref, w_mid_ref, w_out_ref, *refs,
):
    ready, (rendered_ref, grads_ref), work, (draw, *room) = refs[0:6], refs[6:8], refs[8:14], refs[14:]
    pick_ref, low_ref, high_ref, info_ref, w_mid_t_ref, w_out_t_ref = work

    @pl.when(part_ref[0] < EARLY)
    def _():
        for source, target in zip(ready, work):
            target[...] = source[...]

    @pl.when(part_ref[0] >= EARLY)
    def _():
        prepare(
            part_ref[0], crossing_ref, target_ref, order_ref, lists_ref, w_mid_ref, w_out_ref, *work, *room
        )

    part = part_ref[0].astype(F32)
    got = [jnp.concatenate([near_ref[:, h, :], other_ref[:, h, :]], axis=0) for h in range(2)]
    pieces = split(jnp.concatenate(got, axis=1), 2)
    gather = one_hot(iota((8, ZONES), 0) == iota((8, ZONES), 1) // ROWS)
    pick = pick_ref[...]
    low, high = low_ref[...] > 0.5, high_ref[...] > 0.5
    values = jnp.zeros((8, K * SEL), F32)
    for piece in pieces:
        both = dot(pick, piece)
        found = jnp.where(low, both[:, 0:128], jnp.where(high, both[:, 128:256], 0.0))
        values = values + dot_nt(gather, found.astype(BF16))

    mine = [values[:, k * SEL : (k + 1) * SEL] for k in range(K)]
    log = [mine[k][3:4] for k in range(K)]
    color = [mine[k][0:3] for k in range(K)]
    named = [info_ref[k : k + 1] for k in range(K)]
    used = info_ref[9:10] > 0.5
    goal = info_ref[16:19]
    rank = [info_ref[24 + k : 25 + k] for k in range(K)]
    fade = [
        jnp.exp(sum(jnp.where(rank[j] < rank[k], log[j], 0.0) for j in range(K) if j != k)) for k in range(K)
    ]
    clear = jnp.exp(log[0] + log[1] + log[2] + log[3])
    rendered = sum(fade[k] * color[k] for k in range(K)) + clear
    residual = rendered - goal
    share = [fade[k] * jnp.sum(residual * color[k], axis=0, keepdims=True) for k in range(K)]
    owned = [named[k] == part for k in range(K)]
    own_rank = sum(jnp.where(owned[k], rank[k], 0.0) for k in range(K))
    own_fade = sum(jnp.where(owned[k], fade[k], 0.0) for k in range(K))
    dlog = sum(jnp.where(rank[k] > own_rank, share[k], 0.0) for k in range(K))
    dlog = dlog + clear * jnp.sum(residual, axis=0, keepdims=True)
    dcolor = own_fade * residual
    for c in range(3):
        rendered_ref[c] = rendered[c : c + 1, CAP : CAP + OWN]
    slots = jnp.concatenate([dcolor, dlog, jnp.zeros((4, SEL), F32)], axis=0)
    slots = jnp.where(used, slots, 0.0)
    slots = jnp.concatenate([slots, jnp.zeros((8, 128 - SEL), F32)], axis=1).T

    entering, weight, slope, *rest = [shade_ref[i * ROWS : (i + 1) * ROWS] for i in range(9)]
    dcolor_d = [halves(slots[0:CAP, c : c + 1]) for c in range(3)]
    gain = sum(dcolor_d[c] * rest[c] for c in range(3))
    source, target = iota((2 * S, 2 * S), 0), iota((2 * S, 2 * S), 1)
    since = one_hot((source >= target) & ((source < S) == (target < S)))
    behind = split_dot(gain * weight, since, 3)
    draw[0:ROWS] = (gain * entering - behind - halves(slots[0:CAP, 3:4])) * slope
    for c in range(3):
        draw[(c + 1) * ROWS : (c + 2) * ROWS] = dcolor_d[c] * rest[3 + c]
    draw[4 * ROWS : 16 * ROWS] = jnp.zeros((12 * ROWS, 2 * S), F32)

    w_out_t, w_mid_t = w_out_t_ref[...], w_mid_t_ref[...]
    grad_out = jnp.zeros((16, 256), F32)
    grad_mid = jnp.zeros((256, 256), F32)
    grad_in = jnp.zeros((256, 64), F32)
    zero = jnp.zeros((), BF16)
    for tile in range(ROWS // TILE):
        span = slice(tile * TILE * 128, (tile + 1) * TILE * 128)
        low = jnp.concatenate(
            [draw[pl.ds(tile * TILE + j, 16, stride=ROWS), :].astype(BF16) for j in range(TILE)], axis=1
        )
        two, one = two_ref[:, span], one_ref[:, span]
        grad_out = grad_out + dot_nt(low, two)
        d_two = jnp.where(two > 0, dot(w_out_t, low).astype(BF16), zero)
        grad_mid = grad_mid + dot_nt(d_two, one)
        d_one = jnp.where(one > 0, dot(w_mid_t, d_two).astype(BF16), zero)
        grad_in = grad_in + dot_nt(d_one, enc_ref[:, span])
    grad_in = grad_in.T
    for q in range(4):
        for h in range(2):
            half = slice(128 * h, 128 * h + 128)
            grads_ref[q, 64 * h : 64 * h + 64] = grad_mid[64 * q : 64 * q + 64, half]
            grads_ref[q, 128 + 16 * h : 144 + 16 * h] = grad_in[16 * q : 16 * q + 16, half]
            grads_ref[q, 160 + 4 * h : 164 + 4 * h] = jnp.broadcast_to(grad_out[q : q + 1, half], (4, 128))


def unpack_kernel(all_ref, in_ref, mid_ref, out_ref):
    for q in range(4):
        rows = min(16, FEATS - 16 * q)
        for h in range(2):
            half = slice(128 * h, 128 * h + 128)
            mid_ref[64 * q : 64 * q + 64, half] = all_ref[q, 64 * h : 64 * h + 64]
            in_ref[16 * q : 16 * q + rows, 0, half] = all_ref[q, 128 + 16 * h : 128 + 16 * h + rows]
            out_ref[q : q + 1, half] = all_ref[q, 160 + 4 * h : 161 + 4 * h]


def vmem(count):
    return [pl.BlockSpec(memory_space=pltpu.VMEM)] * count


def in_hbm(array):
    return pltpu.with_memory_space_constraint(array, pltpu.HBM)


def local(anchor, direct, entry, step, counts, crossing, order, target, w_in, w_mid, w_out):
    part = lax.axis_index("dom").astype(jnp.int32).reshape(1)
    entry, step, counts, crossing = (jnp.swapaxes(a, 1, 2) for a in (entry, step, counts, crossing))
    w_in_t = jnp.swapaxes(w_in, 1, 2)[0]
    scalar = pl.BlockSpec(memory_space=pltpu.SMEM)
    params = pltpu.CompilerParams(vmem_limit_bytes=40 * 1024 * 1024)
    shape = jax.ShapeDtypeStruct
    listed = listing()
    lists = jnp.asarray(np.array([listed[0] + listed[1], listed[1] + listed[0]], np.float32))
    arguments = [in_hbm(a) for a in (
        anchor, direct, entry, step, counts, crossing, target, order, w_in_t, w_mid[0], w_out[0], lists
    )]
    prepared = (
        shape((K * SEL, ZONES), BF16),
        shape((K * SEL, ZONES), F32),
        shape((K * SEL, ZONES), F32),
        shape((32, SEL), F32),
        shape((256, 256), BF16),
        shape((256, 16), BF16),
    )
    room = [
        pltpu.VMEM((16, RG), F32),
        pltpu.VMEM((8, RG), F32),
        pltpu.VMEM((ZONES, RG), F32),
        pltpu.VMEM((16, 256), F32),
    ]
    send, *kept = pl.pallas_call(
        forward_kernel,
        out_shape=(
            shape((ZONES // 2, 2, 128), F32),
            shape((64, COLS), BF16),
            shape((256, COLS), BF16),
            shape((256, COLS), BF16),
            shape((9 * ROWS, 128), F32),
            *(shape(a.shape, a.dtype) for a in (crossing, target, order, lists, w_mid[0], w_out[0])),
            *prepared,
        ),
        in_specs=[scalar] + [pl.BlockSpec(memory_space=pltpu.HBM)] * len(arguments),
        out_specs=vmem(17),
        scratch_shapes=[pltpu.VMEM(a.shape, a.dtype) for a in (anchor, direct, entry, step, counts, w_in_t)]
        + [
            pltpu.VMEM((16, RG), F32),
            pltpu.VMEM((65 * ROWS, 128), F32),
            pltpu.VMEM((5 * ROWS, 128), F32),
            pltpu.VMEM((64, 256), F32),
            *room,
            pltpu.SemaphoreType.DMA((len(arguments),)),
        ],
        compiler_params=params,
        name="forward",
    )(part, *arguments)
    near = lax.all_to_all(send, "dom", 0, 0, axis_index_groups=listed)
    other = lax.ppermute(near, "dom", [(i, i ^ 1) for i in range(ZONES)])
    rendered, grads = pl.pallas_call(
        backward_kernel,
        out_shape=(shape((3, 1, OWN), F32), shape((4, CHUNK, 128), F32)),
        in_specs=[scalar] + vmem(2 + len(kept)),
        out_specs=vmem(2),
        scratch_shapes=[pltpu.VMEM(a.shape, a.dtype) for a in prepared] + [pltpu.VMEM((17 * ROWS, 128), F32), *room],
        compiler_params=params,
        name="backward",
    )(part, near, other, *kept)
    shares = lax.all_to_all(grads, "ray", 0, 0, axis_index_groups=[[2, 1, 0, 3]])
    total = jnp.sum(shares, axis=0)
    everything = lax.all_to_all(jnp.broadcast_to(total[None], grads.shape), "ray", 0, 0, axis_index_groups=[[2, 1, 0, 3]])
    grad_i, grad_m, grad_o = pl.pallas_call(
        unpack_kernel,
        out_shape=(shape((FEATS, 1, 256), F32), shape((256, 256), F32), shape((4, 256), F32)),
        in_specs=vmem(1),
        out_specs=vmem(3),
        compiler_params=params,
        name="unpack",
    )(everything)
    return rendered, jnp.transpose(grad_i, (1, 2, 0)), grad_m[None], grad_o[None]


def solution(mesh):
    in_specs = (
        P(None, "ray", None),
        P(None, "ray", None),
        P("ray", None, None),
        P("ray", None, None),
        P("ray", None, None),
        P("ray", None, None),
        P("ray", None, None),
        P(None, "ray", None),
        P("dom", None, None),
        P("dom", None, None),
        P("dom", None, None),
    )
    out_specs = (
        P(None, "ray", "dom"),
        P("dom", None, None),
        P("dom", None, None),
        P("dom", None, None),
    )
    return jax.shard_map(local, mesh=mesh, in_specs=in_specs, out_specs=out_specs, check_vma=False)
```
